32 devices in a mesh: expert: 4 (over z), hidden: 2 (over core), dp: 4 (over y, x).
Axes of the slice: x: 2, y: 2, z: 4, core: 2. Of those that a mesh axis runs over, the one named last changes fastest.
Arguments:
- tokens: bfloat16 [20480, 768], P(('expert', 'hidden', 'dp')), may hold values from -6 to 6
- cotangent: bfloat16 [20480, 768], P(('expert', 'hidden', 'dp')), may hold values from -6 to 6
- ln1_gain: float32 [768], replicated, may hold values from 0.5 to 1.5
- ln1_shift: float32 [768], replicated, may hold values from -1.5 to 1.5
- w_query: bfloat16 [768, 768], replicated, may hold values from -0.21875 to 0.21875
- w_key: bfloat16 [768, 768], replicated, may hold values from -0.21875 to 0.21875
- w_value: bfloat16 [768, 768], replicated, may hold values from -0.21875 to 0.21875
- w_output: bfloat16 [768, 768], replicated, may hold values from -1.75 to 1.75
- ln2_gain: float32 [768], replicated, may hold values from 0.5 to 1.5
- ln2_shift: float32 [768], replicated, may hold values from -1.5 to 1.5
- w_router: bfloat16 [768, 4], replicated, may hold values from -0.15625 to 0.15625
- w_inner: bfloat16 [4, 768, 3072], P('expert', None, 'hidden'), may hold values from -0.21875 to 0.21875
- b_inner: bfloat16 [4, 3072], P('expert', 'hidden'), may hold values from -0.59765625 to 0.59765625
- w_outer: bfloat16 [4, 3072, 768], P('expert', 'hidden'), may hold values from -1.75 to 1.75
- b_outer: bfloat16 [4, 768], P('expert'), may hold values from -6 to 6
- image_count: int32 [32], P(('expert', 'hidden', 'dp')), may hold values from 1 to 3, as said below
- patches: int32 [32], P(('expert', 'hidden', 'dp')), may hold values from 196 to 576, as said below
- picks: int32 [20480, 2], P(('expert', 'hidden', 'dp')), may hold values from 0 to 3, as said below
- slots: int32 [20480, 2], P(('expert', 'hidden', 'dp')), may hold values from -1 to 335, as said below
Outputs:
- block_out: bfloat16 [20480, 768], P(('expert', 'hidden', 'dp'))
- grad_tokens: float32 [20480, 768], P(('expert', 'hidden', 'dp'))
- grad_ln1_gain: float32 [768], replicated
- grad_ln1_shift: float32 [768], replicated
- grad_w_query: float32 [768, 768], replicated
- grad_w_key: float32 [768, 768], replicated
- grad_w_value: float32 [768, 768], replicated
- grad_w_output: float32 [768, 768], replicated
- grad_ln2_gain: float32 [768], replicated
- grad_ln2_shift: float32 [768], replicated
- grad_w_router: float32 [768, 4], replicated
- grad_w_inner: float32 [4, 768, 3072], P('expert', None, 'hidden')
- grad_b_inner: float32 [4, 3072], P('expert', 'hidden')
- grad_w_outer: float32 [4, 3072, 768], P('expert', 'hidden')
- grad_b_outer: float32 [4, 768], P('expert')
The draws below stay inside these ranges and needn't reach their ends.
Inputs may be any that keep to these rules, and one draw needn't show every extreme that they name: `image_count`: rows of a device are its images in order, each of patches rows, then padding. Each device's images are all of 196 or all of 576 patches; image_count times patches is at most 640. `picks`: the two experts of a row differ. `slots`: slot of the choice in the buffer of expert picks[t, k] for the rows of t's device, -1 where the choice is dropped and for both choices of a padding row; on one device no two choices share an expert and a slot.
All inputs are finite; a program needn't handle non-finite values.
Results may differ from the reference program's by a relative error of at most 0.017.
Values may be sent and summed in bfloat16 or wider, within the bound.
No kernel may reach another device: no remote copies, remote signals or barrier semaphores. Data moves between devices by JAX's collectives and lax.ppermute only.
A program may use at most 192 MiB of HBM per device.

```python
import jax
import jax.numpy as jnp
from jax import lax

D = 768
HEADS = 12
HEAD_DIM = 64
FF = 3072
TOK_DEV = 640
PATCH_LOW = 196
PATCH_HIGH = 576
EXPERTS = 4
TOKENS = 20480
CAP = 336


def image_layout(base_key):
    local_key = jax.random.fold_in(base_key, 11)
    devices = TOKENS // TOK_DEV
    key_res, key_low, key_high = jax.random.split(local_key, 3)
    high_res = jax.random.randint(key_res, (devices,), 0, 2)
    high_res = high_res.at[0].set(0).at[1].set(1)
    count_low = jax.random.randint(key_low, (devices,), 1, TOK_DEV // PATCH_LOW + 1)
    count_low = count_low.at[0].set(TOK_DEV // PATCH_LOW)
    count_high = jax.random.randint(key_high, (devices,), 1, TOK_DEV // PATCH_HIGH + 1)
    counts = jnp.where(high_res == 1, count_high, count_low)
    patch_rows = jnp.where(high_res == 1, PATCH_HIGH, PATCH_LOW)
    return (counts.astype(jnp.int32), patch_rows.astype(jnp.int32))


def routing(base_key):
    counts, patch_rows = image_layout(base_key)
    local_key = jax.random.fold_in(base_key, 23)
    devices = TOKENS // TOK_DEV
    key_weight, key_jitter, key_busy, key_order = jax.random.split(local_key, 4)
    weight = jax.random.randint(key_weight, (EXPERTS,), 0, 4) * 150
    jitter = jax.random.randint(key_jitter, (devices, TOK_DEV, EXPERTS), 0, 1000)
    busiest = jax.random.randint(key_busy, (devices,), 0, EXPERTS)
    priority = jax.vmap(lambda sub_key: jax.random.permutation(sub_key, TOK_DEV))(jax.random.split(key_order, devices))
    position = jnp.arange(TOK_DEV, dtype=jnp.int32)
    valid_rows = counts * patch_rows
    live_rows = position[None, :] < valid_rows[:, None]
    forced = position[None, :] < jnp.minimum(CAP, valid_rows)[:, None]
    expert_ids = jnp.arange(EXPERTS, dtype=jnp.int32)
    boost_add = jnp.where(forced[:, :, None] & (expert_ids[None, None, :] == busiest[:, None, None]), 100000, 0)
    scores = (jitter + weight[None, None, :] + boost_add) * EXPERTS + expert_ids[None, None, :]
    unused, picks = lax.top_k(scores, 2)
    picks = picks.astype(jnp.int32)
    ranking = jnp.where(forced, position[None, :] - TOK_DEV, priority.astype(jnp.int32))
    order_key = jnp.concatenate([ranking, ranking + 2 * TOK_DEV], axis=1) + TOK_DEV
    chosen = jnp.concatenate([picks[:, :, 0], picks[:, :, 1]], axis=1)
    alive = jnp.concatenate([live_rows, live_rows], axis=1)
    target = jnp.where(alive, chosen, EXPERTS)
    sort_key = target * (4 * TOK_DEV) + order_key

    def slot_for_device(keys_row, target_row):
        ordering = jnp.argsort(keys_row)
        sorted_target = target_row[ordering]
        load_counts = jnp.sum((sorted_target[:, None] == expert_ids[None, :]).astype(jnp.int32), axis=0)
        group_start = jnp.cumsum(load_counts) - load_counts
        place = jnp.arange(2 * TOK_DEV, dtype=jnp.int32) - group_start[jnp.minimum(sorted_target, EXPERTS - 1)]
        slot_sorted = jnp.where((sorted_target < EXPERTS) & (place < CAP), place, -1)
        return jnp.zeros((2 * TOK_DEV,), jnp.int32).at[ordering].set(slot_sorted.astype(jnp.int32))
    slot_all = jax.vmap(slot_for_device)(sort_key, target)
    slot_pair = jnp.stack([slot_all[:, :TOK_DEV], slot_all[:, TOK_DEV:]], axis=-1)
    return (picks.reshape(TOKENS, 2), slot_pair.reshape(TOKENS, 2))


def draw_image_count(key, part):
    return image_layout(key)[0]


def draw_patches(key, part):
    return image_layout(key)[1]


def draw_picks(key, part):
    return routing(key)[0]


def draw_slots(key, part):
    return routing(key)[1]


def level_of(stream_key, dims, pieces, least, high):
    loudness, own = 1.0, jax.random.fold_in(stream_key, 6)
    for dim, shards_of in pieces:
        draws = jnp.exp(jax.random.uniform(jax.random.fold_in(own, dim), (shards_of,), jnp.float32, least / len(pieces), high / len(pieces)))
        loudness = loudness * jnp.repeat(draws, dims[dim] // shards_of).reshape([-1 if axis == dim else 1 for axis in range(len(dims))])
    return loudness


def noise(stream_key, extent, width, reach, cuts=(), held_as=jnp.bfloat16):
    entries = width * jax.random.normal(stream_key, extent, jnp.float32)
    if cuts:
        entries = entries * level_of(stream_key, extent, cuts, -0.22, 0.18)
    return jnp.clip(entries, -reach, reach).astype(held_as)


def setup_inputs(seed: int = 0) -> dict:
    keys = jax.random.split(jax.random.key(seed), 20)
    return {
        "tokens": noise(keys[0], (TOKENS, D), 1.0, 6.0, ((0, 32),)),
        "cotangent": noise(keys[1], (TOKENS, D), 1.0, 6.0, ((0, 32),)),
        "ln1_gain": jnp.clip(1.0 + 0.1 * jax.random.normal(keys[2], (D,), jnp.float32), 0.5, 1.5),
        "ln1_shift": noise(keys[3], (D,), 0.3, 1.5, (), jnp.float32),
        "w_query": noise(keys[4], (D, D), D ** -0.5, 0.21875),
        "w_key": noise(keys[5], (D, D), D ** -0.5, 0.21875),
        "w_value": noise(keys[6], (D, D), D ** -0.5, 0.21875),
        "w_output": noise(keys[7], (D, D), (max(D // 64, 1)) ** -0.5, 1.75),
        "ln2_gain": jnp.clip(1.0 + 0.1 * jax.random.normal(keys[8], (D,), jnp.float32), 0.5, 1.5),
        "ln2_shift": noise(keys[9], (D,), 0.3, 1.5, (), jnp.float32),
        "w_router": noise(keys[10], (D, EXPERTS), (2 * D) ** -0.5, 0.15625),
        "w_inner": noise(keys[11], (EXPERTS, D, FF), D ** -0.5, 0.21875, ((0, 4), (2, 2))),
        "b_inner": noise(keys[12], (EXPERTS, FF), 0.1, 0.59765625, ((0, 4), (1, 2))),
        "w_outer": noise(keys[13], (EXPERTS, FF, D), (max(FF // 256, 1)) ** -0.5, 1.75, ((0, 4), (1, 2))),
        "b_outer": noise(keys[14], (EXPERTS, D), 1.0, 6.0, ((0, 4),)),
        "image_count": draw_image_count(jax.random.fold_in(keys[19], 71), 0),
        "patches": draw_patches(jax.random.fold_in(keys[19], 71), 0),
        "picks": draw_picks(jax.random.fold_in(keys[19], 71), 0),
        "slots": draw_slots(jax.random.fold_in(keys[19], 71), 0),
    }


NORM_EPS = 1e-06
MASKED = -1e+30

@jax.custom_vjp
def low(v):
    return lax.optimization_barrier(v.astype(jnp.bfloat16)).astype(jnp.float32)

@jax.custom_vjp
def low_back(v):
    return v

def low_keep(v):
    return (low(v), None)

def low_pass(kept, grad):
    return (grad,)

def back_keep(v):
    return (v, None)

def back_low(kept, grad):
    return (low(grad),)
low.defvjp(low_keep, low_pass)
low_back.defvjp(back_keep, back_low)

def matmul(left_side, right_side):
    return jnp.dot(left_side, right_side, precision=lax.Precision.HIGHEST, preferred_element_type=jnp.float32)

def layer_norm(values, gain_vec, shift_vec):
    center = lax.optimization_barrier(jnp.mean(values, axis=-1, keepdims=True))
    centered = values - center
    moment = lax.optimization_barrier(jnp.mean(centered * centered, axis=-1, keepdims=True))
    return centered * lax.rsqrt(moment + NORM_EPS) * gain_vec + shift_vec

def softmax_last(scores):
    largest = lax.optimization_barrier(jnp.max(scores, axis=-1, keepdims=True))
    powers = jnp.exp(scores - largest)
    return powers / lax.optimization_barrier(jnp.sum(powers, axis=-1, keepdims=True))

def attend(block_args):
    query_block, key_block, value_block, segment_block = block_args
    query_heads = query_block.reshape(TOK_DEV, HEADS, HEAD_DIM)
    key_heads = key_block.reshape(TOK_DEV, HEADS, HEAD_DIM)
    value_heads = value_block.reshape(TOK_DEV, HEADS, HEAD_DIM)
    scores = jnp.einsum('thd,shd->hts', query_heads, key_heads, precision=lax.Precision.HIGHEST) * HEAD_DIM ** (-0.5)
    allowed = segment_block[:, None] == segment_block[None, :]
    scores = low_back(jnp.where(allowed[None], scores, MASKED))
    weights = low(softmax_last(scores))
    mixed_rows = jnp.einsum('hts,shd->thd', weights, value_heads, precision=lax.Precision.HIGHEST)
    return mixed_rows.reshape(TOK_DEV, D)

def expert(expert_args):
    slot_rows, inner_w, inner_b, outer_w, outer_b = expert_args
    pre_act = low_back(matmul(slot_rows, inner_w) + inner_b)
    hidden_act = low(jax.nn.gelu(pre_act, approximate=True))
    return low_back(low(matmul(hidden_act, outer_w) + outer_b))

def reference(tokens, cotangent, ln1_gain, ln1_shift, w_query, w_key, w_value, w_output, ln2_gain, ln2_shift, w_router, w_inner, b_inner, w_outer, b_outer, image_count, patches, picks, slots):
    blocks = TOKENS // TOK_DEV
    position = jnp.arange(TOK_DEV, dtype=jnp.int32)
    live_mask = position[None, :] < (image_count * patches)[:, None]
    segment = jnp.where(live_mask, position[None, :] // patches[:, None], -1 - position[None, :]).astype(jnp.int32)
    live_rows = live_mask.reshape(TOKENS, 1).astype(jnp.float32)
    device = (jnp.arange(TOKENS, dtype=jnp.int32) // TOK_DEV).astype(jnp.int32)
    assigned = slots >= 0
    assigned_float = assigned.astype(jnp.float32)
    target = jnp.where(assigned, picks, EXPERTS).astype(jnp.int32)
    slot_row = (device[:, None] * CAP + jnp.maximum(slots, 0)).astype(jnp.int32)

    def forward(inputs, gain_one, shift_one, query_w, key_w, value_w, output_w, gain_two, shift_two, router_w, inner_w, inner_b, outer_w, outer_b):
        normed_one = low(layer_norm(inputs, gain_one, shift_one))
        query = low_back(low(matmul(normed_one, query_w)))
        key_rows = low_back(low(matmul(normed_one, key_w)))
        value_rows = low_back(low(matmul(normed_one, value_w)))
        mixed_rows = lax.map(jax.checkpoint(attend), (query.reshape(blocks, TOK_DEV, D), key_rows.reshape(blocks, TOK_DEV, D), value_rows.reshape(blocks, TOK_DEV, D), segment))
        mixed_rows = low_back(low(mixed_rows.reshape(TOKENS, D)))
        residual_one = inputs + low_back(matmul(mixed_rows, output_w))
        normed_two = low(layer_norm(residual_one, gain_two, shift_two))
        gate_probs = softmax_last(matmul(normed_two, router_w))
        spread = jnp.broadcast_to(normed_two[:, None, :], (TOKENS, 2, D))
        inbound = jnp.zeros((EXPERTS, blocks * CAP, D), jnp.float32).at[target, slot_row].set(spread, mode='drop')
        inbound = low_back(inbound)
        outbound = lax.map(jax.checkpoint(expert), (inbound, inner_w, inner_b, outer_w, outer_b))
        fetched = outbound[jnp.minimum(target, EXPERTS - 1), slot_row]
        chosen = jnp.take_along_axis(gate_probs, picks, axis=1) * assigned_float
        return (residual_one + lax.optimization_barrier(jnp.sum(chosen[:, :, None] * fetched, axis=1))) * live_rows
    output_rows, pullback = jax.vjp(forward, tokens.astype(jnp.float32), ln1_gain, ln1_shift, w_query.astype(jnp.float32), w_key.astype(jnp.float32), w_value.astype(jnp.float32), w_output.astype(jnp.float32), ln2_gain, ln2_shift, w_router.astype(jnp.float32), w_inner.astype(jnp.float32), b_inner.astype(jnp.float32), w_outer.astype(jnp.float32), b_outer.astype(jnp.float32))
    gradients = pullback(cotangent.astype(jnp.float32))
    return (output_rows.astype(jnp.bfloat16), gradients[0], gradients[1], gradients[2], gradients[3], gradients[4], gradients[5], gradients[6], gradients[7], gradients[8], gradients[9], gradients[10], gradients[11], gradients[12], gradients[13])
```

```python
import functools

import jax
import jax.numpy as jnp
from jax import lax
from jax.experimental import pallas as pl
from jax.experimental.pallas import tpu as pltpu
from jax.sharding import PartitionSpec as P

HEADS = 12
NORM_EPS = 1e-06
MASKED = -1e30
IMAGES_MAX = 8
BF = jnp.bfloat16
F32 = jnp.float32
VMEM_LIMIT = 56 * 1024 * 1024

VM = pltpu.VMEM
SMEM = pltpu.SMEM


def mm(a, b):
    return lax.dot_general(a, b, (((1,), (0,)), ((), ())), preferred_element_type=F32)


def mm_nt(a, b):
    return lax.dot_general(a, b, (((1,), (1,)), ((), ())), preferred_element_type=F32)


def mm_tn(a, b):
    return lax.dot_general(a, b, (((0,), (0,)), ((), ())), preferred_element_type=F32)


def standardize(values):
    center = jnp.mean(values, axis=-1, keepdims=True)
    centered = values - center
    moment = jnp.mean(centered * centered, axis=-1, keepdims=True)
    inv = lax.rsqrt(moment + NORM_EPS)
    return centered * inv, inv


def norm_back(grad_normed, gain, unit, inv):
    g = grad_normed * gain
    first = jnp.mean(g, axis=-1, keepdims=True)
    second = jnp.mean(g * unit, axis=-1, keepdims=True)
    return (g - first - unit * second) * inv


def targets(picks, slots, capacity):
    return jnp.where(slots >= 0, picks * capacity + slots, -1)


def pack_into(out_ref, rows_ref, pick_ref, slot_ref, capacity, step):
    dest = targets(pick_ref[...], slot_ref[...], capacity)
    total, rows = out_ref.shape[0], rows_ref.shape[0]
    for start in range(0, total, step):
        index = lax.broadcasted_iota(jnp.int32, (step, rows), 0) + start
        hit = (index == dest[0:1, :]) | (index == dest[1:2, :])
        out_ref[start : start + step, :] = mm(hit.astype(BF), rows_ref[...]).astype(BF)


def unpack_rows(buffer_ref, pick, slot, capacity):
    dest = targets(pick, slot, capacity)
    rows, total = dest.shape[0], buffer_ref.shape[0]
    index = lax.broadcasted_iota(jnp.int32, (rows, total), 1)
    hit = (index == dest[:, 0:1]) | (index == dest[:, 1:2])
    return mm(hit.astype(BF), buffer_ref[...])


def pack_step(total):
    for step in (448, 336, 224, 192, 112, 96, 64, 48, 32, 16):
        if total % step == 0:
            return step
    return total


def pack_kernel(pick_ref, slot_ref, rows_ref, out_ref, *, capacity):
    pack_into(out_ref, rows_ref, pick_ref, slot_ref, capacity, pack_step(out_ref.shape[0]))


def params():
    return pltpu.CompilerParams(vmem_limit_bytes=VMEM_LIMIT)


def whole(shape):
    return pl.BlockSpec(shape, lambda *_: (0,) * len(shape))


def pack(pick_rows, slot_rows, rows, total, capacity):
    count, width = rows.shape
    return pl.pallas_call(
        functools.partial(pack_kernel, capacity=capacity),
        out_shape=jax.ShapeDtypeStruct((total, width), BF),
        in_specs=[pl.BlockSpec(memory_space=VM)] * 3,
        out_specs=pl.BlockSpec(memory_space=VM),
        compiler_params=params(),
        cost_estimate=pl.CostEstimate(
            flops=2 * total * count * width, bytes_accessed=4 * total * width, transcendentals=0
        ),
        name="pack_rows",
    )(pick_rows, slot_rows, rows)


def classes(count, patch, rows, padding):
    row = lax.broadcasted_iota(jnp.int32, (rows, 1), 0)
    image = jnp.zeros((rows, 1), jnp.int32)
    for i in range(1, IMAGES_MAX):
        image = image + (row >= i * patch).astype(jnp.int32)
    return jnp.where(row < count * patch, image, padding)


def front_kernel(
    count_ref,
    patch_ref,
    tokens_ref,
    gain1_ref,
    shift1_ref,
    wq_ref,
    wk_ref,
    wv_ref,
    wo_ref,
    gain2_ref,
    shift2_ref,
    pick_ref,
    slot_ref,
    n1_ref,
    q_ref,
    k_ref,
    v_ref,
    p_ref,
    linv_ref,
    mixed_ref,
    res_ref,
    out_ref,
    n2_ref,
    *,
    capacity,
    head_dim,
    qb,
):
    j = pl.program_id(0)
    rows, width = tokens_ref.shape
    cols = wq_ref.shape[1]

    @pl.when(j == 0)
    def _():
        x = tokens_ref[...].astype(F32)
        unit, _ = standardize(x)
        n1_ref[...] = (unit * gain1_ref[...] + shift1_ref[...]).astype(BF)
        res_ref[...] = x

    n1 = n1_ref[...]
    q_ref[...] = mm(n1, wq_ref[...]).astype(BF)
    k_ref[...] = mm(n1, wk_ref[...]).astype(BF)
    v_ref[...] = mm(n1, wv_ref[...]).astype(BF)
    cls = classes(count_ref[0], patch_ref[0], rows, head_dim - 1)
    lane = lax.broadcasted_iota(jnp.int32, (rows, 2 * head_dim), 1)
    inner = lane % head_dim
    apart = jnp.where(inner == cls, 0.0, MASKED).astype(BF)
    member = jnp.where(inner == cls, 1.0, 0.0).astype(BF)
    ones = jnp.ones((rows, 2 * head_dim), BF)
    scale = head_dim ** (-0.5)
    for pair in range(cols // (2 * head_dim)):
        sl = slice(pair * 2 * head_dim, (pair + 1) * 2 * head_dim)
        q_pair = q_ref[:, sl] * jnp.asarray(scale, BF)
        k_pair = k_ref[:, sl]
        v_ext = jnp.concatenate([v_ref[:, sl], ones], axis=1)
        for h in range(2):
            mine = (lane >= h * head_dim) & (lane < (h + 1) * head_dim)
            qm = jnp.where(mine, q_pair, apart)
            km = jnp.where(mine, k_pair, member)
            for b in range(0, rows, qb):
                s = mm_nt(qm[b : b + qb], km)
                top = jnp.max(s, axis=-1, keepdims=True)
                p = jnp.exp(s - top).astype(BF)
                p_ref[pair * 2 + h, b : b + qb, :] = p
                ov = mm(p, v_ext)
                linv = 1.0 / ov[:, 2 * head_dim :]
                o = (ov[:, : 2 * head_dim] * linv).astype(BF)
                if h == 0:
                    mixed_ref[b : b + qb, sl] = o
                    linv_ref[b : b + qb, sl] = linv
                else:
                    keep = mine[b : b + qb]
                    mixed_ref[b : b + qb, sl] = jnp.where(keep, o, mixed_ref[b : b + qb, sl])
                    linv_ref[b : b + qb, sl] = jnp.where(keep, linv, linv_ref[b : b + qb, sl])
    res_ref[...] += mm(mixed_ref[...], wo_ref[...])

    @pl.when(j == pl.num_programs(0) - 1)
    def _():
        unit, _ = standardize(res_ref[...])
        n2_ref[...] = (unit * gain2_ref[...] + shift2_ref[...]).astype(BF)
        pack_into(out_ref, n2_ref, pick_ref, slot_ref, capacity, pack_step(out_ref.shape[0]))


def front(count, patch, tokens, g1, s1, wq, wk, wv, wo, g2, s2, pick_rows, slot_rows, total, capacity):
    rows, width = tokens.shape
    head_dim = width // HEADS
    quad = 4 * head_dim
    steps = width // quad
    col = pl.BlockSpec((width, quad), lambda j: (0, j))
    seq = pl.BlockSpec((rows, quad), lambda j: (0, j))
    smem = pl.BlockSpec(memory_space=SMEM)
    flops = 2 * rows * width * (4 * width + 2 * rows + total)
    return pl.pallas_call(
        functools.partial(front_kernel, capacity=capacity, head_dim=head_dim, qb=rows // 5),
        grid=(steps,),
        out_shape=(
            jax.ShapeDtypeStruct((rows, width), BF),
            jax.ShapeDtypeStruct((rows, width), BF),
            jax.ShapeDtypeStruct((rows, width), BF),
            jax.ShapeDtypeStruct((rows, width), BF),
            jax.ShapeDtypeStruct((HEADS, rows, rows), BF),
            jax.ShapeDtypeStruct((rows, width), F32),
            jax.ShapeDtypeStruct((rows, width), BF),
            jax.ShapeDtypeStruct((rows, width), F32),
            jax.ShapeDtypeStruct((total, width), BF),
        ),
        in_specs=[
            smem,
            smem,
            whole((rows, width)),
            whole((1, width)),
            whole((1, width)),
            col,
            col,
            col,
            pl.BlockSpec((quad, width), lambda j: (j, 0)),
            whole((1, width)),
            whole((1, width)),
            whole(pick_rows.shape),
            whole(slot_rows.shape),
        ],
        out_specs=(
            whole((rows, width)),
            seq,
            seq,
            seq,
            pl.BlockSpec((4, rows, rows), lambda j: (j, 0, 0)),
            seq,
            seq,
            whole((rows, width)),
            whole((total, width)),
        ),
        scratch_shapes=[pltpu.VMEM((rows, width), BF)],
        compiler_params=params(),
        cost_estimate=pl.CostEstimate(
            flops=flops, bytes_accessed=30 * 1024 * 1024, transcendentals=HEADS * rows * rows
        ),
        name="front",
    )(count, patch, tokens, g1, s1, wq, wk, wv, wo, g2, s2, pick_rows, slot_rows)


GELU_A = 0.7978845608028654
GELU_B = 0.044715


def expert_kernel(
    x_ref,
    c_ref,
    wi_own_ref,
    wi_far_ref,
    wo_own_ref,
    wo_far_ref,
    bi_ref,
    bo_ref,
    router_ref,
    hid_ref,
    gp_ref,
    gout_ref,
    out_ref,
    gin_ref,
    gbi_ref,
    gbo_ref,
    grouter_ref,
    acc_out,
    acc_gin,
    prob,
    *,
    rb,
    axis,
):
    f = pl.program_id(0)
    steps = pl.num_programs(0)
    total, width = x_ref.shape
    experts = router_ref.shape[1]
    mine = lax.broadcasted_iota(jnp.int32, (total, experts), 1) == lax.axis_index(axis)

    @pl.when(f == 0)
    def _():
        logits = mm(x_ref[...], router_ref[...])
        powers = jnp.exp(logits - jnp.max(logits, axis=-1, keepdims=True))
        probs = powers / jnp.sum(powers, axis=-1, keepdims=True)
        prob[...] = probs
        chosen = jnp.sum(jnp.where(mine, probs, 0.0), axis=-1, keepdims=True)
        grads = (chosen * c_ref[...].astype(F32)).astype(BF)
        gout_ref[...] = grads
        gbo_ref[...] = jnp.sum(grads.astype(F32), axis=0, keepdims=True)
        acc_out[...] = jnp.broadcast_to(bo_ref[...].astype(F32), (total, width))
        acc_gin[...] = jnp.zeros((total, width), F32)

    near = f < steps // 2
    wi = jnp.where(near, wi_own_ref[...], wi_far_ref[...])
    wo = jnp.where(near, wo_own_ref[...], wo_far_ref[...])
    bi = bi_ref[...].astype(F32)
    bias_sum = jnp.zeros(gbi_ref.shape, F32)
    for b in range(0, total, rb):
        sl = slice(b, b + rb)
        v = mm(x_ref[sl, :], wi) + bi
        gh = mm_nt(gout_ref[sl, :], wo)
        vv = v * v
        t = jnp.tanh(v * (GELU_A + (GELU_A * GELU_B) * vv))
        half = 0.5 + 0.5 * t
        hid = (v * half).astype(BF)
        slope = half + (half * (1.0 - t)) * (v * (GELU_A + (3.0 * GELU_A * GELU_B) * vv))
        gp = (gh * slope).astype(BF)
        hid_ref[sl, :] = hid
        gp_ref[sl, :] = gp
        bias_sum = bias_sum + jnp.sum(gp.astype(F32), axis=0, keepdims=True)
        acc_out[sl, :] += mm(hid, wo)
        acc_gin[sl, :] += mm_nt(gp, wi)
    gbi_ref[...] = bias_sum

    @pl.when(f == steps - 1)
    def _():
        probs = prob[...]
        chosen = jnp.sum(jnp.where(mine, probs, 0.0), axis=-1, keepdims=True)
        eo = acc_out[...].astype(BF).astype(F32)
        out_ref[...] = (chosen * eo).astype(BF)
        gc = jnp.sum(eo * c_ref[...].astype(F32), axis=-1, keepdims=True)
        gl = (gc * chosen) * (jnp.where(mine, 1.0, 0.0) - probs)
        router = router_ref[...].astype(F32)
        extra = lax.dot_general(
            gl, router, (((1,), (1,)), ((), ())), precision=lax.Precision.HIGHEST, preferred_element_type=F32
        )
        gin_ref[...] = (acc_gin[...] + extra).astype(BF)
        high = gl.astype(BF)
        low = (gl - high.astype(F32)).astype(BF)
        grouter_ref[...] = mm_tn(x_ref[...], high) + mm_tn(x_ref[...], low)


def expert_pass(x, c, wi_own, wi_far, wo_own, wo_far, bi, bo, router, axis):
    total, width = x.shape
    half = wi_own.shape[1]
    chunk = 512 if half % 512 == 0 else half
    per = half // chunk
    steps = 2 * per
    experts = router.shape[1]
    near = lambda f: jnp.minimum(f, per - 1)
    far = lambda f: jnp.maximum(f - per, 0)
    act = pl.BlockSpec((total, chunk), lambda f: (0, f))
    return pl.pallas_call(
        functools.partial(expert_kernel, rb=pack_step(total), axis=axis),
        grid=(steps,),
        out_shape=(
            jax.ShapeDtypeStruct((total, 2 * half), BF),
            jax.ShapeDtypeStruct((total, 2 * half), BF),
            jax.ShapeDtypeStruct((total, width), BF),
            jax.ShapeDtypeStruct((total, width), BF),
            jax.ShapeDtypeStruct((total, width), BF),
            jax.ShapeDtypeStruct((1, 2 * half), F32),
            jax.ShapeDtypeStruct((1, width), F32),
            jax.ShapeDtypeStruct((width, experts), F32),
        ),
        in_specs=[
            whole((total, width)),
            whole((total, width)),
            pl.BlockSpec((width, chunk), lambda f: (0, near(f))),
            pl.BlockSpec((width, chunk), lambda f: (0, far(f))),
            pl.BlockSpec((chunk, width), lambda f: (near(f), 0)),
            pl.BlockSpec((chunk, width), lambda f: (far(f), 0)),
            pl.BlockSpec((1, chunk), lambda f: (0, f)),
            whole((1, width)),
            whole((width, experts)),
        ],
        out_specs=(
            act,
            act,
            whole((total, width)),
            whole((total, width)),
            whole((total, width)),
            pl.BlockSpec((1, chunk), lambda f: (0, f)),
            whole((1, width)),
            whole((width, experts)),
        ),
        scratch_shapes=[
            pltpu.VMEM((total, width), F32),
            pltpu.VMEM((total, width), F32),
            pltpu.VMEM((total, experts), F32),
        ],
        compiler_params=params(),
        cost_estimate=pl.CostEstimate(
            flops=16 * total * width * half, bytes_accessed=40 * 1024 * 1024, transcendentals=2 * total * half
        ),
        name="expert_pass",
    )(x, c, wi_own, wi_far, wo_own, wo_far, bi, bo, router)


def weight_kernel(x_ref, hid_ref, g_ref, gp_ref, dwi_ref, dwo_ref):
    dwo_ref[...] = mm_tn(hid_ref[...], g_ref[...]).astype(BF)
    dwi_ref[...] = mm_tn(x_ref[...], gp_ref[...]).astype(BF)


def weight_pass(x, hid, g, gp, first):
    total, width = x.shape
    half = hid.shape[1] // 2
    chunk = 512 if half % 512 == 0 else half
    per = half // chunk
    act = pl.BlockSpec((total, chunk), lambda f: (0, f + first * per))
    return pl.pallas_call(
        weight_kernel,
        grid=(per,),
        out_shape=(
            jax.ShapeDtypeStruct((width, half), BF),
            jax.ShapeDtypeStruct((half, width), BF),
        ),
        in_specs=[whole((total, width)), act, whole((total, width)), act],
        out_specs=(
            pl.BlockSpec((width, chunk), lambda f: (0, f)),
            pl.BlockSpec((chunk, width), lambda f: (f, 0)),
        ),
        compiler_params=params(),
        cost_estimate=pl.CostEstimate(
            flops=4 * total * width * half, bytes_accessed=20 * 1024 * 1024, transcendentals=0
        ),
        name="weight_pass",
    )(x, hid, g, gp)


def live_rows(count, patch, rows):
    row = lax.broadcasted_iota(jnp.int32, (rows, 1), 0)
    return row < count * patch


def output_kernel(count_ref, patch_ref, pick_ref, slot_ref, back_ref, res_ref, out_ref, *, capacity):
    live = live_rows(count_ref[0], patch_ref[0], res_ref.shape[0])
    mixture = unpack_rows(back_ref, pick_ref[...], slot_ref[...], capacity)
    out_ref[...] = jnp.where(live, res_ref[...] + mixture, 0.0).astype(BF)


def output_pass(count, patch, picks, slots, back, res, capacity):
    rows, width = res.shape
    return pl.pallas_call(
        functools.partial(output_kernel, capacity=capacity),
        out_shape=jax.ShapeDtypeStruct((rows, width), BF),
        in_specs=[pl.BlockSpec(memory_space=SMEM)] * 2 + [pl.BlockSpec(memory_space=VM)] * 4,
        out_specs=pl.BlockSpec(memory_space=VM),
        compiler_params=params(),
        cost_estimate=pl.CostEstimate(
            flops=2 * back.shape[0] * rows * width, bytes_accessed=6 * 1024 * 1024, transcendentals=0
        ),
        name="output_pass",
    )(count, patch, picks, slots, back, res)


def middle_kernel(
    count_ref,
    patch_ref,
    pick_ref,
    slot_ref,
    back_ref,
    cot_ref,
    res_ref,
    gain2_ref,
    mixed_ref,
    wo_ref,
    gres_ref,
    gmix_ref,
    dwo_ref,
    ggain_ref,
    gshift_ref,
    *,
    capacity,
):
    live = live_rows(count_ref[0], patch_ref[0], res_ref.shape[0])
    gn = unpack_rows(back_ref, pick_ref[...], slot_ref[...], capacity)
    unit, inv = standardize(res_ref[...])
    ggain_ref[...] = jnp.sum(gn * unit, axis=0, keepdims=True)
    gshift_ref[...] = jnp.sum(gn, axis=0, keepdims=True)
    gout = jnp.where(live, cot_ref[...].astype(F32), 0.0)
    gres = gout + norm_back(gn, gain2_ref[...], unit, inv)
    gres_ref[...] = gres
    branch = gres.astype(BF)
    gmix_ref[...] = mm_nt(branch, wo_ref[...]).astype(BF)
    dwo_ref[...] = mm_tn(mixed_ref[...], branch).astype(BF)


def middle_pass(count, patch, picks, slots, back, cot, res, g2, mixed, wo, capacity):
    rows, width = res.shape
    vm = pl.BlockSpec(memory_space=VM)
    return pl.pallas_call(
        functools.partial(middle_kernel, capacity=capacity),
        out_shape=(
            jax.ShapeDtypeStruct((rows, width), F32),
            jax.ShapeDtypeStruct((rows, width), BF),
            jax.ShapeDtypeStruct((width, width), BF),
            jax.ShapeDtypeStruct((1, width), F32),
            jax.ShapeDtypeStruct((1, width), F32),
        ),
        in_specs=[pl.BlockSpec(memory_space=SMEM)] * 2 + [vm] * 8,
        out_specs=(vm,) * 5,
        compiler_params=params(),
        cost_estimate=pl.CostEstimate(
            flops=2 * rows * width * (back.shape[0] + 2 * width),
            bytes_accessed=14 * 1024 * 1024,
            transcendentals=0,
        ),
        name="middle_pass",
    )(count, patch, picks, slots, back, cot, res, g2, mixed, wo)


def attend_back_kernel(
    n1_ref,
    q_ref,
    k_ref,
    v_ref,
    p_ref,
    linv_ref,
    mixed_ref,
    gmix_ref,
    dq_ref,
    dk_ref,
    dv_ref,
    dwq_ref,
    dwk_ref,
    dwv_ref,
    ds_ref,
    *,
    head_dim,
    qb,
):
    rows, cols = q_ref.shape
    lane = lax.broadcasted_iota(jnp.int32, (rows, 2 * head_dim), 1)
    scale = jnp.asarray(head_dim ** (-0.5), BF)
    zero = jnp.zeros((rows, 2 * head_dim), BF)
    for pair in range(cols // (2 * head_dim)):
        sl = slice(pair * 2 * head_dim, (pair + 1) * 2 * head_dim)
        q_pair = q_ref[:, sl] * scale
        k_pair = k_ref[:, sl] * scale
        v_pair = v_ref[:, sl]
        do_pair = (gmix_ref[:, sl].astype(F32) * linv_ref[:, sl]).astype(BF)
        inner = do_pair.astype(F32) * mixed_ref[:, sl].astype(F32)
        dq = None
        for h in range(2):
            mine = (lane >= h * head_dim) & (lane < (h + 1) * head_dim)
            dom = jnp.where(mine, do_pair, zero)
            qm = jnp.where(mine, q_pair, zero)
            km = jnp.where(mine, k_pair, zero)
            row_inner = jnp.sum(jnp.where(mine, inner, 0.0), axis=-1, keepdims=True)
            head = pair * 2 + h
            for b in range(0, rows, qb):
                dp = mm_nt(dom[b : b + qb], v_pair)
                p = p_ref[head, b : b + qb, :].astype(F32)
                ds_ref[b : b + qb, :] = (p * (dp - row_inner[b : b + qb])).astype(BF)
            ds = ds_ref[...]
            dq_h = mm(ds, km)
            dk_h = mm_tn(ds, qm)
            dv_h = mm_tn(p_ref[head], dom)
            if h == 0:
                dq, dk, dv = dq_h, dk_h, dv_h
            else:
                dq, dk, dv = dq + dq_h, dk + dk_h, dv + dv_h
        dq_ref[:, sl] = dq.astype(BF)
        dk_ref[:, sl] = dk.astype(BF)
        dv_ref[:, sl] = dv.astype(BF)
    dwq_ref[...] = mm_tn(n1_ref[...], dq_ref[...]).astype(BF)
    dwk_ref[...] = mm_tn(n1_ref[...], dk_ref[...]).astype(BF)
    dwv_ref[...] = mm_tn(n1_ref[...], dv_ref[...]).astype(BF)


def attend_back(n1, q, k, v, p, linv, mixed, gmix):
    rows, width = n1.shape
    head_dim = width // HEADS
    quad = 4 * head_dim
    steps = width // quad
    seq = pl.BlockSpec((rows, quad), lambda j: (0, j))
    col = pl.BlockSpec((width, quad), lambda j: (0, j))
    return pl.pallas_call(
        functools.partial(attend_back_kernel, head_dim=head_dim, qb=rows // 5),
        grid=(steps,),
        out_shape=(jax.ShapeDtypeStruct((rows, width), BF),) * 3
        + (jax.ShapeDtypeStruct((width, width), BF),) * 3,
        in_specs=[
            whole((rows, width)),
            seq,
            seq,
            seq,
            pl.BlockSpec((4, rows, rows), lambda j: (j, 0, 0)),
            seq,
            seq,
            seq,
        ],
        out_specs=(seq, seq, seq, col, col, col),
        scratch_shapes=[pltpu.VMEM((rows, rows), BF)],
        compiler_params=params(),
        cost_estimate=pl.CostEstimate(
            flops=2 * rows * width * (3 * width + 4 * rows), bytes_accessed=24 * 1024 * 1024, transcendentals=0
        ),
        name="attend_back",
    )(n1, q, k, v, p, linv, mixed, gmix)


def tokens_kernel(
    dq_ref, dk_ref, dv_ref, wq_ref, wk_ref, wv_ref, tokens_ref, gain1_ref, gres_ref, gtok_ref, ggain_ref, gshift_ref
):
    gn = mm_nt(dq_ref[...], wq_ref[...]) + mm_nt(dk_ref[...], wk_ref[...]) + mm_nt(dv_ref[...], wv_ref[...])
    unit, inv = standardize(tokens_ref[...].astype(F32))
    ggain_ref[...] = jnp.sum(gn * unit, axis=0, keepdims=True)
    gshift_ref[...] = jnp.sum(gn, axis=0, keepdims=True)
    gtok_ref[...] = gres_ref[...] + norm_back(gn, gain1_ref[...], unit, inv)


def tokens_pass(dq, dk, dv, wq, wk, wv, tokens, g1, gres):
    rows, width = tokens.shape
    vm = pl.BlockSpec(memory_space=VM)
    return pl.pallas_call(
        tokens_kernel,
        out_shape=(
            jax.ShapeDtypeStruct((rows, width), F32),
            jax.ShapeDtypeStruct((1, width), F32),
            jax.ShapeDtypeStruct((1, width), F32),
        ),
        in_specs=[vm] * 9,
        out_specs=(vm,) * 3,
        compiler_params=params(),
        cost_estimate=pl.CostEstimate(
            flops=6 * rows * width * width, bytes_accessed=12 * 1024 * 1024, transcendentals=0
        ),
        name="tokens_pass",
    )(dq, dk, dv, wq, wk, wv, tokens, g1, gres)


def swap(value, axis, size, bit):
    return lax.ppermute(value, axis, [(i, i ^ bit) for i in range(size)])


def shards(
    tokens,
    cotangent,
    ln1_gain,
    ln1_shift,
    w_query,
    w_key,
    w_value,
    w_output,
    ln2_gain,
    ln2_shift,
    w_router,
    w_inner,
    b_inner,
    w_outer,
    b_outer,
    image_count,
    patches,
    picks,
    slots,
):
    rows, width = tokens.shape
    experts = w_router.shape[1]
    groups = lax.axis_size("expert")
    capacity = 21 * rows // (10 * experts)
    total = experts * capacity
    half = w_inner.shape[2]
    g1, s1 = ln1_gain[None, :], ln1_shift[None, :]
    g2, s2 = ln2_gain[None, :], ln2_shift[None, :]
    pick_rows, slot_rows = picks.T, slots.T

    def exchange(rows_out):
        return lax.all_to_all(
            rows_out.reshape(experts, capacity, width), "expert", split_axis=0, concat_axis=0, tiled=True
        ).reshape(total, width)

    cot_in = exchange(pack(pick_rows, slot_rows, cotangent, total, capacity))
    wi_own, wo_own = w_inner[0], w_outer[0]
    wi_far = swap(wi_own, "hidden", 2, 1)
    wo_far = swap(wo_own, "hidden", 2, 1)
    bi_all = jnp.concatenate([b_inner, swap(b_inner, "hidden", 2, 1)], axis=1)
    n1, q, k, v, p, linv, mixed, res, outgoing = front(
        image_count, patches, tokens, g1, s1, w_query, w_key, w_value, w_output, g2, s2,
        pick_rows, slot_rows, total, capacity,
    )
    x = exchange(outgoing)
    hid, gp, gout, out_rows, gin_rows, gbi, gbo, grouter = expert_pass(
        x, cot_in, wi_own, wi_far, wo_own, wo_far, bi_all, b_outer, w_router, "expert"
    )
    gin_back = exchange(gin_rows)
    dwi_far, dwo_far = weight_pass(x, hid, gout, gp, 1)
    dwi_own, dwo_own = weight_pass(x, hid, gout, gp, 0)
    out_back = exchange(out_rows)
    dwi = dwi_own.astype(F32) + swap(dwi_far, "hidden", 2, 1).astype(F32)
    dwo = dwo_own.astype(F32) + swap(dwo_far, "hidden", 2, 1).astype(F32)
    dwi = lax.psum(dwi.astype(BF), "dp").astype(F32)
    dwo = lax.psum(dwo.astype(BF), "dp").astype(F32)
    gbi = lax.psum(gbi[:, :half] + swap(gbi[:, half:], "hidden", 2, 1), "dp")
    gbo = lax.psum(gbo, ("hidden", "dp"))

    gres, gmix, dwout, ggain2, gshift2 = middle_pass(
        image_count, patches, picks, slots, gin_back, cotangent, res, g2, mixed, w_output, capacity
    )
    dq, dk, dv, dwq, dwk, dwv = attend_back(n1, q, k, v, p, linv, mixed, gmix)
    gtok, ggain1, gshift1 = tokens_pass(dq, dk, dv, w_query, w_key, w_value, tokens, g1, gres)
    block_out = output_pass(image_count, patches, picks, slots, out_back, res, capacity)
    everyone = ("expert", "hidden", "dp")
    dwq, dwk, dwv, dwout = lax.psum((dwq, dwk, dwv, dwout), everyone)
    ggain1, gshift1, ggain2, gshift2, grouter = lax.psum((ggain1, gshift1, ggain2, gshift2, grouter), everyone)
    return (
        block_out,
        gtok,
        ggain1[0],
        gshift1[0],
        dwq.astype(F32),
        dwk.astype(F32),
        dwv.astype(F32),
        dwout.astype(F32),
        ggain2[0],
        gshift2[0],
        grouter,
        dwi[None],
        gbi,
        dwo[None],
        gbo,
    )


def solution(mesh):
    rows = P(("expert", "hidden", "dp"), None)
    device = P(("expert", "hidden", "dp"))
    inner = P("expert", None, "hidden")
    inner_bias = P("expert", "hidden")
    outer = P("expert", "hidden", None)
    outer_bias = P("expert", None)
    return jax.shard_map(
        shards,
        mesh=mesh,
        in_specs=(rows, rows) + (P(),) * 9 + (inner, inner_bias, outer, outer_bias, device, device, rows, rows),
        out_specs=(rows, rows) + (P(),) * 9 + (inner, inner_bias, outer, outer_bias),
        check_vma=False,
    )
```

```python
import functools

import jax
import jax.numpy as jnp
from jax import lax
from jax.experimental import pallas as pl
from jax.experimental.pallas import tpu as pltpu
from jax.sharding import PartitionSpec as P

HEADS = 12
NORM_EPS = 1e-06
MASKED = -1e30
IMAGES_MAX = 8
BF = jnp.bfloat16
F32 = jnp.float32
VMEM_LIMIT = 63 * 1024 * 1024 + 768 * 1024

VM = pltpu.VMEM
SMEM = pltpu.SMEM


COST = 1.0


def estimate(flops, bytes_accessed, transcendentals):
    return pl.CostEstimate(
        flops=int(COST * flops),
        bytes_accessed=int(COST * bytes_accessed),
        transcendentals=int(COST * transcendentals),
    )


def mm(a, b):
    return lax.dot_general(a, b, (((1,), (0,)), ((), ())), preferred_element_type=F32)


def mm_nt(a, b):
    return lax.dot_general(a, b, (((1,), (1,)), ((), ())), preferred_element_type=F32)


def mm_tn(a, b):
    return lax.dot_general(a, b, (((0,), (0,)), ((), ())), preferred_element_type=F32)


def standardize(values):
    center = jnp.mean(values, axis=-1, keepdims=True)
    centered = values - center
    moment = jnp.mean(centered * centered, axis=-1, keepdims=True)
    inv = lax.rsqrt(moment + NORM_EPS)
    return centered * inv, inv


def norm_back(grad_normed, gain, unit, inv):
    g = grad_normed * gain
    first = jnp.mean(g, axis=-1, keepdims=True)
    second = jnp.mean(g * unit, axis=-1, keepdims=True)
    return (g - first - unit * second) * inv


def targets(picks, slots, capacity, base):
    return jnp.where(slots >= 0, jnp.bitwise_xor(picks, base) * capacity + slots, -1)


def pack_into(out_refs, rows_ref, dest):
    for i, out_ref in enumerate(out_refs):
        total, rows = out_ref.shape[0], rows_ref.shape[0]
        step = pack_step(total)
        for start in range(0, total, step):
            index = lax.broadcasted_iota(jnp.int32, (step, rows), 0) + (start + i * total)
            hit = (index == dest[0:1, :]) | (index == dest[1:2, :])
            out_ref[start : start + step, :] = mm(hit.astype(BF), rows_ref[...]).astype(BF)


def unpack_rows(buffer_refs, dest, place=None):
    values = [ref[...] if len(ref.shape) == 2 else ref[place] for ref in buffer_refs]
    buffer = values[0] if len(values) == 1 else jnp.concatenate(values, axis=0)
    index = lax.broadcasted_iota(jnp.int32, (dest.shape[0], buffer.shape[0]), 1)
    hit = (index == dest[:, 0:1]) | (index == dest[:, 1:2])
    return mm(hit.astype(BF), buffer)


def kernel_call(body, inputs, in_specs, after=(), **options):
    def run(*refs):
        body(*refs[len(after) :])

    specs = [pl.BlockSpec(memory_space=pl.ANY)] * len(after) + list(in_specs)
    return pl.pallas_call(run, in_specs=specs, compiler_params=params(), **options)(*after, *inputs)


def pack_step(total):
    for step in (448, 336, 224, 192, 112, 96, 64, 48, 32, 16):
        if total % step == 0:
            return step
    return total


def params():
    return pltpu.CompilerParams(vmem_limit_bytes=VMEM_LIMIT)


def whole(shape):
    return pl.BlockSpec(shape, lambda *_: (0,) * len(shape))


def pack_kernel(base_ref, pick_ref, slot_ref, rows_ref, *out_refs, capacity):
    pack_into(out_refs, rows_ref, targets(pick_ref[...], slot_ref[...], capacity, base_ref[0]))


def pack(base, pick_rows, slot_rows, rows, buffers, capacity):
    count, width = rows.shape
    total = sum(shape[0] for shape in buffers)
    return kernel_call(
        functools.partial(pack_kernel, capacity=capacity),
        (base, pick_rows, slot_rows, rows),
        [pl.BlockSpec(memory_space=SMEM)] + [pl.BlockSpec(memory_space=VM)] * 3,
        out_shape=tuple(jax.ShapeDtypeStruct(shape, BF) for shape in buffers),
        out_specs=(pl.BlockSpec(memory_space=VM),) * len(buffers),
        cost_estimate=estimate(
            flops=2 * total * count * width, bytes_accessed=4 * total * width, transcendentals=0
        ),
        name="pack_rows",
    )


def classes(count, patch, rows, padding):
    row = lax.broadcasted_iota(jnp.int32, (rows, 1), 0)
    image = jnp.zeros((rows, 1), jnp.int32)
    for i in range(1, IMAGES_MAX):
        image = image + (row >= i * patch).astype(jnp.int32)
    return jnp.where(row < count * patch, image, padding)


def front_kernel(
    base_ref,
    count_ref,
    patch_ref,
    tokens_ref,
    gain1_ref,
    shift1_ref,
    wq_ref,
    wk_ref,
    wv_ref,
    wo_ref,
    gain2_ref,
    shift2_ref,
    pick_ref,
    slot_ref,
    n1_ref,
    q_ref,
    k_ref,
    v_ref,
    p_ref,
    linv_ref,
    mixed_ref,
    res_ref,
    *rest,
    capacity,
    head_dim,
    qb,
):
    *out_refs, n2_ref = rest
    j = pl.program_id(0)
    rows, width = tokens_ref.shape
    cols = wq_ref.shape[1]

    @pl.when(j == 0)
    def _():
        x = tokens_ref[...].astype(F32)
        unit, _ = standardize(x)
        n1_ref[...] = (unit * gain1_ref[...] + shift1_ref[...]).astype(BF)
        res_ref[...] = x

    n1 = n1_ref[...]
    q_ref[...] = mm(n1, wq_ref[...]).astype(BF)
    k_ref[...] = mm(n1, wk_ref[...]).astype(BF)
    v_ref[...] = mm(n1, wv_ref[...]).astype(BF)
    cls = classes(count_ref[0], patch_ref[0], rows, head_dim - 1)
    lane = lax.broadcasted_iota(jnp.int32, (rows, 2 * head_dim), 1)
    inner = lane % head_dim
    apart = jnp.where(inner == cls, 0.0, MASKED).astype(BF)
    member = jnp.where(inner == cls, 1.0, 0.0).astype(BF)
    ones = jnp.ones((rows, 2 * head_dim), BF)
    scale = head_dim ** (-0.5)
    for pair in range(cols // (2 * head_dim)):
        sl = slice(pair * 2 * head_dim, (pair + 1) * 2 * head_dim)
        q_pair = q_ref[:, sl] * jnp.asarray(scale, BF)
        k_pair = k_ref[:, sl]
        v_ext = jnp.concatenate([v_ref[:, sl], ones], axis=1)
        for h in range(2):
            mine = (lane >= h * head_dim) & (lane < (h + 1) * head_dim)
            qm = jnp.where(mine, q_pair, apart)
            km = jnp.where(mine, k_pair, member)
            for b in range(0, rows, qb):
                s = mm_nt(qm[b : b + qb], km)
                top = jnp.max(s, axis=-1, keepdims=True)
                p = jnp.exp(s - top).astype(BF)
                p_ref[pair * 2 + h, b : b + qb, :] = p
                ov = mm(p, v_ext)
                linv = 1.0 / ov[:, 2 * head_dim :]
                o = (ov[:, : 2 * head_dim] * linv).astype(BF)
                if h == 0:
                    mixed_ref[b : b + qb, sl] = o
                    linv_ref[b : b + qb, sl] = linv
                else:
                    keep = mine[b : b + qb]
                    mixed_ref[b : b + qb, sl] = jnp.where(keep, o, mixed_ref[b : b + qb, sl])
                    linv_ref[b : b + qb, sl] = jnp.where(keep, linv, linv_ref[b : b + qb, sl])
    res_ref[...] += mm(mixed_ref[...], wo_ref[...])

    @pl.when(j == pl.num_programs(0) - 1)
    def _():
        unit, _ = standardize(res_ref[...])
        n2_ref[...] = (unit * gain2_ref[...] + shift2_ref[...]).astype(BF)
        pack_into(out_refs, n2_ref, targets(pick_ref[...], slot_ref[...], capacity, base_ref[0]))


def front(base, count, patch, tokens, g1, s1, wq, wk, wv, wo, g2, s2, pick_rows, slot_rows, buffers, capacity, after):
    rows, width = tokens.shape
    head_dim = width // HEADS
    quad = 4 * head_dim
    steps = width // quad
    col = pl.BlockSpec((width, quad), lambda j: (0, j))
    seq = pl.BlockSpec((rows, quad), lambda j: (0, j))
    smem = pl.BlockSpec(memory_space=SMEM)
    total = sum(shape[0] for shape in buffers)
    flops = 2 * rows * width * (4 * width + 2 * rows + total)
    row = jax.ShapeDtypeStruct((rows, width), BF)
    wide = jax.ShapeDtypeStruct((rows, width), F32)
    return kernel_call(
        functools.partial(front_kernel, capacity=capacity, head_dim=head_dim, qb=rows // 5),
        (base, count, patch, tokens, g1, s1, wq, wk, wv, wo, g2, s2, pick_rows, slot_rows),
        [
            smem,
            smem,
            smem,
            whole((rows, width)),
            whole((1, width)),
            whole((1, width)),
            col,
            col,
            col,
            pl.BlockSpec((quad, width), lambda j: (j, 0)),
            whole((1, width)),
            whole((1, width)),
            whole(pick_rows.shape),
            whole(slot_rows.shape),
        ],
        after,
        grid=(steps,),
        out_shape=(row, row, row, row, jax.ShapeDtypeStruct((HEADS, rows, rows), BF), wide, row, wide)
        + tuple(jax.ShapeDtypeStruct(shape, BF) for shape in buffers),
        out_specs=(
            whole((rows, width)),
            seq,
            seq,
            seq,
            pl.BlockSpec((4, rows, rows), lambda j: (j, 0, 0)),
            seq,
            seq,
            whole((rows, width)),
        )
        + tuple(whole(shape) for shape in buffers),
        scratch_shapes=[pltpu.VMEM((rows, width), BF)],
        cost_estimate=estimate(
            flops=flops, bytes_accessed=30 * 1024 * 1024, transcendentals=HEADS * rows * rows
        ),
        name="front",
    )


GELU_A = 0.7978845608028654
GELU_B = 0.044715


def expert_kernel(base_ref, c_ref, *refs, which, axis):
    blocks = len(which)
    x_refs, refs = refs[:blocks], refs[blocks:]
    wi_own_ref, wi_far_ref, wo_own_ref, wo_far_ref, bi_ref, bo_ref, router_ref = refs[:7]
    hid_ref, gp_ref, gout_ref, gbi_ref, gbo_ref, grouter_ref = refs[7:13]
    out_refs, gin_refs = refs[13 : 13 + blocks], refs[13 + blocks : 13 + 2 * blocks]
    acc_out, acc_gin, prob = refs[13 + 2 * blocks :]
    f = pl.program_id(0)
    steps = pl.num_programs(0)
    size, width = x_refs[0].shape
    experts = router_ref.shape[1]
    mine = lax.broadcasted_iota(jnp.int32, (size, experts), 1) == lax.axis_index(axis)

    def cot_rows(i):
        place = jnp.bitwise_xor(base_ref[0], which[i]) * size
        return c_ref[pl.ds(pl.multiple_of(place, 16), size), :].astype(F32)

    @pl.when(f == 0)
    def _():
        total = jnp.zeros((1, width), F32)
        for i in range(blocks):
            sl = slice(i * size, (i + 1) * size)
            logits = mm(x_refs[i][...], router_ref[...])
            powers = jnp.exp(logits - jnp.max(logits, axis=-1, keepdims=True))
            probs = powers / jnp.sum(powers, axis=-1, keepdims=True)
            prob[sl, :] = probs
            chosen = jnp.sum(jnp.where(mine, probs, 0.0), axis=-1, keepdims=True)
            grads = (chosen * cot_rows(i)).astype(BF)
            gout_ref[sl, :] = grads
            total = total + jnp.sum(grads.astype(F32), axis=0, keepdims=True)
        gbo_ref[...] = total
        acc_out[...] = jnp.broadcast_to(bo_ref[...].astype(F32), acc_out.shape)
        acc_gin[...] = jnp.zeros(acc_gin.shape, F32)

    near = f < steps // 2
    wi = jnp.where(near, wi_own_ref[...], wi_far_ref[...])
    wo = jnp.where(near, wo_own_ref[...], wo_far_ref[...])
    bi = bi_ref[...].astype(F32)
    bias_sum = jnp.zeros(gbi_ref.shape, F32)
    step = pack_step(size)
    for i in range(blocks):
        for start in range(0, size, step):
            sl = slice(i * size + start, i * size + start + step)
            v = mm(x_refs[i][start : start + step, :], wi) + bi
            gh = mm_nt(gout_ref[sl, :], wo)
            vv = v * v
            t = jnp.tanh(v * (GELU_A + (GELU_A * GELU_B) * vv))
            half = 0.5 + 0.5 * t
            hid = (v * half).astype(BF)
            slope = half + (half * (1.0 - t)) * (v * (GELU_A + (3.0 * GELU_A * GELU_B) * vv))
            gp = (gh * slope).astype(BF)
            hid_ref[0, sl, :] = hid
            gp_ref[0, sl, :] = gp
            bias_sum = bias_sum + jnp.sum(gp.astype(F32), axis=0, keepdims=True)
            acc_out[sl, :] += mm(hid, wo)
            acc_gin[sl, :] += mm_nt(gp, wi)
    gbi_ref[...] = bias_sum

    @pl.when(f == steps - 1)
    def _():
        router = router_ref[...].astype(F32)
        grouter = jnp.zeros(grouter_ref.shape, F32)
        for i in range(blocks):
            sl = slice(i * size, (i + 1) * size)
            probs = prob[sl, :]
            chosen = jnp.sum(jnp.where(mine, probs, 0.0), axis=-1, keepdims=True)
            eo = acc_out[sl, :].astype(BF).astype(F32)
            out_refs[i][...] = (chosen * eo).astype(BF)
            gc = jnp.sum(eo * cot_rows(i), axis=-1, keepdims=True)
            gl = (gc * chosen) * (jnp.where(mine, 1.0, 0.0) - probs)
            extra = lax.dot_general(
                gl,
                router,
                (((1,), (1,)), ((), ())),
                precision=lax.Precision.HIGHEST,
                preferred_element_type=F32,
            )
            gin = (acc_gin[sl, :] + extra).astype(BF)
            if len(gin_refs[i].shape) == 2:
                gin_refs[i][...] = gin
            else:
                gin_refs[i][0] = gin
                gin_refs[i][1] = gin
            high = gl.astype(BF)
            low = (gl - high.astype(F32)).astype(BF)
            x = x_refs[i][...]
            grouter = grouter + mm_tn(high, x) + mm_tn(low, x)
        grouter_ref[...] = grouter


def expert_pass(base, cot, xs, which, twice, wi_own, wi_far, wo_own, wo_far, bi, bo, router, axis, after):
    size, width = xs[0].shape
    blocks = len(xs)
    total = blocks * size
    half = wi_own.shape[1]
    chunk = 512 if half % 512 == 0 else half
    per = half // chunk
    steps = 2 * per
    experts = router.shape[1]
    near = lambda f: jnp.minimum(f, per - 1)
    far = lambda f: jnp.maximum(f - per, 0)
    act = pl.BlockSpec((1, total, chunk), lambda f: (f, 0, 0))
    piece = (size, width)
    back = (2, size, width) if twice else piece
    results = kernel_call(
        functools.partial(expert_kernel, which=which, axis=axis),
        (base, cot, *xs, wi_own, wi_far, wo_own, wo_far, bi, bo, router),
        [pl.BlockSpec(memory_space=SMEM), whole(cot.shape)]
        + [whole((size, width))] * blocks
        + [
            pl.BlockSpec((width, chunk), lambda f: (0, near(f))),
            pl.BlockSpec((width, chunk), lambda f: (0, far(f))),
            pl.BlockSpec((chunk, width), lambda f: (near(f), 0)),
            pl.BlockSpec((chunk, width), lambda f: (far(f), 0)),
            pl.BlockSpec((1, chunk), lambda f: (0, f)),
            whole((1, width)),
            whole((width, experts)),
        ],
        after,
        grid=(steps,),
        out_shape=(
            jax.ShapeDtypeStruct((steps, total, chunk), BF),
            jax.ShapeDtypeStruct((steps, total, chunk), BF),
            jax.ShapeDtypeStruct((total, width), BF),
            jax.ShapeDtypeStruct((1, 2 * half), F32),
            jax.ShapeDtypeStruct((1, width), F32),
            jax.ShapeDtypeStruct((experts, width), F32),
        )
        + (jax.ShapeDtypeStruct(piece, BF),) * blocks
        + (jax.ShapeDtypeStruct(back, BF),) * blocks,
        out_specs=(
            act,
            act,
            whole((total, width)),
            pl.BlockSpec((1, chunk), lambda f: (0, f)),
            whole((1, width)),
            whole((experts, width)),
        )
        + (whole(piece),) * blocks
        + (whole(back),) * blocks,
        scratch_shapes=[
            pltpu.VMEM((total, width), F32),
            pltpu.VMEM((total, width), F32),
            pltpu.VMEM((total, experts), F32),
        ],
        cost_estimate=estimate(
            flops=16 * total * width * half, bytes_accessed=20 * 1024 * 1024, transcendentals=2 * total * half
        ),
        name="expert_pass",
    )
    return results[:6], results[6 : 6 + blocks], results[6 + blocks :]


def outer_kernel(*refs, counts):
    groups = []
    for count in counts:
        values = [ref[...] if len(ref.shape) == 2 else ref[0] for ref in refs[:count]]
        groups.append(values[0] if count == 1 else jnp.concatenate(values, axis=0))
        refs = refs[count:]
    x, g, hid_far, hid_own, gp_far, gp_own = groups
    wo_far_ref, wo_own_ref, wi_far_ref, wi_own_ref = refs
    wo_far_ref[...] = mm_tn(hid_far, g).astype(BF)
    wo_own_ref[...] = mm_tn(hid_own, g).astype(BF)
    wi_far_ref[...] = mm_tn(x, gp_far).astype(BF)
    wi_own_ref[...] = mm_tn(x, gp_own).astype(BF)


def outer_pass(xs, gouts, hids, gps, half, after=()):
    width = xs[0].shape[1]
    total = sum(x.shape[0] for x in xs)
    chunk = hids[0].shape[2]
    per = half // chunk
    cut = lambda values, first: [
        pl.BlockSpec((1, *value.shape[1:]), lambda f: (f + first * per, 0, 0)) for value in values
    ]
    full = lambda values: [whole(value.shape) for value in values]
    groups = (xs, gouts, hids, hids, gps, gps)
    outer = jax.ShapeDtypeStruct((half, width), BF)
    inner = jax.ShapeDtypeStruct((width, half), BF)
    return kernel_call(
        functools.partial(outer_kernel, counts=tuple(len(group) for group in groups)),
        [value for group in groups for value in group],
        full(xs) + full(gouts) + cut(hids, 1) + cut(hids, 0) + cut(gps, 1) + cut(gps, 0),
        after,
        grid=(per,),
        out_shape=(outer, outer, inner, inner),
        out_specs=(pl.BlockSpec((chunk, width), lambda f: (f, 0)),) * 2
        + (pl.BlockSpec((width, chunk), lambda f: (0, f)),) * 2,
        cost_estimate=estimate(
            flops=8 * total * width * half, bytes_accessed=30 * 1024 * 1024, transcendentals=0
        ),
        name="outer_pass",
    )


def live_rows(count, patch, rows):
    row = lax.broadcasted_iota(jnp.int32, (rows, 1), 0)
    return row < count * patch


def assemble_kernel(base_ref, *refs):
    *block_refs, out_ref = refs
    size = block_refs[0].shape[0]
    for i, block_ref in enumerate(block_refs):
        place = jnp.bitwise_xor(base_ref[0], i) * size
        out_ref[pl.ds(pl.multiple_of(place, 16), size), :] = block_ref[...]


def assemble(base, blocks, after):
    size, width = blocks[0].shape
    return kernel_call(
        assemble_kernel,
        (base, *blocks),
        [pl.BlockSpec(memory_space=SMEM)] + [pl.BlockSpec(memory_space=VM)] * len(blocks),
        after,
        out_shape=jax.ShapeDtypeStruct((len(blocks) * size, width), BF),
        out_specs=pl.BlockSpec(memory_space=VM),
        cost_estimate=estimate(flops=0, bytes_accessed=4 * len(blocks) * size * width, transcendentals=0),
        name="assemble",
    )


def output_kernel(base_ref, count_ref, patch_ref, pick_ref, slot_ref, res_ref, *rest, capacity):
    *back_refs, out_ref = rest
    live = live_rows(count_ref[0], patch_ref[0], res_ref.shape[0])
    mixture = unpack_rows(back_refs, targets(pick_ref[...], slot_ref[...], capacity, base_ref[0]))
    out_ref[...] = jnp.where(live, res_ref[...] + mixture, 0.0).astype(BF)


def output_pass(base, count, patch, picks, slots, back, res, capacity, after):
    rows, width = res.shape
    return kernel_call(
        functools.partial(output_kernel, capacity=capacity),
        (base, count, patch, picks, slots, res, *back),
        [pl.BlockSpec(memory_space=SMEM)] * 3 + [pl.BlockSpec(memory_space=VM)] * (3 + len(back)),
        after,
        out_shape=jax.ShapeDtypeStruct((rows, width), BF),
        out_specs=pl.BlockSpec(memory_space=VM),
        cost_estimate=estimate(
            flops=4 * rows * rows * width, bytes_accessed=6 * 1024 * 1024, transcendentals=0
        ),
        name="output_pass",
    )


def middle_kernel(
    base_ref,
    place_ref,
    core_ref,
    count_ref,
    patch_ref,
    pick_ref,
    slot_ref,
    cot_ref,
    res_ref,
    gain2_ref,
    mixed_ref,
    wo_ref,
    *rest,
    capacity,
):
    *back_refs, gres_ref, gmix_ref, keep_ref, send_ref, ggain_ref, gshift_ref = rest
    live = live_rows(count_ref[0], patch_ref[0], res_ref.shape[0])
    gn = unpack_rows(back_refs, targets(pick_ref[...], slot_ref[...], capacity, base_ref[0]), place_ref[0])
    unit, inv = standardize(res_ref[...])
    ggain_ref[...] = jnp.sum(gn * unit, axis=0, keepdims=True)
    gshift_ref[...] = jnp.sum(gn, axis=0, keepdims=True)
    gout = jnp.where(live, cot_ref[...].astype(F32), 0.0)
    gres = gout + norm_back(gn, gain2_ref[...], unit, inv)
    gres_ref[...] = gres
    branch = gres.astype(BF)
    gmix_ref[...] = mm_nt(branch, wo_ref[...]).astype(BF)
    keep_ref[...] = mm_tn(core_half(mixed_ref, core_ref[0]), branch).astype(BF)
    send_ref[...] = mm_tn(core_half(mixed_ref, 1 - core_ref[0]), branch).astype(BF)


def core_half(ref, core):
    size = ref.shape[1] // 2
    return ref[:, pl.ds(pl.multiple_of(core * size, 128), size)]


def middle_pass(base, place, core, count, patch, picks, slots, back, cot, res, g2, mixed, wo, capacity, after):
    rows, width = res.shape
    vm = pl.BlockSpec(memory_space=VM)
    piece = jax.ShapeDtypeStruct((width // 2, width), BF)
    return kernel_call(
        functools.partial(middle_kernel, capacity=capacity),
        (base, place, core, count, patch, picks, slots, cot, res, g2, mixed, wo, *back),
        [pl.BlockSpec(memory_space=SMEM)] * 5 + [vm] * (7 + len(back)),
        after,
        out_shape=(
            jax.ShapeDtypeStruct((rows, width), F32),
            jax.ShapeDtypeStruct((rows, width), BF),
            piece,
            piece,
            jax.ShapeDtypeStruct((1, width), F32),
            jax.ShapeDtypeStruct((1, width), F32),
        ),
        out_specs=(vm,) * 6,
        cost_estimate=estimate(
            flops=400 * rows * width * (rows + width), bytes_accessed=14 * 1024 * 1024, transcendentals=0
        ),
        name="middle_pass",
    )


def attend_back_kernel(
    core_ref,
    n1_ref,
    q_ref,
    k_ref,
    v_ref,
    p_ref,
    linv_ref,
    mixed_ref,
    gmix_ref,
    dq_ref,
    dk_ref,
    dv_ref,
    keep_ref,
    send_ref,
    ds_ref,
    *,
    head_dim,
    qb,
):
    rows, cols = q_ref.shape
    lane = lax.broadcasted_iota(jnp.int32, (rows, 2 * head_dim), 1)
    scale = jnp.asarray(head_dim ** (-0.5), BF)
    zero = jnp.zeros((rows, 2 * head_dim), BF)
    for pair in range(cols // (2 * head_dim)):
        sl = slice(pair * 2 * head_dim, (pair + 1) * 2 * head_dim)
        q_pair = q_ref[:, sl] * scale
        k_pair = k_ref[:, sl] * scale
        v_pair = v_ref[:, sl]
        do_pair = (gmix_ref[:, sl].astype(F32) * linv_ref[:, sl]).astype(BF)
        inner = do_pair.astype(F32) * mixed_ref[:, sl].astype(F32)
        dq = None
        for h in range(2):
            mine = (lane >= h * head_dim) & (lane < (h + 1) * head_dim)
            dom = jnp.where(mine, do_pair, zero)
            qm = jnp.where(mine, q_pair, zero)
            km = jnp.where(mine, k_pair, zero)
            row_inner = jnp.sum(jnp.where(mine, inner, 0.0), axis=-1, keepdims=True)
            head = pair * 2 + h
            for b in range(0, rows, qb):
                dp = mm_nt(dom[b : b + qb], v_pair)
                p = p_ref[head, b : b + qb, :].astype(F32)
                ds_ref[b : b + qb, :] = (p * (dp - row_inner[b : b + qb])).astype(BF)
            ds = ds_ref[...]
            dq_h = mm(ds, km)
            dk_h = mm_tn(ds, qm)
            dv_h = mm_tn(p_ref[head], dom)
            if h == 0:
                dq, dk, dv = dq_h, dk_h, dv_h
            else:
                dq, dk, dv = dq + dq_h, dk + dk_h, dv + dv_h
        dq_ref[:, sl] = dq.astype(BF)
        dk_ref[:, sl] = dk.astype(BF)
        dv_ref[:, sl] = dv.astype(BF)
    grads = jnp.concatenate([dq_ref[...], dk_ref[...], dv_ref[...]], axis=1)
    keep_ref[...] = mm_tn(core_half(n1_ref, core_ref[0]), grads).astype(BF)
    send_ref[...] = mm_tn(core_half(n1_ref, 1 - core_ref[0]), grads).astype(BF)


def attend_back(core, n1, q, k, v, p, linv, mixed, gmix, after):
    rows, width = n1.shape
    head_dim = width // HEADS
    quad = 4 * head_dim
    steps = width // quad
    seq = pl.BlockSpec((rows, quad), lambda j: (0, j))
    grads = pl.BlockSpec((width // 2, 3 * quad), lambda j: (j, 0))
    return kernel_call(
        functools.partial(attend_back_kernel, head_dim=head_dim, qb=rows // 5),
        (core, n1, q, k, v, p, linv, mixed, gmix),
        [
            pl.BlockSpec(memory_space=SMEM),
            whole((rows, width)),
            seq,
            seq,
            seq,
            pl.BlockSpec((4, rows, rows), lambda j: (j, 0, 0)),
            seq,
            seq,
            seq,
        ],
        after,
        grid=(steps,),
        out_shape=(jax.ShapeDtypeStruct((rows, width), BF),) * 3
        + (jax.ShapeDtypeStruct((steps * (width // 2), 3 * quad), BF),) * 2,
        out_specs=(seq, seq, seq, grads, grads),
        scratch_shapes=[pltpu.VMEM((rows, rows), BF)],
        cost_estimate=estimate(
            flops=2 * rows * width * (3 * width + 4 * rows), bytes_accessed=24 * 1024 * 1024, transcendentals=0
        ),
        name="attend_back",
    )


def tokens_kernel(*refs, parts):
    dq_ref, dk_ref, dv_ref, wq_ref, wk_ref, wv_ref, tokens_ref, gain1_ref, gres_ref, ggain2_ref, gshift2_ref = refs[:11]
    gbi_refs, refs = refs[11 : 11 + parts], refs[11 + parts :]
    gbo_refs, refs = refs[:parts], refs[parts:]
    grouter_refs, (gtok_ref, small_ref, sent_ref) = refs[:parts], refs[parts:]
    gn = mm_nt(dq_ref[...], wq_ref[...]) + mm_nt(dk_ref[...], wk_ref[...]) + mm_nt(dv_ref[...], wv_ref[...])
    unit, inv = standardize(tokens_ref[...].astype(F32))
    gtok_ref[...] = gres_ref[...] + norm_back(gn, gain1_ref[...], unit, inv)
    width = gn.shape[1]
    gbi = sum(ref[...] for ref in gbi_refs)
    rows = gbi.shape[1] // 2 // width
    experts = grouter_refs[0].shape[0]
    for out_ref, first in ((small_ref, 0), (sent_ref, rows)):
        out_ref[...] = jnp.zeros(out_ref.shape, F32)
        for i in range(rows):
            out_ref[i : i + 1, :] = gbi[:, (first + i) * width : (first + i + 1) * width]
        out_ref[rows : rows + 1, :] = sum(ref[...] for ref in gbo_refs)
        out_ref[rows + 1 : rows + 2, :] = jnp.sum(gn * unit, axis=0, keepdims=True)
        out_ref[rows + 2 : rows + 3, :] = jnp.sum(gn, axis=0, keepdims=True)
        out_ref[rows + 3 : rows + 4, :] = ggain2_ref[...]
        out_ref[rows + 4 : rows + 5, :] = gshift2_ref[...]
        out_ref[rows + 5 : rows + 5 + experts, :] = sum(ref[...] for ref in grouter_refs)


def tokens_pass(grads, weights, tokens, g1, gres, ggain2, gshift2, sums, after):
    rows, width = tokens.shape
    vm = pl.BlockSpec(memory_space=VM)
    gbi, gbo, grouter = sums
    height = gbi[0].shape[1] // 2 // width + 5 + grouter[0].shape[0]
    small = jax.ShapeDtypeStruct((height + -height % 16, width), F32)
    inputs = (*grads, *weights, tokens, g1, gres, ggain2, gshift2, *gbi, *gbo, *grouter)
    return kernel_call(
        functools.partial(tokens_kernel, parts=len(gbi)),
        inputs,
        [vm] * len(inputs),
        after,
        out_shape=(jax.ShapeDtypeStruct((rows, width), F32), small, small),
        out_specs=(vm,) * 3,
        cost_estimate=estimate(flops=600 * rows * width * width, bytes_accessed=0, transcendentals=0),
        name="tokens_pass",
    )


def swap(value, axis, bit):
    return lax.ppermute(value, axis, [(i, i ^ bit) for i in range(lax.axis_size(axis))])


def block(value, index, count):
    size = value.shape[0] // count
    return lax.dynamic_slice_in_dim(value, index * size, size, 0)


def narrow_sum(*terms):
    return functools.reduce(jnp.add, [term.astype(F32) for term in terms]).astype(BF)


def axis_bits(axis):
    me = lax.axis_index(axis)
    return [(me >> level) & 1 for level in range(lax.axis_size(axis).bit_length() - 1)]


def prefetch_call(body, scalars, inputs, in_specs, grid, out_specs, after, **options):
    def run(scalar_ref, *refs):
        body(scalar_ref, *refs[len(after) :])

    spec = pltpu.PrefetchScalarGridSpec(
        num_scalar_prefetch=1,
        grid=grid,
        in_specs=[pl.BlockSpec(memory_space=pl.ANY)] * len(after) + list(in_specs),
        out_specs=out_specs,
    )
    return pl.pallas_call(run, grid_spec=spec, compiler_params=params(), **options)(scalars, *after, *inputs)


def pick_kernel(index_ref, *refs, counts):
    outs = refs[sum(counts) :]
    for count, out_ref in zip(counts, outs):
        terms, refs = refs[:count], refs[count:]
        out_ref[...] = sum(ref[...].astype(F32) for ref in terms).astype(BF)


def pick_sums(indices, groups, after):
    flat, in_specs, out_specs, shapes, scalars = [], [], [], [], []
    for group, heights, places in groups_of(groups, indices):
        width = group[0].shape[1]
        for value, place in zip(group, places):
            flat.append(value)
            in_specs.append(pl.BlockSpec((heights, width), lambda i, at, k=len(scalars): (at[k], 0)))
            scalars.append(place)
        out_specs.append(whole((heights, width)))
        shapes.append(jax.ShapeDtypeStruct((heights, width), BF))
    return prefetch_call(
        functools.partial(pick_kernel, counts=tuple(len(group) for group, _ in groups)),
        jnp.stack(scalars),
        flat,
        in_specs,
        (1,),
        tuple(out_specs),
        after,
        out_shape=tuple(shapes),
        cost_estimate=estimate(flops=0, bytes_accessed=2 * sum(v.size for v in flat), transcendentals=0),
        name="pick_sums",
    )


def groups_of(groups, indices):
    return [(group, height, places) for (group, height), places in zip(groups, indices)]


def merge_kernel(bits_ref, *refs):
    outs = refs[len(refs) // 3 * 2 :]
    for i, out_ref in enumerate(outs):
        for ref, bit in ((refs[2 * i], bits_ref[i]), (refs[2 * i + 1], 1 - bits_ref[i])):
            size = ref.shape[0]
            out_ref[pl.ds(pl.multiple_of(bit * size, 16), size), :] = ref[...].astype(out_ref.dtype)


def merge(bits, pairs, dtype, after=()):
    flat = [value for pair in pairs for value in pair]
    vm = pl.BlockSpec(memory_space=VM)
    return kernel_call(
        merge_kernel,
        (bits, *flat),
        [pl.BlockSpec(memory_space=SMEM)] + [vm] * len(flat),
        after,
        out_shape=tuple(jax.ShapeDtypeStruct((2 * mine.shape[0], mine.shape[1]), dtype) for mine, _ in pairs),
        out_specs=(vm,) * len(pairs),
        cost_estimate=estimate(flops=0, bytes_accessed=6 * sum(v.size for v in flat), transcendentals=0),
        name="merge",
    )


def matrices_kernel(me_ref, lead_ref, lead_far_ref, main_ref, main_far_ref, small_ref, small_far_ref, *refs):
    *out_refs, total = refs
    size, tail = lead_ref.shape[0], small_ref.shape[0]
    total[:size, :] = (lead_ref[...].astype(F32) + lead_far_ref[...].astype(F32)).astype(BF)
    total[size:, :] = (main_ref[...].astype(F32) + main_far_ref[...].astype(F32)).astype(BF)
    small = (small_ref[...] + small_far_ref[...]).astype(BF)
    for i, out_ref in enumerate(out_refs):
        place = pl.multiple_of(jnp.bitwise_xor(me_ref[0], i) * size, 16)
        out_ref[:size, :] = total[pl.ds(place, size), :]
        out_ref[size : size + tail, :] = small


def matrices(me, lead, lead_far, main, main_far, small, small_far):
    size, width = lead.shape
    count = 1 + main.shape[0] // size
    shape = jax.ShapeDtypeStruct((size + small.shape[0], width), BF)
    vm = pl.BlockSpec(memory_space=VM)
    return kernel_call(
        matrices_kernel,
        (me, lead, lead_far, main, main_far, small, small_far),
        [pl.BlockSpec(memory_space=SMEM)] + [vm] * 6,
        out_shape=(shape,) * count,
        out_specs=(vm,) * count,
        scratch_shapes=[pltpu.VMEM((size * count, width), BF)],
        cost_estimate=estimate(flops=0, bytes_accessed=8 * size * count * width, transcendentals=0),
        name="matrices",
    )


def layers_kernel(me_ref, *refs, terms, rows):
    parts, (small_ref, *out_refs, total) = refs[:terms], refs[terms:]
    total[...] = sum(ref[...].astype(F32) for ref in parts)
    small_ref[...] = total[rows:, :]
    size = rows // len(out_refs)
    for i, out_ref in enumerate(out_refs):
        place = pl.multiple_of(jnp.bitwise_xor(me_ref[0], i) * size, 8)
        out_ref[:size, :] = total[pl.ds(place, size), :].astype(BF)
        out_ref[size:, :] = total[rows:, :].astype(BF)


def layers(me, parts, rows, count):
    height, width = parts[0].shape
    vm = pl.BlockSpec(memory_space=VM)
    block_shape = jax.ShapeDtypeStruct((rows // count + height - rows, width), BF)
    return kernel_call(
        functools.partial(layers_kernel, terms=len(parts), rows=rows),
        (me, *parts),
        [pl.BlockSpec(memory_space=SMEM)] + [vm] * len(parts),
        out_shape=(jax.ShapeDtypeStruct((height - rows, width), F32),) + (block_shape,) * count,
        out_specs=(vm,) * (1 + count),
        scratch_shapes=[pltpu.VMEM((height, width), F32)],
        cost_estimate=estimate(flops=0, bytes_accessed=4 * len(parts) * height * width, transcendentals=0),
        name="layers",
    )


def spread_kernel(core_ref, me_ref, *refs):
    *block_refs, dwq_ref, dwk_ref, dwv_ref, dwo_ref = refs
    count = len(block_refs) // 2
    size, width = block_refs[0].shape
    third = width // 3
    for i, ref in enumerate(block_refs):
        core = core_ref[0] if i < count else 1 - core_ref[0]
        rows = pl.ds(pl.multiple_of(core * size, 16), size)
        matrix = jnp.bitwise_xor(me_ref[0], i % count)

        @pl.when(matrix == 0)
        def _():
            dwo_ref[rows, :] = ref[...].astype(F32)

        @pl.when(matrix > 0)
        def _():
            columns = pl.ds(pl.multiple_of((matrix - 1) * third, 128), third)
            for j, out_ref in enumerate((dwq_ref, dwk_ref, dwv_ref)):
                out_ref[rows, columns] = ref[:, j * third : (j + 1) * third].astype(F32)


def spread(core, me, own, far):
    width = own[0].shape[1]
    vm = pl.BlockSpec(memory_space=VM)
    return kernel_call(
        spread_kernel,
        (core, me, *own, *far),
        [pl.BlockSpec(memory_space=SMEM)] * 2 + [vm] * (2 * len(own)),
        out_shape=(jax.ShapeDtypeStruct((width, width), F32),) * 4,
        out_specs=(vm,) * 4,
        cost_estimate=estimate(flops=0, bytes_accessed=24 * width * width, transcendentals=0),
        name="spread",
    )


def butterfly(value, axis):
    step = 1
    while step < lax.axis_size(axis):
        value = (value.astype(F32) + swap(value, axis, step).astype(F32)).astype(value.dtype)
        step *= 2
    return value


def hold(value, after):
    return pl.pallas_call(
        lambda *refs: None,
        out_shape=jax.ShapeDtypeStruct(value.shape, value.dtype),
        in_specs=[pl.BlockSpec(memory_space=pl.ANY)] * 2,
        out_specs=pl.BlockSpec(memory_space=pl.ANY),
        input_output_aliases={0: 0},
        name="hold",
    )(value, after)


def shards(
    tokens,
    cotangent,
    ln1_gain,
    ln1_shift,
    w_query,
    w_key,
    w_value,
    w_output,
    ln2_gain,
    ln2_shift,
    w_router,
    w_inner,
    b_inner,
    w_outer,
    b_outer,
    image_count,
    patches,
    picks,
    slots,
):
    rows, width = tokens.shape
    experts = w_router.shape[1]
    groups = lax.axis_size("expert")
    capacity = 21 * rows // (10 * experts)
    half = w_inner.shape[2]
    g1, s1 = ln1_gain[None, :], ln1_shift[None, :]
    g2, s2 = ln2_gain[None, :], ln2_shift[None, :]
    pick_rows, slot_rows = picks.T, slots.T
    start = jnp.zeros((1,), jnp.int32)
    whole_buffer = [(experts * capacity, width)]

    def exchange(rows_out):
        cut = rows_out.reshape(experts, capacity, width)
        cut = lax.all_to_all(cut, "expert", split_axis=0, concat_axis=0, tiled=True)
        return cut.reshape(experts * capacity, width)

    if groups <= 4:
        me = lax.axis_index("expert").astype(jnp.int32)
        base = me.reshape(1)
        buffers = [(capacity, width)] * groups
        parts = [[i] for i in range(groups)]

        def exchange_block(blocks, i):
            return blocks[i] if i == 0 else swap(blocks[i], "expert", i)

        def exchange_pair(pair, i):
            members = [[j, j ^ i] for j in range(groups) if j < j ^ i]
            return lax.all_to_all(
                pair, "expert", split_axis=0, concat_axis=0, tiled=True, axis_index_groups=members
            )

    else:
        me = jnp.zeros((), jnp.int32)
        base, buffers, parts = start, whole_buffer, [[0]]

        def exchange_block(blocks, i):
            return exchange(blocks[0])

    place = (1 - ((me >> 1) & 1)).reshape(1)
    core = lax.axis_index("hidden").astype(jnp.int32).reshape(1)
    column = lax.axis_index("dp").astype(jnp.int32).reshape(1)
    columns = lax.axis_size("dp")
    cot_out = pack(start, pick_rows, slot_rows, cotangent, whole_buffer, capacity)[0]
    cot_in = exchange(cot_out)
    wi_own, wo_own = w_inner[0], w_outer[0]
    wi_far, wo_far = swap(wi_own, "hidden", 1), swap(wo_own, "hidden", 1)
    bi_all = jnp.concatenate([b_inner, swap(b_inner, "hidden", 1)], axis=1)
    n1, q, k, v, p, linv, mixed, res, *outgoing = front(
        base, image_count, patches, tokens, g1, s1, w_query, w_key, w_value, w_output, g2, s2,
        pick_rows, slot_rows, buffers, capacity, [cot_out],
    )
    xs, sums, hids, gps, gouts, out_rows, gin_back = [], [], [], [], [], [], []
    for which in parts:
        i = which[0]
        local = i == 0 and groups <= 4
        if i > 1:
            outgoing[i] = hold(outgoing[i], cot_in if i == 2 else xs[-1])
        x = [exchange_block(outgoing, i)]
        (hid, gp, gout, *small), outs, gins = expert_pass(
            base, cot_out if local else cot_in, x, which, i > 1, wi_own, wi_far, wo_own, wo_far, bi_all, b_outer,
            w_router, "expert", hids[-1:],
        )
        xs.extend(x)
        hids.append(hid)
        gps.append(gp)
        gouts.append(gout)
        sums.append(small)
        out_rows.extend(outs)
        gin_back.append(exchange_pair(gins[0], i) if i > 1 else exchange_block([gins[0]] * groups, i))
    assembled = assemble(base, out_rows, [])
    dwo_far, dwo_own, dwi_far, dwi_own = outer_pass(xs, gouts, hids, gps, half, [assembled])

    gres, gmix, dwout_keep, dwout_send, ggain2, gshift2 = middle_pass(
        base, place, core, image_count, patches, picks, slots, gin_back, cotangent, res, g2, mixed, w_output,
        capacity, [dwi_own],
    )
    bit_x, bit_y = axis_bits("dp")
    bits, bits_after = jnp.stack([bit_x, bit_y]), jnp.stack([bit_y, bit_x])
    dwo_far, dwi_far = swap(dwo_far, "hidden", 1), swap(dwi_far, "hidden", 1)
    half_o, half_i = half // 2, width // 2
    dwo_send, dwi_send = pick_sums(
        [[1 - bit_x] * 2, [1 - bit_y] * 2],
        [([dwo_own, dwo_far], half_o), ([dwi_own, dwi_far], half_i)],
        [gmix],
    )
    dwo_got, dwi_got = swap(dwo_send, "dp", 1), swap(dwi_send, "dp", 2)
    dq, dk, dv, main_keep, main_send = attend_back(core, n1, q, k, v, p, linv, mixed, gmix, [dwo_send])
    gtok, small, small_sent = tokens_pass(
        (dq, dk, dv), (w_query, w_key, w_value), tokens, g1, gres, ggain2, gshift2, list(zip(*sums)), []
    )
    place_o, place_i = 2 * bit_x + 1 - bit_y, 2 * bit_y + 1 - bit_x
    dwo_send, dwi_send = pick_sums(
        [[place_o, place_o, 1 - bit_y], [place_i, place_i, 1 - bit_x]],
        [([dwo_own, dwo_far, dwo_got], half_o // 2), ([dwi_own, dwi_far, dwi_got], half_i // 2)],
        [small],
    )
    dwo_last, dwi_last = swap(dwo_send, "dp", 2), swap(dwi_send, "dp", 1)
    blocks = matrices(
        column,
        dwout_keep,
        swap(dwout_send, "hidden", 1),
        main_keep,
        swap(main_send, "hidden", 1),
        small,
        swap(small_sent, "hidden", 1),
    )
    arrived = [blocks[0]] + [swap(blocks[i], "dp", i) for i in range(1, columns)]
    out_back = exchange(hold(assembled, gin_back[-1]))
    place_o, place_i, zero = 2 * bit_x + bit_y, 2 * bit_y + bit_x, jnp.zeros_like(bit_x)
    dwo_piece, dwi_piece = pick_sums(
        [[place_o, place_o, bit_y, zero], [place_i, place_i, bit_x, zero]],
        [([dwo_own, dwo_far, dwo_got, dwo_last], half_o // 2), ([dwi_own, dwi_far, dwi_got, dwi_last], half_i // 2)],
        [blocks[0]],
    )
    rows_half = width // 2
    if groups <= 4:
        expert_small, *quarters = layers(base, arrived, rows_half, groups)
        piece = narrow_sum(quarters[0], *(swap(quarters[i], "expert", i) for i in range(1, groups)))
        small, piece = piece[rows_half // groups :], piece[: rows_half // groups]
        matrix = assemble(base, [piece] + [swap(piece, "expert", i) for i in range(1, groups)], [])
    else:
        expert_small, piece = layers(start, arrived, rows_half, 1)
        piece = butterfly(piece, "expert")
        small, matrix = piece[rows_half:], piece[:rows_half]
    dwo_half, dwi_half = merge(
        bits_after,
        [(dwo_piece, swap(dwo_piece, "dp", 2)), (dwi_piece, swap(dwi_piece, "dp", 1))],
        BF,
        [expert_small],
    )
    block_out = output_pass(start, image_count, patches, picks, slots, [out_back], res, capacity, [blocks[0]])
    dwo, dwi = merge(
        bits, [(dwo_half, swap(dwo_half, "dp", 1)), (dwi_half, swap(dwi_half, "dp", 2))], F32, [block_out]
    )
    own = [matrix] + [hold(swap(matrix, "dp", i), dwi) for i in range(1, columns)]
    far = [swap(value, "hidden", 1) for value in own]
    dwq, dwk, dwv, dwout = spread(core, column, own, far)
    small = small.astype(F32)
    half_rows = half // width
    offset = half_rows + 1
    return (
        block_out,
        gtok,
        small[offset],
        small[offset + 1],
        dwq,
        dwk,
        dwv,
        dwout,
        small[offset + 2],
        small[offset + 3],
        small[offset + 4 : offset + 4 + experts].T,
        dwi[None],
        expert_small[:half_rows].reshape(1, half),
        dwo[None],
        expert_small[half_rows:offset],
    )


def solution(mesh):
    rows = P(("expert", "hidden", "dp"), None)
    device = P(("expert", "hidden", "dp"))
    inner = P("expert", None, "hidden")
    inner_bias = P("expert", "hidden")
    outer = P("expert", "hidden", None)
    outer_bias = P("expert", None)
    return jax.shard_map(
        shards,
        mesh=mesh,
        in_specs=(rows, rows) + (P(),) * 9 + (inner, inner_bias, outer, outer_bias, device, device, rows, rows),
        out_specs=(rows, rows) + (P(),) * 9 + (inner, inner_bias, outer, outer_bias),
        check_vma=False,
    )
```

```python
import functools

import jax
import jax.numpy as jnp
from jax import lax
from jax.experimental import pallas as pl
from jax.experimental.pallas import tpu as pltpu
from jax.sharding import PartitionSpec as P

HEADS = 12
NORM_EPS = 1e-06
MASKED = -1e30
IMAGES_MAX = 8
BF = jnp.bfloat16
F32 = jnp.float32
VMEM_LIMIT = 63 * 1024 * 1024 + 768 * 1024

VM = pltpu.VMEM
SMEM = pltpu.SMEM


COST = 1.0


def estimate(flops, bytes_accessed, transcendentals):
    return pl.CostEstimate(
        flops=int(COST * flops),
        bytes_accessed=int(COST * bytes_accessed),
        transcendentals=int(COST * transcendentals),
    )


def mm(a, b):
    return lax.dot_general(a, b, (((1,), (0,)), ((), ())), preferred_element_type=F32)


def mm_nt(a, b):
    return lax.dot_general(a, b, (((1,), (1,)), ((), ())), preferred_element_type=F32)


def mm_tn(a, b):
    return lax.dot_general(a, b, (((0,), (0,)), ((), ())), preferred_element_type=F32)


def standardize(values):
    center = jnp.mean(values, axis=-1, keepdims=True)
    centered = values - center
    moment = jnp.mean(centered * centered, axis=-1, keepdims=True)
    inv = lax.rsqrt(moment + NORM_EPS)
    return centered * inv, inv


def norm_back(grad_normed, gain, unit, inv):
    g = grad_normed * gain
    first = jnp.mean(g, axis=-1, keepdims=True)
    second = jnp.mean(g * unit, axis=-1, keepdims=True)
    return (g - first - unit * second) * inv


def targets(picks, slots, capacity, base):
    return jnp.where(slots >= 0, jnp.bitwise_xor(picks, base) * capacity + slots, -1)


def pack_into(out_refs, rows_ref, dest):
    for i, out_ref in enumerate(out_refs):
        total, rows = out_ref.shape[0], rows_ref.shape[0]
        step = pack_step(total)
        for start in range(0, total, step):
            index = lax.broadcasted_iota(jnp.int32, (step, rows), 0) + (start + i * total)
            hit = (index == dest[0:1, :]) | (index == dest[1:2, :])
            out_ref[start : start + step, :] = mm(hit.astype(BF), rows_ref[...]).astype(BF)


def unpack_rows(buffer_refs, dest, place=None):
    values = [ref[...] if len(ref.shape) == 2 else ref[place] for ref in buffer_refs]
    buffer = values[0] if len(values) == 1 else jnp.concatenate(values, axis=0)
    index = lax.broadcasted_iota(jnp.int32, (dest.shape[0], buffer.shape[0]), 1)
    hit = (index == dest[:, 0:1]) | (index == dest[:, 1:2])
    return mm(hit.astype(BF), buffer)


def kernel_call(body, inputs, in_specs, after=(), **options):
    def run(*refs):
        body(*refs[len(after) :])

    specs = [pl.BlockSpec(memory_space=pl.ANY)] * len(after) + list(in_specs)
    return pl.pallas_call(run, in_specs=specs, compiler_params=params(), **options)(*after, *inputs)


def pack_step(total):
    for step in (448, 336, 224, 192, 112, 96, 64, 48, 32, 16):
        if total % step == 0:
            return step
    return total


def params():
    return pltpu.CompilerParams(vmem_limit_bytes=VMEM_LIMIT)


def whole(shape):
    return pl.BlockSpec(shape, lambda *_: (0,) * len(shape))


def pack_kernel(base_ref, pick_ref, slot_ref, rows_ref, *out_refs, capacity):
    pack_into(out_refs, rows_ref, targets(pick_ref[...], slot_ref[...], capacity, base_ref[0]))


def pack(base, pick_rows, slot_rows, rows, buffers, capacity):
    count, width = rows.shape
    total = sum(shape[0] for shape in buffers)
    return kernel_call(
        functools.partial(pack_kernel, capacity=capacity),
        (base, pick_rows, slot_rows, rows),
        [pl.BlockSpec(memory_space=SMEM)] + [pl.BlockSpec(memory_space=VM)] * 3,
        out_shape=tuple(jax.ShapeDtypeStruct(shape, BF) for shape in buffers),
        out_specs=(pl.BlockSpec(memory_space=VM),) * len(buffers),
        cost_estimate=estimate(
            flops=2 * total * count * width, bytes_accessed=4 * total * width, transcendentals=0
        ),
        name="pack_rows",
    )


def classes(count, patch, rows, padding):
    row = lax.broadcasted_iota(jnp.int32, (rows, 1), 0)
    image = jnp.zeros((rows, 1), jnp.int32)
    for i in range(1, IMAGES_MAX):
        image = image + (row >= i * patch).astype(jnp.int32)
    return jnp.where(row < count * patch, image, padding)


def front_kernel(
    base_ref,
    count_ref,
    patch_ref,
    tokens_ref,
    gain1_ref,
    shift1_ref,
    wq_ref,
    wk_ref,
    wv_ref,
    wo_ref,
    gain2_ref,
    shift2_ref,
    pick_ref,
    slot_ref,
    n1_ref,
    q_ref,
    k_ref,
    v_ref,
    p_ref,
    linv_ref,
    mixed_ref,
    res_ref,
    *rest,
    capacity,
    head_dim,
    qb,
):
    *out_refs, n2_ref = rest
    j = pl.program_id(0)
    rows, width = tokens_ref.shape
    cols = wq_ref.shape[1]

    @pl.when(j == 0)
    def _():
        x = tokens_ref[...].astype(F32)
        unit, _ = standardize(x)
        n1_ref[...] = (unit * gain1_ref[...] + shift1_ref[...]).astype(BF)
        res_ref[...] = x

    n1 = n1_ref[...]
    q_ref[...] = mm(n1, wq_ref[...]).astype(BF)
    k_ref[...] = mm(n1, wk_ref[...]).astype(BF)
    v_ref[...] = mm(n1, wv_ref[...]).astype(BF)
    cls = classes(count_ref[0], patch_ref[0], rows, head_dim - 1)
    lane = lax.broadcasted_iota(jnp.int32, (rows, 2 * head_dim), 1)
    inner = lane % head_dim
    apart = jnp.where(inner == cls, 0.0, MASKED).astype(BF)
    member = jnp.where(inner == cls, 1.0, 0.0).astype(BF)
    ones = jnp.ones((rows, 2 * head_dim), BF)
    scale = head_dim ** (-0.5)
    for pair in range(cols // (2 * head_dim)):
        sl = slice(pair * 2 * head_dim, (pair + 1) * 2 * head_dim)
        q_pair = q_ref[:, sl] * jnp.asarray(scale, BF)
        k_pair = k_ref[:, sl]
        v_ext = jnp.concatenate([v_ref[:, sl], ones], axis=1)
        for h in range(2):
            mine = (lane >= h * head_dim) & (lane < (h + 1) * head_dim)
            qm = jnp.where(mine, q_pair, apart)
            km = jnp.where(mine, k_pair, member)
            for b in range(0, rows, qb):
                s = mm_nt(qm[b : b + qb], km)
                top = jnp.max(s, axis=-1, keepdims=True)
                p = jnp.exp(s - top).astype(BF)
                p_ref[pair * 2 + h, b : b + qb, :] = p
                ov = mm(p, v_ext)
                linv = 1.0 / ov[:, 2 * head_dim :]
                o = (ov[:, : 2 * head_dim] * linv).astype(BF)
                if h == 0:
                    mixed_ref[b : b + qb, sl] = o
                    linv_ref[b : b + qb, sl] = linv
                else:
                    keep = mine[b : b + qb]
                    mixed_ref[b : b + qb, sl] = jnp.where(keep, o, mixed_ref[b : b + qb, sl])
                    linv_ref[b : b + qb, sl] = jnp.where(keep, linv, linv_ref[b : b + qb, sl])
    res_ref[...] += mm(mixed_ref[...], wo_ref[...])

    @pl.when(j == pl.num_programs(0) - 1)
    def _():
        unit, _ = standardize(res_ref[...])
        n2_ref[...] = (unit * gain2_ref[...] + shift2_ref[...]).astype(BF)
        pack_into(out_refs, n2_ref, targets(pick_ref[...], slot_ref[...], capacity, base_ref[0]))


def front(base, count, patch, tokens, g1, s1, wq, wk, wv, wo, g2, s2, pick_rows, slot_rows, buffers, capacity, after):
    rows, width = tokens.shape
    head_dim = width // HEADS
    quad = 4 * head_dim
    steps = width // quad
    col = pl.BlockSpec((width, quad), lambda j: (0, j))
    seq = pl.BlockSpec((rows, quad), lambda j: (0, j))
    smem = pl.BlockSpec(memory_space=SMEM)
    total = sum(shape[0] for shape in buffers)
    flops = 2 * rows * width * (4 * width + 2 * rows + total)
    row = jax.ShapeDtypeStruct((rows, width), BF)
    wide = jax.ShapeDtypeStruct((rows, width), F32)
    return kernel_call(
        functools.partial(front_kernel, capacity=capacity, head_dim=head_dim, qb=rows // 5),
        (base, count, patch, tokens, g1, s1, wq, wk, wv, wo, g2, s2, pick_rows, slot_rows),
        [
            smem,
            smem,
            smem,
            whole((rows, width)),
            whole((1, width)),
            whole((1, width)),
            col,
            col,
            col,
            pl.BlockSpec((quad, width), lambda j: (j, 0)),
            whole((1, width)),
            whole((1, width)),
            whole(pick_rows.shape),
            whole(slot_rows.shape),
        ],
        after,
        grid=(steps,),
        out_shape=(row, row, row, row, jax.ShapeDtypeStruct((HEADS, rows, rows), BF), wide, row, wide)
        + tuple(jax.ShapeDtypeStruct(shape, BF) for shape in buffers),
        out_specs=(
            whole((rows, width)),
            seq,
            seq,
            seq,
            pl.BlockSpec((4, rows, rows), lambda j: (j, 0, 0)),
            seq,
            seq,
            whole((rows, width)),
        )
        + tuple(whole(shape) for shape in buffers),
        scratch_shapes=[pltpu.VMEM((rows, width), BF)],
        cost_estimate=estimate(
            flops=flops, bytes_accessed=30 * 1024 * 1024, transcendentals=HEADS * rows * rows
        ),
        name="front",
    )


GELU_A = 0.7978845608028654
GELU_B = 0.044715


def expert_kernel(base_ref, c_ref, *refs, which, axis):
    blocks = len(which)
    x_refs, refs = refs[:blocks], refs[blocks:]
    wi_own_ref, wi_far_ref, wo_own_ref, wo_far_ref, bi_ref, bo_ref, router_ref = refs[:7]
    hid_ref, gp_ref, gout_ref, gbi_ref, gbo_ref, grouter_ref = refs[7:13]
    out_refs, gin_refs = refs[13 : 13 + blocks], refs[13 + blocks : 13 + 2 * blocks]
    acc_out, acc_gin, prob = refs[13 + 2 * blocks :]
    f = pl.program_id(0)
    steps = pl.num_programs(0)
    size, width = x_refs[0].shape
    experts = router_ref.shape[1]
    mine = lax.broadcasted_iota(jnp.int32, (size, experts), 1) == lax.axis_index(axis)

    def cot_rows(i):
        place = jnp.bitwise_xor(base_ref[0], which[i]) * size
        return c_ref[pl.ds(pl.multiple_of(place, 16), size), :].astype(F32)

    @pl.when(f == 0)
    def _():
        total = jnp.zeros((1, width), F32)
        for i in range(blocks):
            sl = slice(i * size, (i + 1) * size)
            logits = mm(x_refs[i][...], router_ref[...])
            powers = jnp.exp(logits - jnp.max(logits, axis=-1, keepdims=True))
            probs = powers / jnp.sum(powers, axis=-1, keepdims=True)
            prob[sl, :] = probs
            chosen = jnp.sum(jnp.where(mine, probs, 0.0), axis=-1, keepdims=True)
            grads = (chosen * cot_rows(i)).astype(BF)
            gout_ref[sl, :] = grads
            total = total + jnp.sum(grads.astype(F32), axis=0, keepdims=True)
        gbo_ref[...] = total
        acc_out[...] = jnp.broadcast_to(bo_ref[...].astype(F32), acc_out.shape)
        acc_gin[...] = jnp.zeros(acc_gin.shape, F32)

    near = f < steps // 2
    wi = jnp.where(near, wi_own_ref[...], wi_far_ref[...])
    wo = jnp.where(near, wo_own_ref[...], wo_far_ref[...])
    bi = bi_ref[...].astype(F32)
    bias_sum = jnp.zeros(gbi_ref.shape, F32)
    step = pack_step(size)
    for i in range(blocks):
        for start in range(0, size, step):
            sl = slice(i * size + start, i * size + start + step)
            v = mm(x_refs[i][start : start + step, :], wi) + bi
            gh = mm_nt(gout_ref[sl, :], wo)
            vv = v * v
            t = jnp.tanh(v * (GELU_A + (GELU_A * GELU_B) * vv))
            half = 0.5 + 0.5 * t
            hid = (v * half).astype(BF)
            slope = half + (half * (1.0 - t)) * (v * (GELU_A + (3.0 * GELU_A * GELU_B) * vv))
            gp = (gh * slope).astype(BF)
            hid_ref[0, sl, :] = hid
            gp_ref[0, sl, :] = gp
            bias_sum = bias_sum + jnp.sum(gp.astype(F32), axis=0, keepdims=True)
            acc_out[sl, :] += mm(hid, wo)
            acc_gin[sl, :] += mm_nt(gp, wi)
    gbi_ref[...] = bias_sum

    @pl.when(f == steps - 1)
    def _():
        router = router_ref[...].astype(F32)
        grouter = jnp.zeros(grouter_ref.shape, F32)
        for i in range(blocks):
            sl = slice(i * size, (i + 1) * size)
            probs = prob[sl, :]
            chosen = jnp.sum(jnp.where(mine, probs, 0.0), axis=-1, keepdims=True)
            eo = acc_out[sl, :].astype(BF).astype(F32)
            out_refs[i][...] = (chosen * eo).astype(BF)
            gc = jnp.sum(eo * cot_rows(i), axis=-1, keepdims=True)
            gl = (gc * chosen) * (jnp.where(mine, 1.0, 0.0) - probs)
            extra = lax.dot_general(
                gl,
                router,
                (((1,), (1,)), ((), ())),
                precision=lax.Precision.HIGHEST,
                preferred_element_type=F32,
            )
            gin = (acc_gin[sl, :] + extra).astype(BF)
            if len(gin_refs[i].shape) == 2:
                gin_refs[i][...] = gin
            else:
                gin_refs[i][0] = gin
                gin_refs[i][1] = gin
            high = gl.astype(BF)
            low = (gl - high.astype(F32)).astype(BF)
            x = x_refs[i][...]
            grouter = grouter + mm_tn(high, x) + mm_tn(low, x)
        grouter_ref[...] = grouter


def expert_pass(base, cot, xs, which, twice, wi_own, wi_far, wo_own, wo_far, bi, bo, router, axis, after):
    size, width = xs[0].shape
    blocks = len(xs)
    total = blocks * size
    half = wi_own.shape[1]
    chunk = 512 if half % 512 == 0 else half
    per = half // chunk
    steps = 2 * per
    experts = router.shape[1]
    near = lambda f: jnp.minimum(f, per - 1)
    far = lambda f: jnp.maximum(f - per, 0)
    act = pl.BlockSpec((1, total, chunk), lambda f: (f, 0, 0))
    piece = (size, width)
    back = (2, size, width) if twice else piece
    results = kernel_call(
        functools.partial(expert_kernel, which=which, axis=axis),
        (base, cot, *xs, wi_own, wi_far, wo_own, wo_far, bi, bo, router),
        [pl.BlockSpec(memory_space=SMEM), whole(cot.shape)]
        + [whole((size, width))] * blocks
        + [
            pl.BlockSpec((width, chunk), lambda f: (0, near(f))),
            pl.BlockSpec((width, chunk), lambda f: (0, far(f))),
            pl.BlockSpec((chunk, width), lambda f: (near(f), 0)),
            pl.BlockSpec((chunk, width), lambda f: (far(f), 0)),
            pl.BlockSpec((1, chunk), lambda f: (0, f)),
            whole((1, width)),
            whole((width, experts)),
        ],
        after,
        grid=(steps,),
        out_shape=(
            jax.ShapeDtypeStruct((steps, total, chunk), BF),
            jax.ShapeDtypeStruct((steps, total, chunk), BF),
            jax.ShapeDtypeStruct((total, width), BF),
            jax.ShapeDtypeStruct((1, 2 * half), F32),
            jax.ShapeDtypeStruct((1, width), F32),
            jax.ShapeDtypeStruct((experts, width), F32),
        )
        + (jax.ShapeDtypeStruct(piece, BF),) * blocks
        + (jax.ShapeDtypeStruct(back, BF),) * blocks,
        out_specs=(
            act,
            act,
            whole((total, width)),
            pl.BlockSpec((1, chunk), lambda f: (0, f)),
            whole((1, width)),
            whole((experts, width)),
        )
        + (whole(piece),) * blocks
        + (whole(back),) * blocks,
        scratch_shapes=[
            pltpu.VMEM((total, width), F32),
            pltpu.VMEM((total, width), F32),
            pltpu.VMEM((total, experts), F32),
        ],
        cost_estimate=estimate(
            flops=16 * total * width * half, bytes_accessed=20 * 1024 * 1024, transcendentals=2 * total * half
        ),
        name="expert_pass",
    )
    return results[:6], results[6 : 6 + blocks], results[6 + blocks :]


def outer_kernel(*refs, counts):
    groups = []
    for count in counts:
        values = [ref[...] if len(ref.shape) == 2 else ref[0] for ref in refs[:count]]
        groups.append(values[0] if count == 1 else jnp.concatenate(values, axis=0))
        refs = refs[count:]
    x, g, hid_far, hid_own, gp_far, gp_own = groups
    wo_far_ref, wo_own_ref, wi_far_ref, wi_own_ref = refs
    wo_far_ref[...] = mm_tn(hid_far, g).astype(BF)
    wo_own_ref[...] = mm_tn(hid_own, g).astype(BF)
    wi_far_ref[...] = mm_tn(x, gp_far).astype(BF)
    wi_own_ref[...] = mm_tn(x, gp_own).astype(BF)


def outer_pass(xs, gouts, hids, gps, half, after=()):
    width = xs[0].shape[1]
    total = sum(x.shape[0] for x in xs)
    chunk = hids[0].shape[2]
    per = half // chunk
    cut = lambda values, first: [
        pl.BlockSpec((1, *value.shape[1:]), lambda f: (f + first * per, 0, 0)) for value in values
    ]
    full = lambda values: [whole(value.shape) for value in values]
    groups = (xs, gouts, hids, hids, gps, gps)
    outer = jax.ShapeDtypeStruct((half, width), BF)
    inner = jax.ShapeDtypeStruct((width, half), BF)
    return kernel_call(
        functools.partial(outer_kernel, counts=tuple(len(group) for group in groups)),
        [value for group in groups for value in group],
        full(xs) + full(gouts) + cut(hids, 1) + cut(hids, 0) + cut(gps, 1) + cut(gps, 0),
        after,
        grid=(per,),
        out_shape=(outer, outer, inner, inner),
        out_specs=(pl.BlockSpec((chunk, width), lambda f: (f, 0)),) * 2
        + (pl.BlockSpec((width, chunk), lambda f: (0, f)),) * 2,
        cost_estimate=estimate(
            flops=8 * total * width * half, bytes_accessed=30 * 1024 * 1024, transcendentals=0
        ),
        name="outer_pass",
    )


def live_rows(count, patch, rows):
    row = lax.broadcasted_iota(jnp.int32, (rows, 1), 0)
    return row < count * patch


def assemble_kernel(base_ref, *refs):
    *block_refs, out_ref = refs
    size = block_refs[0].shape[0]
    for i, block_ref in enumerate(block_refs):
        place = jnp.bitwise_xor(base_ref[0], i) * size
        out_ref[pl.ds(pl.multiple_of(place, 16), size), :] = block_ref[...]


def assemble(base, blocks, after):
    size, width = blocks[0].shape
    return kernel_call(
        assemble_kernel,
        (base, *blocks),
        [pl.BlockSpec(memory_space=SMEM)] + [pl.BlockSpec(memory_space=VM)] * len(blocks),
        after,
        out_shape=jax.ShapeDtypeStruct((len(blocks) * size, width), BF),
        out_specs=pl.BlockSpec(memory_space=VM),
        cost_estimate=estimate(flops=0, bytes_accessed=4 * len(blocks) * size * width, transcendentals=0),
        name="assemble",
    )


def output_kernel(base_ref, count_ref, patch_ref, pick_ref, slot_ref, res_ref, *rest, capacity):
    *back_refs, out_ref = rest
    live = live_rows(count_ref[0], patch_ref[0], res_ref.shape[0])
    mixture = unpack_rows(back_refs, targets(pick_ref[...], slot_ref[...], capacity, base_ref[0]))
    out_ref[...] = jnp.where(live, res_ref[...] + mixture, 0.0).astype(BF)


def output_pass(base, count, patch, picks, slots, back, res, capacity, after):
    rows, width = res.shape
    return kernel_call(
        functools.partial(output_kernel, capacity=capacity),
        (base, count, patch, picks, slots, res, *back),
        [pl.BlockSpec(memory_space=SMEM)] * 3 + [pl.BlockSpec(memory_space=VM)] * (3 + len(back)),
        after,
        out_shape=jax.ShapeDtypeStruct((rows, width), BF),
        out_specs=pl.BlockSpec(memory_space=VM),
        cost_estimate=estimate(
            flops=4 * rows * rows * width, bytes_accessed=6 * 1024 * 1024, transcendentals=0
        ),
        name="output_pass",
    )


def middle_kernel(
    base_ref,
    place_ref,
    core_ref,
    count_ref,
    patch_ref,
    pick_ref,
    slot_ref,
    cot_ref,
    res_ref,
    gain2_ref,
    mixed_ref,
    wo_ref,
    *rest,
    capacity,
):
    *back_refs, gres_ref, gmix_ref, keep_ref, send_ref, ggain_ref, gshift_ref = rest
    live = live_rows(count_ref[0], patch_ref[0], res_ref.shape[0])
    gn = unpack_rows(back_refs, targets(pick_ref[...], slot_ref[...], capacity, base_ref[0]), place_ref[0])
    unit, inv = standardize(res_ref[...])
    ggain_ref[...] = jnp.sum(gn * unit, axis=0, keepdims=True)
    gshift_ref[...] = jnp.sum(gn, axis=0, keepdims=True)
    gout = jnp.where(live, cot_ref[...].astype(F32), 0.0)
    gres = gout + norm_back(gn, gain2_ref[...], unit, inv)
    gres_ref[...] = gres
    branch = gres.astype(BF)
    gmix_ref[...] = mm_nt(branch, wo_ref[...]).astype(BF)
    keep_ref[...] = mm_tn(core_half(mixed_ref, core_ref[0]), branch).astype(BF)
    send_ref[...] = mm_tn(core_half(mixed_ref, 1 - core_ref[0]), branch).astype(BF)


def core_half(ref, core):
    size = ref.shape[1] // 2
    return ref[:, pl.ds(pl.multiple_of(core * size, 128), size)]


def middle_pass(base, place, core, count, patch, picks, slots, back, cot, res, g2, mixed, wo, capacity, after):
    rows, width = res.shape
    vm = pl.BlockSpec(memory_space=VM)
    piece = jax.ShapeDtypeStruct((width // 2, width), BF)
    return kernel_call(
        functools.partial(middle_kernel, capacity=capacity),
        (base, place, core, count, patch, picks, slots, cot, res, g2, mixed, wo, *back),
        [pl.BlockSpec(memory_space=SMEM)] * 5 + [vm] * (7 + len(back)),
        after,
        out_shape=(
            jax.ShapeDtypeStruct((rows, width), F32),
            jax.ShapeDtypeStruct((rows, width), BF),
            piece,
            piece,
            jax.ShapeDtypeStruct((1, width), F32),
            jax.ShapeDtypeStruct((1, width), F32),
        ),
        out_specs=(vm,) * 6,
        cost_estimate=estimate(
            flops=400 * rows * width * (rows + width), bytes_accessed=14 * 1024 * 1024, transcendentals=0
        ),
        name="middle_pass",
    )


def attend_back_kernel(
    core_ref,
    n1_ref,
    q_ref,
    k_ref,
    v_ref,
    p_ref,
    linv_ref,
    mixed_ref,
    gmix_ref,
    dq_ref,
    dk_ref,
    dv_ref,
    keep_ref,
    send_ref,
    ds_ref,
    *,
    head_dim,
    qb,
):
    rows, cols = q_ref.shape
    lane = lax.broadcasted_iota(jnp.int32, (rows, 2 * head_dim), 1)
    scale = jnp.asarray(head_dim ** (-0.5), BF)
    zero = jnp.zeros((rows, 2 * head_dim), BF)
    for pair in range(cols // (2 * head_dim)):
        sl = slice(pair * 2 * head_dim, (pair + 1) * 2 * head_dim)
        q_pair = q_ref[:, sl] * scale
        k_pair = k_ref[:, sl] * scale
        v_pair = v_ref[:, sl]
        do_pair = (gmix_ref[:, sl].astype(F32) * linv_ref[:, sl]).astype(BF)
        inner = do_pair.astype(F32) * mixed_ref[:, sl].astype(F32)
        dq = None
        for h in range(2):
            mine = (lane >= h * head_dim) & (lane < (h + 1) * head_dim)
            dom = jnp.where(mine, do_pair, zero)
            qm = jnp.where(mine, q_pair, zero)
            km = jnp.where(mine, k_pair, zero)
            row_inner = jnp.sum(jnp.where(mine, inner, 0.0), axis=-1, keepdims=True)
            head = pair * 2 + h
            for b in range(0, rows, qb):
                dp = mm_nt(dom[b : b + qb], v_pair)
                p = p_ref[head, b : b + qb, :].astype(F32)
                ds_ref[b : b + qb, :] = (p * (dp - row_inner[b : b + qb])).astype(BF)
            ds = ds_ref[...]
            dq_h = mm(ds, km)
            dk_h = mm_tn(ds, qm)
            dv_h = mm_tn(p_ref[head], dom)
            if h == 0:
                dq, dk, dv = dq_h, dk_h, dv_h
            else:
                dq, dk, dv = dq + dq_h, dk + dk_h, dv + dv_h
        dq_ref[:, sl] = dq.astype(BF)
        dk_ref[:, sl] = dk.astype(BF)
        dv_ref[:, sl] = dv.astype(BF)
    grads = jnp.concatenate([dq_ref[...], dk_ref[...], dv_ref[...]], axis=1)
    keep_ref[...] = mm_tn(core_half(n1_ref, core_ref[0]), grads).astype(BF)
    send_ref[...] = mm_tn(core_half(n1_ref, 1 - core_ref[0]), grads).astype(BF)


def attend_back(core, n1, q, k, v, p, linv, mixed, gmix, after):
    rows, width = n1.shape
    head_dim = width // HEADS
    quad = 4 * head_dim
    steps = width // quad
    seq = pl.BlockSpec((rows, quad), lambda j: (0, j))
    grads = pl.BlockSpec((width // 2, 3 * quad), lambda j: (j, 0))
    return kernel_call(
        functools.partial(attend_back_kernel, head_dim=head_dim, qb=rows // 5),
        (core, n1, q, k, v, p, linv, mixed, gmix),
        [
            pl.BlockSpec(memory_space=SMEM),
            whole((rows, width)),
            seq,
            seq,
            seq,
            pl.BlockSpec((4, rows, rows), lambda j: (j, 0, 0)),
            seq,
            seq,
            seq,
        ],
        after,
        grid=(steps,),
        out_shape=(jax.ShapeDtypeStruct((rows, width), BF),) * 3
        + (jax.ShapeDtypeStruct((steps * (width // 2), 3 * quad), BF),) * 2,
        out_specs=(seq, seq, seq, grads, grads),
        scratch_shapes=[pltpu.VMEM((rows, rows), BF)],
        cost_estimate=estimate(
            flops=2 * rows * width * (3 * width + 4 * rows), bytes_accessed=24 * 1024 * 1024, transcendentals=0
        ),
        name="attend_back",
    )


def tokens_kernel(*refs, parts):
    dq_ref, dk_ref, dv_ref, wq_ref, wk_ref, wv_ref, tokens_ref, gain1_ref, gres_ref, ggain2_ref, gshift2_ref = refs[:11]
    gbi_refs, refs = refs[11 : 11 + parts], refs[11 + parts :]
    gbo_refs, refs = refs[:parts], refs[parts:]
    grouter_refs, (gtok_ref, small_ref, sent_ref) = refs[:parts], refs[parts:]
    gn = mm_nt(dq_ref[...], wq_ref[...]) + mm_nt(dk_ref[...], wk_ref[...]) + mm_nt(dv_ref[...], wv_ref[...])
    unit, inv = standardize(tokens_ref[...].astype(F32))
    gtok_ref[...] = gres_ref[...] + norm_back(gn, gain1_ref[...], unit, inv)
    width = gn.shape[1]
    gbi = sum(ref[...] for ref in gbi_refs)
    rows = gbi.shape[1] // 2 // width
    experts = grouter_refs[0].shape[0]
    for out_ref, first in ((small_ref, 0), (sent_ref, rows)):
        out_ref[...] = jnp.zeros(out_ref.shape, F32)
        for i in range(rows):
            out_ref[i : i + 1, :] = gbi[:, (first + i) * width : (first + i + 1) * width]
        out_ref[rows : rows + 1, :] = sum(ref[...] for ref in gbo_refs)
        out_ref[rows + 1 : rows + 2, :] = jnp.sum(gn * unit, axis=0, keepdims=True)
        out_ref[rows + 2 : rows + 3, :] = jnp.sum(gn, axis=0, keepdims=True)
        out_ref[rows + 3 : rows + 4, :] = ggain2_ref[...]
        out_ref[rows + 4 : rows + 5, :] = gshift2_ref[...]
        out_ref[rows + 5 : rows + 5 + experts, :] = sum(ref[...] for ref in grouter_refs)


def tokens_pass(grads, weights, tokens, g1, gres, ggain2, gshift2, sums, after):
    rows, width = tokens.shape
    vm = pl.BlockSpec(memory_space=VM)
    gbi, gbo, grouter = sums
    height = gbi[0].shape[1] // 2 // width + 5 + grouter[0].shape[0]
    small = jax.ShapeDtypeStruct((height + -height % 16, width), F32)
    inputs = (*grads, *weights, tokens, g1, gres, ggain2, gshift2, *gbi, *gbo, *grouter)
    return kernel_call(
        functools.partial(tokens_kernel, parts=len(gbi)),
        inputs,
        [vm] * len(inputs),
        after,
        out_shape=(jax.ShapeDtypeStruct((rows, width), F32), small, small),
        out_specs=(vm,) * 3,
        cost_estimate=estimate(flops=600 * rows * width * width, bytes_accessed=0, transcendentals=0),
        name="tokens_pass",
    )


def swap(value, axis, bit):
    return lax.ppermute(value, axis, [(i, i ^ bit) for i in range(lax.axis_size(axis))])


def block(value, index, count):
    size = value.shape[0] // count
    return lax.dynamic_slice_in_dim(value, index * size, size, 0)


def narrow_sum(*terms):
    return functools.reduce(jnp.add, [term.astype(F32) for term in terms]).astype(BF)


def axis_bits(axis):
    me = lax.axis_index(axis)
    return [(me >> level) & 1 for level in range(lax.axis_size(axis).bit_length() - 1)]


def prefetch_call(body, scalars, inputs, in_specs, grid, out_specs, after, **options):
    def run(scalar_ref, *refs):
        body(scalar_ref, *refs[len(after) :])

    spec = pltpu.PrefetchScalarGridSpec(
        num_scalar_prefetch=1,
        grid=grid,
        in_specs=[pl.BlockSpec(memory_space=pl.ANY)] * len(after) + list(in_specs),
        out_specs=out_specs,
    )
    return pl.pallas_call(run, grid_spec=spec, compiler_params=params(), **options)(scalars, *after, *inputs)


def pick_kernel(index_ref, *refs, counts):
    outs = refs[sum(counts) :]
    for count, out_ref in zip(counts, outs):
        terms, refs = refs[:count], refs[count:]
        out_ref[...] = sum(ref[...].astype(F32) for ref in terms).astype(BF)


def pick_sums(indices, groups, after):
    flat, in_specs, out_specs, shapes, scalars = [], [], [], [], []
    for group, heights, places in groups_of(groups, indices):
        width = group[0].shape[1]
        for value, place in zip(group, places):
            flat.append(value)
            in_specs.append(pl.BlockSpec((heights, width), lambda i, at, k=len(scalars): (at[k], 0)))
            scalars.append(place)
        out_specs.append(whole((heights, width)))
        shapes.append(jax.ShapeDtypeStruct((heights, width), BF))
    return prefetch_call(
        functools.partial(pick_kernel, counts=tuple(len(group) for group, _ in groups)),
        jnp.stack(scalars),
        flat,
        in_specs,
        (1,),
        tuple(out_specs),
        after,
        out_shape=tuple(shapes),
        cost_estimate=estimate(flops=0, bytes_accessed=2 * sum(v.size for v in flat), transcendentals=0),
        name="pick_sums",
    )


def groups_of(groups, indices):
    return [(group, height, places) for (group, height), places in zip(groups, indices)]


def merge_kernel(bits_ref, *refs):
    outs = refs[len(refs) // 3 * 2 :]
    for i, out_ref in enumerate(outs):
        for ref, bit in ((refs[2 * i], bits_ref[i]), (refs[2 * i + 1], 1 - bits_ref[i])):
            size = ref.shape[0]
            out_ref[pl.ds(pl.multiple_of(bit * size, 16), size), :] = ref[...].astype(out_ref.dtype)


def merge(bits, pairs, dtype, after=()):
    flat = [value for pair in pairs for value in pair]
    vm = pl.BlockSpec(memory_space=VM)
    return kernel_call(
        merge_kernel,
        (bits, *flat),
        [pl.BlockSpec(memory_space=SMEM)] + [vm] * len(flat),
        after,
        out_shape=tuple(jax.ShapeDtypeStruct((2 * mine.shape[0], mine.shape[1]), dtype) for mine, _ in pairs),
        out_specs=(vm,) * len(pairs),
        cost_estimate=estimate(flops=0, bytes_accessed=6 * sum(v.size for v in flat), transcendentals=0),
        name="merge",
    )


def matrices_kernel(me_ref, lead_ref, lead_far_ref, main_ref, main_far_ref, small_ref, small_far_ref, *refs):
    *out_refs, total = refs
    size, tail = lead_ref.shape[0], small_ref.shape[0]
    total[:size, :] = (lead_ref[...].astype(F32) + lead_far_ref[...].astype(F32)).astype(BF)
    total[size:, :] = (main_ref[...].astype(F32) + main_far_ref[...].astype(F32)).astype(BF)
    small = (small_ref[...] + small_far_ref[...]).astype(BF)
    for i, out_ref in enumerate(out_refs):
        place = pl.multiple_of(jnp.bitwise_xor(me_ref[0], i) * size, 16)
        out_ref[:size, :] = total[pl.ds(place, size), :]
        out_ref[size : size + tail, :] = small


def matrices(me, lead, lead_far, main, main_far, small, small_far, after):
    size, width = lead.shape
    count = 1 + main.shape[0] // size
    shape = jax.ShapeDtypeStruct((size + small.shape[0], width), BF)
    vm = pl.BlockSpec(memory_space=VM)
    return kernel_call(
        matrices_kernel,
        (me, lead, lead_far, main, main_far, small, small_far),
        [pl.BlockSpec(memory_space=SMEM)] + [vm] * 6,
        after,
        out_shape=(shape,) * count,
        out_specs=(vm,) * count,
        scratch_shapes=[pltpu.VMEM((size * count, width), BF)],
        cost_estimate=estimate(flops=0, bytes_accessed=0, transcendentals=0),
        name="matrices",
    )


def layers_kernel(*refs, terms, rows, half_rows):
    parts, (gbi_ref, gbo_ref, out_ref, total) = refs[:terms], refs[terms:]
    total[...] = sum(ref[...].astype(F32) for ref in parts)
    width = total.shape[1]
    for i in range(half_rows):
        gbi_ref[:, i * width : (i + 1) * width] = total[rows + i : rows + i + 1, :]
    gbo_ref[...] = total[rows + half_rows : rows + half_rows + 1, :]
    size = rows // out_ref.shape[0]
    for i in range(out_ref.shape[0]):
        out_ref[i, :size, :] = total[i * size : (i + 1) * size, :].astype(BF)
        out_ref[i, size:, :] = total[rows:, :].astype(BF)


def layers(parts, rows, half_rows, count, after):
    height, width = parts[0].shape
    vm = pl.BlockSpec(memory_space=VM)
    block_shape = jax.ShapeDtypeStruct((count, rows // count + height - rows, width), BF)
    return kernel_call(
        functools.partial(layers_kernel, terms=len(parts), rows=rows, half_rows=half_rows),
        parts,
        [vm] * len(parts),
        after,
        out_shape=(jax.ShapeDtypeStruct((1, half_rows * width), F32), jax.ShapeDtypeStruct((1, width), F32))
        + (block_shape,),
        out_specs=(vm,) * 3,
        scratch_shapes=[pltpu.VMEM((height, width), F32)],
        cost_estimate=estimate(flops=0, bytes_accessed=0, transcendentals=0),
        name="layers",
    )


def quarter_kernel(parts_ref, piece_ref, *rest, rows, skip, experts):
    *vector_refs, router_ref = rest
    total = sum(parts_ref[i].astype(F32) for i in range(parts_ref.shape[0]))
    piece_ref[...] = total[:rows].astype(BF)
    for i, ref in enumerate(vector_refs):
        ref[...] = total[rows + skip + i]
    router_ref[...] = total[rows + skip + len(vector_refs) : rows + skip + len(vector_refs) + experts]


def quarter(parts, rows, skip, experts):
    width = parts.shape[2]
    vm = pl.BlockSpec(memory_space=VM)
    return kernel_call(
        functools.partial(quarter_kernel, rows=rows, skip=skip, experts=experts),
        [parts],
        [vm],
        out_shape=(jax.ShapeDtypeStruct((rows, width), BF),)
        + (jax.ShapeDtypeStruct((width,), F32),) * 4
        + (jax.ShapeDtypeStruct((experts, width), F32),),
        out_specs=(vm,) * 6,
        cost_estimate=estimate(flops=0, bytes_accessed=0, transcendentals=0),
        name="quarter",
    )


def spread_kernel(core_ref, me_ref, *refs):
    *block_refs, dwq_ref, dwk_ref, dwv_ref, dwo_ref = refs
    count = len(block_refs) // 2
    size, width = block_refs[0].shape
    third = width // 3
    for i, ref in enumerate(block_refs):
        core = core_ref[0] if i < count else 1 - core_ref[0]
        rows = pl.ds(pl.multiple_of(core * size, 16), size)
        matrix = jnp.bitwise_xor(me_ref[0], i % count)

        @pl.when(matrix == 0)
        def _():
            dwo_ref[rows, :] = ref[...].astype(F32)

        @pl.when(matrix > 0)
        def _():
            columns = pl.ds(pl.multiple_of((matrix - 1) * third, 128), third)
            for j, out_ref in enumerate((dwq_ref, dwk_ref, dwv_ref)):
                out_ref[rows, columns] = ref[:, j * third : (j + 1) * third].astype(F32)


def spread(core, me, own, far):
    width = own[0].shape[1]
    vm = pl.BlockSpec(memory_space=VM)
    return kernel_call(
        spread_kernel,
        (core, me, *own, *far),
        [pl.BlockSpec(memory_space=SMEM)] * 2 + [vm] * (2 * len(own)),
        out_shape=(jax.ShapeDtypeStruct((width, width), F32),) * 4,
        out_specs=(vm,) * 4,
        cost_estimate=estimate(flops=0, bytes_accessed=24 * width * width, transcendentals=0),
        name="spread",
    )


def butterfly(value, axis):
    step = 1
    while step < lax.axis_size(axis):
        value = (value.astype(F32) + swap(value, axis, step).astype(F32)).astype(value.dtype)
        step *= 2
    return value


def hold(value, after):
    return pl.pallas_call(
        lambda *refs: None,
        out_shape=jax.ShapeDtypeStruct(value.shape, value.dtype),
        in_specs=[pl.BlockSpec(memory_space=pl.ANY)] * 2,
        out_specs=pl.BlockSpec(memory_space=pl.ANY),
        input_output_aliases={0: 0},
        name="hold",
    )(value, after)


def shards(
    tokens,
    cotangent,
    ln1_gain,
    ln1_shift,
    w_query,
    w_key,
    w_value,
    w_output,
    ln2_gain,
    ln2_shift,
    w_router,
    w_inner,
    b_inner,
    w_outer,
    b_outer,
    image_count,
    patches,
    picks,
    slots,
):
    rows, width = tokens.shape
    experts = w_router.shape[1]
    groups = lax.axis_size("expert")
    capacity = 21 * rows // (10 * experts)
    half = w_inner.shape[2]
    g1, s1 = ln1_gain[None, :], ln1_shift[None, :]
    g2, s2 = ln2_gain[None, :], ln2_shift[None, :]
    pick_rows, slot_rows = picks.T, slots.T
    start = jnp.zeros((1,), jnp.int32)
    whole_buffer = [(experts * capacity, width)]

    def exchange(rows_out):
        cut = rows_out.reshape(experts, capacity, width)
        cut = lax.all_to_all(cut, "expert", split_axis=0, concat_axis=0, tiled=True)
        return cut.reshape(experts * capacity, width)

    if groups <= 4:
        me = lax.axis_index("expert").astype(jnp.int32)
        base = me.reshape(1)
        buffers = [(capacity, width)] * groups
        parts = [[i] for i in range(groups)]

        def exchange_block(blocks, i):
            return blocks[i] if i == 0 else swap(blocks[i], "expert", i)

        def exchange_pair(pair, i):
            members = [[j, j ^ i] for j in range(groups) if j < j ^ i]
            return lax.all_to_all(
                pair, "expert", split_axis=0, concat_axis=0, tiled=True, axis_index_groups=members
            )

    else:
        me = jnp.zeros((), jnp.int32)
        base, buffers, parts = start, whole_buffer, [[0]]

        def exchange_block(blocks, i):
            return exchange(blocks[0])

    place = (1 - ((me >> 1) & 1)).reshape(1)
    core = lax.axis_index("hidden").astype(jnp.int32).reshape(1)
    column = lax.axis_index("dp").astype(jnp.int32).reshape(1)
    columns = lax.axis_size("dp")
    cot_out = pack(start, pick_rows, slot_rows, cotangent, whole_buffer, capacity)[0]
    cot_in = exchange(cot_out)
    wi_own, wo_own = w_inner[0], w_outer[0]
    wi_far, wo_far = swap(wi_own, "hidden", 1), swap(wo_own, "hidden", 1)
    bi_all = jnp.concatenate([b_inner, swap(b_inner, "hidden", 1)], axis=1)
    n1, q, k, v, p, linv, mixed, res, *outgoing = front(
        base, image_count, patches, tokens, g1, s1, w_query, w_key, w_value, w_output, g2, s2,
        pick_rows, slot_rows, buffers, capacity, [cot_out],
    )
    xs, sums, hids, gps, gouts, out_rows, gin_back = [], [], [], [], [], [], []
    for which in parts:
        i = which[0]
        local = i == 0 and groups <= 4
        if i > 1:
            outgoing[i] = hold(outgoing[i], cot_in if i == 2 else xs[-1])
        x = [exchange_block(outgoing, i)]
        (hid, gp, gout, *small), outs, gins = expert_pass(
            base, cot_out if local else cot_in, x, which, i > 1, wi_own, wi_far, wo_own, wo_far, bi_all, b_outer,
            w_router, "expert", hids[-1:],
        )
        xs.extend(x)
        hids.append(hid)
        gps.append(gp)
        gouts.append(gout)
        sums.append(small)
        out_rows.extend(outs)
        gin_back.append(exchange_pair(gins[0], i) if i > 1 else exchange_block([gins[0]] * groups, i))
    assembled = assemble(base, out_rows, [])
    dwo_far, dwo_own, dwi_far, dwi_own = outer_pass(xs, gouts, hids, gps, half, [assembled])

    gres, gmix, dwout_keep, dwout_send, ggain2, gshift2 = middle_pass(
        base, place, core, image_count, patches, picks, slots, gin_back, cotangent, res, g2, mixed, w_output,
        capacity, [dwi_own],
    )
    bit_x, bit_y = axis_bits("dp")
    bits, bits_after = jnp.stack([bit_x, bit_y]), jnp.stack([bit_y, bit_x])
    dwo_far, dwi_far = swap(dwo_far, "hidden", 1), swap(dwi_far, "hidden", 1)
    half_o, half_i = half // 2, width // 2
    dwo_send, dwi_send = pick_sums(
        [[1 - bit_x] * 2, [1 - bit_y] * 2],
        [([dwo_own, dwo_far], half_o), ([dwi_own, dwi_far], half_i)],
        [gmix],
    )
    dwo_got, dwi_got = swap(dwo_send, "dp", 1), swap(dwi_send, "dp", 2)
    dq, dk, dv, main_keep, main_send = attend_back(core, n1, q, k, v, p, linv, mixed, gmix, [dwo_send])
    place_o, place_i = 2 * bit_x + 1 - bit_y, 2 * bit_y + 1 - bit_x
    dwo_send, dwi_send = pick_sums(
        [[place_o, place_o, 1 - bit_y], [place_i, place_i, 1 - bit_x]],
        [([dwo_own, dwo_far, dwo_got], half_o // 2), ([dwi_own, dwi_far, dwi_got], half_i // 2)],
        [main_send],
    )
    dwo_last, dwi_last = swap(dwo_send, "dp", 2), swap(dwi_send, "dp", 1)
    gtok, small, small_sent = tokens_pass(
        (dq, dk, dv), (w_query, w_key, w_value), tokens, g1, gres, ggain2, gshift2, list(zip(*sums)), [dwo_send]
    )
    place_o, place_i, zero = 2 * bit_x + bit_y, 2 * bit_y + bit_x, jnp.zeros_like(bit_x)
    dwo_piece, dwi_piece = pick_sums(
        [[place_o, place_o, bit_y, zero], [place_i, place_i, bit_x, zero]],
        [([dwo_own, dwo_far, dwo_got, dwo_last], half_o // 2), ([dwi_own, dwi_far, dwi_got, dwi_last], half_i // 2)],
        [small],
    )
    blocks = matrices(
        column,
        dwout_keep,
        swap(dwout_send, "hidden", 1),
        main_keep,
        swap(main_send, "hidden", 1),
        small,
        swap(small_sent, "hidden", 1),
        [dwo_piece],
    )
    arrived = [blocks[0]] + [swap(blocks[i], "dp", i) for i in range(1, columns)]
    out_back = exchange(hold(assembled, gin_back[-1]))
    rows_half = width // 2
    half_rows = half // width
    offset = half_rows + 1
    if groups <= 4:
        gbi, gbo, quarters = layers(arrived, rows_half, half_rows, groups, [out_back])
        parts = lax.all_to_all(quarters, "expert", split_axis=0, concat_axis=0, tiled=True)
        piece, *vectors = quarter(parts, rows_half // groups, offset, experts)
        matrix = assemble(base, [piece] + [swap(piece, "expert", i) for i in range(1, groups)], [])
    else:
        gbi, gbo, piece = layers(arrived, rows_half, half_rows, 1, [out_back])
        matrix, *vectors = quarter(butterfly(piece, "expert"), rows_half, offset, experts)
    dwo_half, dwi_half = merge(
        bits_after,
        [(dwo_piece, swap(dwo_piece, "dp", 2)), (dwi_piece, swap(dwi_piece, "dp", 1))],
        BF,
    )
    block_out = output_pass(start, image_count, patches, picks, slots, [out_back], res, capacity, [blocks[0]])
    dwo, dwi = merge(
        bits, [(dwo_half, swap(dwo_half, "dp", 1)), (dwi_half, swap(dwi_half, "dp", 2))], F32, [block_out]
    )
    own = [matrix] + [hold(swap(matrix, "dp", i), dwi) for i in range(1, columns)]
    far = [swap(value, "hidden", 1) for value in own]
    dwq, dwk, dwv, dwout = spread(core, column, own, far)
    return (
        block_out,
        gtok,
        vectors[0],
        vectors[1],
        dwq,
        dwk,
        dwv,
        dwout,
        vectors[2],
        vectors[3],
        vectors[4].T,
        dwi[None],
        gbi,
        dwo[None],
        gbo,
    )


def solution(mesh):
    rows = P(("expert", "hidden", "dp"), None)
    device = P(("expert", "hidden", "dp"))
    inner = P("expert", None, "hidden")
    inner_bias = P("expert", "hidden")
    outer = P("expert", "hidden", None)
    outer_bias = P("expert", None)
    return jax.shard_map(
        shards,
        mesh=mesh,
        in_specs=(rows, rows) + (P(),) * 9 + (inner, inner_bias, outer, outer_bias, device, device, rows, rows),
        out_specs=(rows, rows) + (P(),) * 9 + (inner, inner_bias, outer, outer_bias),
        check_vma=False,
    )
```

```python
import functools

import jax
import jax.numpy as jnp
from jax import lax
from jax.experimental import pallas as pl
from jax.experimental.pallas import tpu as pltpu
from jax.sharding import PartitionSpec as P

HEADS = 12
NORM_EPS = 1e-06
MASKED = -1e30
IMAGES_MAX = 8
BF = jnp.bfloat16
F32 = jnp.float32
VMEM_LIMIT = 63 * 1024 * 1024 + 768 * 1024

VM = pltpu.VMEM
SMEM = pltpu.SMEM


COST = 1.0


def estimate(flops, bytes_accessed, transcendentals):
    return pl.CostEstimate(
        flops=int(COST * flops),
        bytes_accessed=int(COST * bytes_accessed),
        transcendentals=int(COST * transcendentals),
    )


def mm(a, b):
    return lax.dot_general(a, b, (((1,), (0,)), ((), ())), preferred_element_type=F32)


def mm_nt(a, b):
    return lax.dot_general(a, b, (((1,), (1,)), ((), ())), preferred_element_type=F32)


def mm_tn(a, b):
    return lax.dot_general(a, b, (((0,), (0,)), ((), ())), preferred_element_type=F32)


def standardize(values):
    center = jnp.mean(values, axis=-1, keepdims=True)
    centered = values - center
    moment = jnp.mean(centered * centered, axis=-1, keepdims=True)
    inv = lax.rsqrt(moment + NORM_EPS)
    return centered * inv, inv


def norm_back(grad_normed, gain, unit, inv):
    g = grad_normed * gain
    first = jnp.mean(g, axis=-1, keepdims=True)
    second = jnp.mean(g * unit, axis=-1, keepdims=True)
    return (g - first - unit * second) * inv


def targets(picks, slots, capacity, base):
    return jnp.where(slots >= 0, jnp.bitwise_xor(picks, base) * capacity + slots, -1)


def pack_into(out_refs, rows_ref, dest):
    for i, out_ref in enumerate(out_refs):
        total, rows = out_ref.shape[0], rows_ref.shape[0]
        step = pack_step(total)
        for start in range(0, total, step):
            index = lax.broadcasted_iota(jnp.int32, (step, rows), 0) + (start + i * total)
            hit = (index == dest[0:1, :]) | (index == dest[1:2, :])
            out_ref[start : start + step, :] = mm(hit.astype(BF), rows_ref[...]).astype(BF)


def unpack_rows(buffer_refs, dest, place=None):
    values = [ref[...] if len(ref.shape) == 2 else ref[place] for ref in buffer_refs]
    buffer = values[0] if len(values) == 1 else jnp.concatenate(values, axis=0)
    index = lax.broadcasted_iota(jnp.int32, (dest.shape[0], buffer.shape[0]), 1)
    hit = (index == dest[:, 0:1]) | (index == dest[:, 1:2])
    return mm(hit.astype(BF), buffer)


def kernel_call(body, inputs, in_specs, after=(), **options):
    def run(*refs):
        body(*refs[len(after) :])

    specs = [pl.BlockSpec(memory_space=pl.ANY)] * len(after) + list(in_specs)
    return pl.pallas_call(run, in_specs=specs, compiler_params=params(), **options)(*after, *inputs)


def pack_step(total):
    for step in (448, 336, 224, 192, 112, 96, 64, 48, 32, 16):
        if total % step == 0:
            return step
    return total


def params():
    return pltpu.CompilerParams(vmem_limit_bytes=VMEM_LIMIT)


def whole(shape):
    return pl.BlockSpec(shape, lambda *_: (0,) * len(shape))


def pack_kernel(base_ref, pick_ref, slot_ref, rows_ref, *out_refs, capacity):
    pack_into(out_refs, rows_ref, targets(pick_ref[...], slot_ref[...], capacity, base_ref[0]))


def pack(base, pick_rows, slot_rows, rows, buffers, capacity):
    count, width = rows.shape
    total = sum(shape[0] for shape in buffers)
    return kernel_call(
        functools.partial(pack_kernel, capacity=capacity),
        (base, pick_rows, slot_rows, rows),
        [pl.BlockSpec(memory_space=SMEM)] + [pl.BlockSpec(memory_space=VM)] * 3,
        out_shape=tuple(jax.ShapeDtypeStruct(shape, BF) for shape in buffers),
        out_specs=(pl.BlockSpec(memory_space=VM),) * len(buffers),
        cost_estimate=estimate(
            flops=2 * total * count * width, bytes_accessed=4 * total * width, transcendentals=0
        ),
        name="pack_rows",
    )


def classes(count, patch, rows, padding):
    row = lax.broadcasted_iota(jnp.int32, (rows, 1), 0)
    image = jnp.zeros((rows, 1), jnp.int32)
    for i in range(1, IMAGES_MAX):
        image = image + (row >= i * patch).astype(jnp.int32)
    return jnp.where(row < count * patch, image, padding)


def front_kernel(
    base_ref,
    count_ref,
    patch_ref,
    tokens_ref,
    gain1_ref,
    shift1_ref,
    wq_ref,
    wk_ref,
    wv_ref,
    wo_ref,
    gain2_ref,
    shift2_ref,
    pick_ref,
    slot_ref,
    n1_ref,
    q_ref,
    k_ref,
    v_ref,
    p_ref,
    linv_ref,
    mixed_ref,
    res_ref,
    *rest,
    capacity,
    head_dim,
    qb,
):
    *out_refs, n2_ref = rest
    j = pl.program_id(0)
    rows, width = tokens_ref.shape
    cols = wq_ref.shape[1]

    @pl.when(j == 0)
    def _():
        x = tokens_ref[...].astype(F32)
        unit, _ = standardize(x)
        n1_ref[...] = (unit * gain1_ref[...] + shift1_ref[...]).astype(BF)
        res_ref[...] = x

    n1 = n1_ref[...]
    q_ref[...] = mm(n1, wq_ref[...]).astype(BF)
    k_ref[...] = mm(n1, wk_ref[...]).astype(BF)
    v_ref[...] = mm(n1, wv_ref[...]).astype(BF)
    cls = classes(count_ref[0], patch_ref[0], rows, head_dim - 1)
    lane = lax.broadcasted_iota(jnp.int32, (rows, 2 * head_dim), 1)
    inner = lane % head_dim
    apart = jnp.where(inner == cls, 0.0, MASKED).astype(BF)
    member = jnp.where(inner == cls, 1.0, 0.0).astype(BF)
    ones = jnp.ones((rows, 2 * head_dim), BF)
    scale = head_dim ** (-0.5)
    for pair in range(cols // (2 * head_dim)):
        sl = slice(pair * 2 * head_dim, (pair + 1) * 2 * head_dim)
        q_pair = q_ref[:, sl] * jnp.asarray(scale, BF)
        k_pair = k_ref[:, sl]
        v_ext = jnp.concatenate([v_ref[:, sl], ones], axis=1)
        for h in range(2):
            mine = (lane >= h * head_dim) & (lane < (h + 1) * head_dim)
            qm = jnp.where(mine, q_pair, apart)
            km = jnp.where(mine, k_pair, member)
            for b in range(0, rows, qb):
                s = mm_nt(qm[b : b + qb], km)
                top = jnp.max(s, axis=-1, keepdims=True)
                p = jnp.exp(s - top).astype(BF)
                p_ref[pair * 2 + h, b : b + qb, :] = p
                ov = mm(p, v_ext)
                linv = 1.0 / ov[:, 2 * head_dim :]
                o = (ov[:, : 2 * head_dim] * linv).astype(BF)
                if h == 0:
                    mixed_ref[b : b + qb, sl] = o
                    linv_ref[b : b + qb, sl] = linv
                else:
                    keep = mine[b : b + qb]
                    mixed_ref[b : b + qb, sl] = jnp.where(keep, o, mixed_ref[b : b + qb, sl])
                    linv_ref[b : b + qb, sl] = jnp.where(keep, linv, linv_ref[b : b + qb, sl])
    res_ref[...] += mm(mixed_ref[...], wo_ref[...])

    @pl.when(j == pl.num_programs(0) - 1)
    def _():
        unit, _ = standardize(res_ref[...])
        n2_ref[...] = (unit * gain2_ref[...] + shift2_ref[...]).astype(BF)
        pack_into(out_refs, n2_ref, targets(pick_ref[...], slot_ref[...], capacity, base_ref[0]))


def front(base, count, patch, tokens, g1, s1, wq, wk, wv, wo, g2, s2, pick_rows, slot_rows, buffers, capacity, after):
    rows, width = tokens.shape
    head_dim = width // HEADS
    quad = 4 * head_dim
    steps = width // quad
    col = pl.BlockSpec((width, quad), lambda j: (0, j))
    seq = pl.BlockSpec((rows, quad), lambda j: (0, j))
    smem = pl.BlockSpec(memory_space=SMEM)
    total = sum(shape[0] for shape in buffers)
    flops = 2 * rows * width * (4 * width + 2 * rows + total)
    row = jax.ShapeDtypeStruct((rows, width), BF)
    wide = jax.ShapeDtypeStruct((rows, width), F32)
    return kernel_call(
        functools.partial(front_kernel, capacity=capacity, head_dim=head_dim, qb=rows // 5),
        (base, count, patch, tokens, g1, s1, wq, wk, wv, wo, g2, s2, pick_rows, slot_rows),
        [
            smem,
            smem,
            smem,
            whole((rows, width)),
            whole((1, width)),
            whole((1, width)),
            col,
            col,
            col,
            pl.BlockSpec((quad, width), lambda j: (j, 0)),
            whole((1, width)),
            whole((1, width)),
            whole(pick_rows.shape),
            whole(slot_rows.shape),
        ],
        after,
        grid=(steps,),
        out_shape=(row, row, row, row, jax.ShapeDtypeStruct((HEADS, rows, rows), BF), wide, row, wide)
        + tuple(jax.ShapeDtypeStruct(shape, BF) for shape in buffers),
        out_specs=(
            whole((rows, width)),
            seq,
            seq,
            seq,
            pl.BlockSpec((4, rows, rows), lambda j: (j, 0, 0)),
            seq,
            seq,
            whole((rows, width)),
        )
        + tuple(whole(shape) for shape in buffers),
        scratch_shapes=[pltpu.VMEM((rows, width), BF)],
        cost_estimate=estimate(
            flops=flops, bytes_accessed=30 * 1024 * 1024, transcendentals=HEADS * rows * rows
        ),
        name="front",
    )


GELU_A = 0.7978845608028654
GELU_B = 0.044715


def expert_kernel(base_ref, c_ref, *refs, which, axis):
    blocks = len(which)
    x_refs, refs = refs[:blocks], refs[blocks:]
    wi_own_ref, wi_far_ref, wo_own_ref, wo_far_ref, bi_ref, bo_ref, router_ref = refs[:7]
    hid_ref, gp_ref, gout_ref, gbi_ref, gbo_ref, grouter_ref = refs[7:13]
    out_refs, gin_refs = refs[13 : 13 + blocks], refs[13 + blocks : 13 + 2 * blocks]
    acc_out, acc_gin, prob = refs[13 + 2 * blocks :]
    f = pl.program_id(0)
    steps = pl.num_programs(0)
    size, width = x_refs[0].shape
    experts = router_ref.shape[1]
    mine = lax.broadcasted_iota(jnp.int32, (size, experts), 1) == lax.axis_index(axis)

    def cot_rows(i):
        place = jnp.bitwise_xor(base_ref[0], which[i]) * size
        return c_ref[pl.ds(pl.multiple_of(place, 16), size), :].astype(F32)

    @pl.when(f == 0)
    def _():
        total = jnp.zeros((1, width), F32)
        for i in range(blocks):
            sl = slice(i * size, (i + 1) * size)
            logits = mm(x_refs[i][...], router_ref[...])
            powers = jnp.exp(logits - jnp.max(logits, axis=-1, keepdims=True))
            probs = powers / jnp.sum(powers, axis=-1, keepdims=True)
            prob[sl, :] = probs
            chosen = jnp.sum(jnp.where(mine, probs, 0.0), axis=-1, keepdims=True)
            grads = (chosen * cot_rows(i)).astype(BF)
            gout_ref[sl, :] = grads
            total = total + jnp.sum(grads.astype(F32), axis=0, keepdims=True)
        gbo_ref[...] = total
        acc_out[...] = jnp.broadcast_to(bo_ref[...].astype(F32), acc_out.shape)
        acc_gin[...] = jnp.zeros(acc_gin.shape, F32)

    near = f < steps // 2
    wi = jnp.where(near, wi_own_ref[...], wi_far_ref[...])
    wo = jnp.where(near, wo_own_ref[...], wo_far_ref[...])
    bi = bi_ref[...].astype(F32)
    bias_sum = jnp.zeros(gbi_ref.shape, F32)
    step = pack_step(size)
    for i in range(blocks):
        for start in range(0, size, step):
            sl = slice(i * size + start, i * size + start + step)
            v = mm(x_refs[i][start : start + step, :], wi) + bi
            gh = mm_nt(gout_ref[sl, :], wo)
            vv = v * v
            t = jnp.tanh(v * (GELU_A + (GELU_A * GELU_B) * vv))
            half = 0.5 + 0.5 * t
            hid = (v * half).astype(BF)
            slope = half + (half * (1.0 - t)) * (v * (GELU_A + (3.0 * GELU_A * GELU_B) * vv))
            gp = (gh * slope).astype(BF)
            hid_ref[0, sl, :] = hid
            gp_ref[0, sl, :] = gp
            bias_sum = bias_sum + jnp.sum(gp.astype(F32), axis=0, keepdims=True)
            acc_out[sl, :] += mm(hid, wo)
            acc_gin[sl, :] += mm_nt(gp, wi)
    gbi_ref[...] = bias_sum

    @pl.when(f == steps - 1)
    def _():
        router = router_ref[...].astype(F32)
        grouter = jnp.zeros(grouter_ref.shape, F32)
        for i in range(blocks):
            sl = slice(i * size, (i + 1) * size)
            probs = prob[sl, :]
            chosen = jnp.sum(jnp.where(mine, probs, 0.0), axis=-1, keepdims=True)
            eo = acc_out[sl, :].astype(BF).astype(F32)
            out_refs[i][...] = (chosen * eo).astype(BF)
            gc = jnp.sum(eo * cot_rows(i), axis=-1, keepdims=True)
            gl = (gc * chosen) * (jnp.where(mine, 1.0, 0.0) - probs)
            extra = lax.dot_general(
                gl,
                router,
                (((1,), (1,)), ((), ())),
                precision=lax.Precision.HIGHEST,
                preferred_element_type=F32,
            )
            gin = (acc_gin[sl, :] + extra).astype(BF)
            if len(gin_refs[i].shape) == 2:
                gin_refs[i][...] = gin
            else:
                gin_refs[i][0] = gin
                gin_refs[i][1] = gin
            high = gl.astype(BF)
            low = (gl - high.astype(F32)).astype(BF)
            x = x_refs[i][...]
            grouter = grouter + mm_tn(high, x) + mm_tn(low, x)
        grouter_ref[...] = grouter


def expert_pass(base, cot, xs, which, twice, wi_own, wi_far, wo_own, wo_far, bi, bo, router, axis, after):
    size, width = xs[0].shape
    blocks = len(xs)
    total = blocks * size
    half = wi_own.shape[1]
    chunk = 512 if half % 512 == 0 else half
    per = half // chunk
    steps = 2 * per
    experts = router.shape[1]
    near = lambda f: jnp.minimum(f, per - 1)
    far = lambda f: jnp.maximum(f - per, 0)
    act = pl.BlockSpec((1, total, chunk), lambda f: (f, 0, 0))
    piece = (size, width)
    back = (2, size, width) if twice else piece
    results = kernel_call(
        functools.partial(expert_kernel, which=which, axis=axis),
        (base, cot, *xs, wi_own, wi_far, wo_own, wo_far, bi, bo, router),
        [pl.BlockSpec(memory_space=SMEM), whole(cot.shape)]
        + [whole((size, width))] * blocks
        + [
            pl.BlockSpec((width, chunk), lambda f: (0, near(f))),
            pl.BlockSpec((width, chunk), lambda f: (0, far(f))),
            pl.BlockSpec((chunk, width), lambda f: (near(f), 0)),
            pl.BlockSpec((chunk, width), lambda f: (far(f), 0)),
            pl.BlockSpec((1, chunk), lambda f: (0, f)),
            whole((1, width)),
            whole((width, experts)),
        ],
        after,
        grid=(steps,),
        out_shape=(
            jax.ShapeDtypeStruct((steps, total, chunk), BF),
            jax.ShapeDtypeStruct((steps, total, chunk), BF),
            jax.ShapeDtypeStruct((total, width), BF),
            jax.ShapeDtypeStruct((1, 2 * half), F32),
            jax.ShapeDtypeStruct((1, width), F32),
            jax.ShapeDtypeStruct((experts, width), F32),
        )
        + (jax.ShapeDtypeStruct(piece, BF),) * blocks
        + (jax.ShapeDtypeStruct(back, BF),) * blocks,
        out_specs=(
            act,
            act,
            whole((total, width)),
            pl.BlockSpec((1, chunk), lambda f: (0, f)),
            whole((1, width)),
            whole((experts, width)),
        )
        + (whole(piece),) * blocks
        + (whole(back),) * blocks,
        scratch_shapes=[
            pltpu.VMEM((total, width), F32),
            pltpu.VMEM((total, width), F32),
            pltpu.VMEM((total, experts), F32),
        ],
        cost_estimate=estimate(
            flops=16 * total * width * half, bytes_accessed=20 * 1024 * 1024, transcendentals=2 * total * half
        ),
        name="expert_pass",
    )
    return results[:6], results[6 : 6 + blocks], results[6 + blocks :]


def outer_kernel(*refs, counts):
    groups = []
    for count in counts:
        values = [ref[...] if len(ref.shape) == 2 else ref[0] for ref in refs[:count]]
        groups.append(values[0] if count == 1 else jnp.concatenate(values, axis=0))
        refs = refs[count:]
    x, g, hid_far, hid_own, gp_far, gp_own = groups
    wo_far_ref, wo_own_ref, wi_far_ref, wi_own_ref = refs
    wo_far_ref[...] = mm_tn(hid_far, g).astype(BF)
    wo_own_ref[...] = mm_tn(hid_own, g).astype(BF)
    wi_far_ref[...] = mm_tn(x, gp_far).astype(BF)
    wi_own_ref[...] = mm_tn(x, gp_own).astype(BF)


def outer_pass(xs, gouts, hids, gps, half, after=()):
    width = xs[0].shape[1]
    total = sum(x.shape[0] for x in xs)
    chunk = hids[0].shape[2]
    per = half // chunk
    cut = lambda values, first: [
        pl.BlockSpec((1, *value.shape[1:]), lambda f: (f + first * per, 0, 0)) for value in values
    ]
    full = lambda values: [whole(value.shape) for value in values]
    groups = (xs, gouts, hids, hids, gps, gps)
    outer = jax.ShapeDtypeStruct((half, width), BF)
    inner = jax.ShapeDtypeStruct((width, half), BF)
    return kernel_call(
        functools.partial(outer_kernel, counts=tuple(len(group) for group in groups)),
        [value for group in groups for value in group],
        full(xs) + full(gouts) + cut(hids, 1) + cut(hids, 0) + cut(gps, 1) + cut(gps, 0),
        after,
        grid=(per,),
        out_shape=(outer, outer, inner, inner),
        out_specs=(pl.BlockSpec((chunk, width), lambda f: (f, 0)),) * 2
        + (pl.BlockSpec((width, chunk), lambda f: (0, f)),) * 2,
        cost_estimate=estimate(
            flops=8 * total * width * half, bytes_accessed=30 * 1024 * 1024, transcendentals=0
        ),
        name="outer_pass",
    )


def live_rows(count, patch, rows):
    row = lax.broadcasted_iota(jnp.int32, (rows, 1), 0)
    return row < count * patch


def assemble_kernel(base_ref, *refs):
    *block_refs, out_ref = refs
    size = block_refs[0].shape[0]
    for i, block_ref in enumerate(block_refs):
        place = jnp.bitwise_xor(base_ref[0], i) * size
        out_ref[pl.ds(pl.multiple_of(place, 16), size), :] = block_ref[...]


def assemble(base, blocks, after):
    size, width = blocks[0].shape
    return kernel_call(
        assemble_kernel,
        (base, *blocks),
        [pl.BlockSpec(memory_space=SMEM)] + [pl.BlockSpec(memory_space=VM)] * len(blocks),
        after,
        out_shape=jax.ShapeDtypeStruct((len(blocks) * size, width), BF),
        out_specs=pl.BlockSpec(memory_space=VM),
        cost_estimate=estimate(flops=0, bytes_accessed=4 * len(blocks) * size * width, transcendentals=0),
        name="assemble",
    )


def output_kernel(base_ref, count_ref, patch_ref, pick_ref, slot_ref, res_ref, *rest, capacity):
    *back_refs, out_ref = rest
    live = live_rows(count_ref[0], patch_ref[0], res_ref.shape[0])
    mixture = unpack_rows(back_refs, targets(pick_ref[...], slot_ref[...], capacity, base_ref[0]))
    out_ref[...] = jnp.where(live, res_ref[...] + mixture, 0.0).astype(BF)


def output_pass(base, count, patch, picks, slots, back, res, capacity, after):
    rows, width = res.shape
    return kernel_call(
        functools.partial(output_kernel, capacity=capacity),
        (base, count, patch, picks, slots, res, *back),
        [pl.BlockSpec(memory_space=SMEM)] * 3 + [pl.BlockSpec(memory_space=VM)] * (3 + len(back)),
        after,
        out_shape=jax.ShapeDtypeStruct((rows, width), BF),
        out_specs=pl.BlockSpec(memory_space=VM),
        cost_estimate=estimate(
            flops=4 * rows * rows * width, bytes_accessed=6 * 1024 * 1024, transcendentals=0
        ),
        name="output_pass",
    )


def middle_kernel(
    base_ref,
    place_ref,
    core_ref,
    count_ref,
    patch_ref,
    pick_ref,
    slot_ref,
    cot_ref,
    res_ref,
    gain2_ref,
    mixed_ref,
    wo_ref,
    *rest,
    capacity,
):
    *back_refs, gres_ref, gmix_ref, keep_ref, send_ref, ggain_ref, gshift_ref = rest
    live = live_rows(count_ref[0], patch_ref[0], res_ref.shape[0])
    gn = unpack_rows(back_refs, targets(pick_ref[...], slot_ref[...], capacity, base_ref[0]), place_ref[0])
    unit, inv = standardize(res_ref[...])
    ggain_ref[...] = jnp.sum(gn * unit, axis=0, keepdims=True)
    gshift_ref[...] = jnp.sum(gn, axis=0, keepdims=True)
    gout = jnp.where(live, cot_ref[...].astype(F32), 0.0)
    gres = gout + norm_back(gn, gain2_ref[...], unit, inv)
    gres_ref[...] = gres
    branch = gres.astype(BF)
    gmix_ref[...] = mm_nt(branch, wo_ref[...]).astype(BF)
    keep_ref[...] = mm_tn(core_half(mixed_ref, core_ref[0]), branch).astype(BF)
    send_ref[...] = mm_tn(core_half(mixed_ref, 1 - core_ref[0]), branch).astype(BF)


def core_half(ref, core):
    size = ref.shape[1] // 2
    return ref[:, pl.ds(pl.multiple_of(core * size, 128), size)]


def middle_pass(base, place, core, count, patch, picks, slots, back, cot, res, g2, mixed, wo, capacity, after):
    rows, width = res.shape
    vm = pl.BlockSpec(memory_space=VM)
    piece = jax.ShapeDtypeStruct((width // 2, width), BF)
    return kernel_call(
        functools.partial(middle_kernel, capacity=capacity),
        (base, place, core, count, patch, picks, slots, cot, res, g2, mixed, wo, *back),
        [pl.BlockSpec(memory_space=SMEM)] * 5 + [vm] * (7 + len(back)),
        after,
        out_shape=(
            jax.ShapeDtypeStruct((rows, width), F32),
            jax.ShapeDtypeStruct((rows, width), BF),
            piece,
            piece,
            jax.ShapeDtypeStruct((1, width), F32),
            jax.ShapeDtypeStruct((1, width), F32),
        ),
        out_specs=(vm,) * 6,
        cost_estimate=estimate(
            flops=400 * rows * width * (rows + width), bytes_accessed=14 * 1024 * 1024, transcendentals=0
        ),
        name="middle_pass",
    )


def attend_back_kernel(
    core_ref,
    n1_ref,
    q_ref,
    k_ref,
    v_ref,
    p_ref,
    linv_ref,
    mixed_ref,
    gmix_ref,
    dq_ref,
    dk_ref,
    dv_ref,
    keep_ref,
    send_ref,
    ds_ref,
    *,
    head_dim,
    qb,
):
    rows, cols = q_ref.shape
    lane = lax.broadcasted_iota(jnp.int32, (rows, 2 * head_dim), 1)
    scale = jnp.asarray(head_dim ** (-0.5), BF)
    zero = jnp.zeros((rows, 2 * head_dim), BF)
    for pair in range(cols // (2 * head_dim)):
        sl = slice(pair * 2 * head_dim, (pair + 1) * 2 * head_dim)
        q_pair = q_ref[:, sl] * scale
        k_pair = k_ref[:, sl] * scale
        v_pair = v_ref[:, sl]
        do_pair = (gmix_ref[:, sl].astype(F32) * linv_ref[:, sl]).astype(BF)
        inner = do_pair.astype(F32) * mixed_ref[:, sl].astype(F32)
        dq = None
        for h in range(2):
            mine = (lane >= h * head_dim) & (lane < (h + 1) * head_dim)
            dom = jnp.where(mine, do_pair, zero)
            qm = jnp.where(mine, q_pair, zero)
            km = jnp.where(mine, k_pair, zero)
            row_inner = jnp.sum(jnp.where(mine, inner, 0.0), axis=-1, keepdims=True)
            head = pair * 2 + h
            for b in range(0, rows, qb):
                dp = mm_nt(dom[b : b + qb], v_pair)
                p = p_ref[head, b : b + qb, :].astype(F32)
                ds_ref[b : b + qb, :] = (p * (dp - row_inner[b : b + qb])).astype(BF)
            ds = ds_ref[...]
            dq_h = mm(ds, km)
            dk_h = mm_tn(ds, qm)
            dv_h = mm_tn(p_ref[head], dom)
            if h == 0:
                dq, dk, dv = dq_h, dk_h, dv_h
            else:
                dq, dk, dv = dq + dq_h, dk + dk_h, dv + dv_h
        dq_ref[:, sl] = dq.astype(BF)
        dk_ref[:, sl] = dk.astype(BF)
        dv_ref[:, sl] = dv.astype(BF)
    grads = jnp.concatenate([dq_ref[...], dk_ref[...], dv_ref[...]], axis=1)
    keep_ref[...] = mm_tn(core_half(n1_ref, core_ref[0]), grads).astype(BF)
    send_ref[...] = mm_tn(core_half(n1_ref, 1 - core_ref[0]), grads).astype(BF)


def attend_back(core, n1, q, k, v, p, linv, mixed, gmix, after):
    rows, width = n1.shape
    head_dim = width // HEADS
    quad = 4 * head_dim
    steps = width // quad
    seq = pl.BlockSpec((rows, quad), lambda j: (0, j))
    grads = pl.BlockSpec((width // 2, 3 * quad), lambda j: (j, 0))
    return kernel_call(
        functools.partial(attend_back_kernel, head_dim=head_dim, qb=rows // 5),
        (core, n1, q, k, v, p, linv, mixed, gmix),
        [
            pl.BlockSpec(memory_space=SMEM),
            whole((rows, width)),
            seq,
            seq,
            seq,
            pl.BlockSpec((4, rows, rows), lambda j: (j, 0, 0)),
            seq,
            seq,
            seq,
        ],
        after,
        grid=(steps,),
        out_shape=(jax.ShapeDtypeStruct((rows, width), BF),) * 3
        + (jax.ShapeDtypeStruct((steps * (width // 2), 3 * quad), BF),) * 2,
        out_specs=(seq, seq, seq, grads, grads),
        scratch_shapes=[pltpu.VMEM((rows, rows), BF)],
        cost_estimate=estimate(
            flops=2 * rows * width * (3 * width + 4 * rows), bytes_accessed=24 * 1024 * 1024, transcendentals=0
        ),
        name="attend_back",
    )


def tokens_kernel(*refs, parts):
    core_ref, dq_ref, dk_ref, dv_ref, wq_ref, wk_ref, wv_ref, tokens_ref, gain1_ref, gres_ref = refs[:10]
    ggain2_ref, gshift2_ref = refs[10:12]
    gbi_refs, refs = refs[12 : 12 + parts], refs[12 + parts :]
    gbo_refs, refs = refs[:parts], refs[parts:]
    grouter_refs, (gtok_ref, small_ref) = refs[:parts], refs[parts:]
    gn = mm_nt(dq_ref[...], wq_ref[...]) + mm_nt(dk_ref[...], wk_ref[...]) + mm_nt(dv_ref[...], wv_ref[...])
    unit, inv = standardize(tokens_ref[...].astype(F32))
    gtok_ref[...] = gres_ref[...] + norm_back(gn, gain1_ref[...], unit, inv)
    width = gn.shape[1]
    gbi = sum(ref[...] for ref in gbi_refs)
    rows = gbi.shape[1] // 2 // width
    experts = grouter_refs[0].shape[0]
    zeros = jnp.zeros((small_ref.shape[1] - rows - 5 - experts, width), F32)
    common = [
        sum(ref[...] for ref in gbo_refs),
        jnp.sum(gn * unit, axis=0, keepdims=True),
        jnp.sum(gn, axis=0, keepdims=True),
        ggain2_ref[...],
        gshift2_ref[...],
        sum(ref[...] for ref in grouter_refs),
    ]
    columns = small_ref.shape[0] // 2
    for core in range(2):
        mine = core_ref[0] == core
        for column in range(columns):
            at = core * columns + column
            for i in range(rows):
                own, far = (gbi[:, (first + i) * width : (first + i + 1) * width] for first in (0, rows))
                small_ref[at, i : i + 1, :] = jnp.where(mine, own, far)
            place = rows
            for value in common:
                small_ref[at, place : place + value.shape[0], :] = value
                place += value.shape[0]
            if zeros.shape[0]:
                small_ref[at, place:, :] = zeros


def tokens_pass(core, columns, grads, weights, tokens, g1, gres, ggain2, gshift2, sums, after):
    rows, width = tokens.shape
    vm = pl.BlockSpec(memory_space=VM)
    gbi, gbo, grouter = sums
    height = gbi[0].shape[1] // 2 // width + 5 + grouter[0].shape[0]
    inputs = (*grads, *weights, tokens, g1, gres, ggain2, gshift2, *gbi, *gbo, *grouter)
    return kernel_call(
        functools.partial(tokens_kernel, parts=len(gbi)),
        (core, *inputs),
        [pl.BlockSpec(memory_space=SMEM)] + [vm] * len(inputs),
        after,
        out_shape=(
            jax.ShapeDtypeStruct((rows, width), F32),
            jax.ShapeDtypeStruct((2 * columns, height + -height % 16, width), F32),
        ),
        out_specs=(vm,) * 2,
        cost_estimate=estimate(flops=600 * rows * width * width, bytes_accessed=0, transcendentals=0),
        name="tokens_pass",
    )


def swap(value, axis, bit):
    return lax.ppermute(value, axis, [(i, i ^ bit) for i in range(lax.axis_size(axis))])


def block(value, index, count):
    size = value.shape[0] // count
    return lax.dynamic_slice_in_dim(value, index * size, size, 0)


def narrow_sum(*terms):
    return functools.reduce(jnp.add, [term.astype(F32) for term in terms]).astype(BF)


def axis_bits(axis):
    me = lax.axis_index(axis)
    return [(me >> level) & 1 for level in range(lax.axis_size(axis).bit_length() - 1)]


def prefetch_call(body, scalars, inputs, in_specs, grid, out_specs, after, **options):
    def run(scalar_ref, *refs):
        body(scalar_ref, *refs[len(after) :])

    spec = pltpu.PrefetchScalarGridSpec(
        num_scalar_prefetch=1,
        grid=grid,
        in_specs=[pl.BlockSpec(memory_space=pl.ANY)] * len(after) + list(in_specs),
        out_specs=out_specs,
    )
    return pl.pallas_call(run, grid_spec=spec, compiler_params=params(), **options)(scalars, *after, *inputs)


def pick_kernel(index_ref, *refs, counts):
    outs = refs[sum(counts) :]
    for count, out_ref in zip(counts, outs):
        terms, refs = refs[:count], refs[count:]
        out_ref[...] = sum(ref[...].astype(F32) for ref in terms).astype(BF)


def pick_sums(indices, groups, after, cost=0):
    flat, in_specs, out_specs, shapes, scalars = [], [], [], [], []
    for group, heights, places in groups_of(groups, indices):
        width = group[0].shape[1]
        for value, place in zip(group, places):
            flat.append(value)
            in_specs.append(pl.BlockSpec((heights, width), lambda i, at, k=len(scalars): (at[k], 0)))
            scalars.append(place)
        out_specs.append(whole((heights, width)))
        shapes.append(jax.ShapeDtypeStruct((heights, width), BF))
    return prefetch_call(
        functools.partial(pick_kernel, counts=tuple(len(group) for group, _ in groups)),
        jnp.stack(scalars),
        flat,
        in_specs,
        (1,),
        tuple(out_specs),
        after,
        out_shape=tuple(shapes),
        cost_estimate=estimate(flops=cost, bytes_accessed=2 * sum(v.size for v in flat), transcendentals=0),
        name="pick_sums",
    )


def groups_of(groups, indices):
    return [(group, height, places) for (group, height), places in zip(groups, indices)]


def merge_kernel(bits_ref, *refs):
    outs = refs[len(refs) // 3 * 2 :]
    for i, out_ref in enumerate(outs):
        for ref, bit in ((refs[2 * i], bits_ref[i]), (refs[2 * i + 1], 1 - bits_ref[i])):
            size = ref.shape[0]
            out_ref[pl.ds(pl.multiple_of(bit * size, 16), size), :] = ref[...].astype(out_ref.dtype)


def merge(bits, pairs, dtype, after=()):
    flat = [value for pair in pairs for value in pair]
    vm = pl.BlockSpec(memory_space=VM)
    return kernel_call(
        merge_kernel,
        (bits, *flat),
        [pl.BlockSpec(memory_space=SMEM)] + [vm] * len(flat),
        after,
        out_shape=tuple(jax.ShapeDtypeStruct((2 * mine.shape[0], mine.shape[1]), dtype) for mine, _ in pairs),
        out_specs=(vm,) * len(pairs),
        cost_estimate=estimate(flops=0, bytes_accessed=6 * sum(v.size for v in flat), transcendentals=0),
        name="merge",
    )


def matrices_kernel(me_ref, lead_ref, lead_far_ref, main_ref, main_far_ref, *out_refs):
    size = lead_ref.shape[0]
    for i, out_ref in enumerate(out_refs):
        matrix = jnp.bitwise_xor(me_ref[0], i)

        @pl.when(matrix == 0)
        def _():
            out_ref[...] = (lead_ref[...].astype(F32) + lead_far_ref[...].astype(F32)).astype(BF)

        @pl.when(matrix > 0)
        def _():
            place = pl.ds(pl.multiple_of((matrix - 1) * size, 16), size)
            out_ref[...] = (main_ref[place, :].astype(F32) + main_far_ref[place, :].astype(F32)).astype(BF)


def matrices(me, lead, lead_far, main, main_far, after):
    size, width = lead.shape
    count = 1 + main.shape[0] // size
    shape = jax.ShapeDtypeStruct((size, width), BF)
    vm = pl.BlockSpec(memory_space=VM)
    return kernel_call(
        matrices_kernel,
        (me, lead, lead_far, main, main_far),
        [pl.BlockSpec(memory_space=SMEM)] + [vm] * 4,
        after,
        out_shape=(shape,) * count,
        out_specs=(vm,) * count,
        cost_estimate=estimate(flops=0, bytes_accessed=0, transcendentals=0),
        name="matrices",
    )


def layers_kernel(*refs):
    *part_refs, out_ref = refs
    size = out_ref.shape[1]
    for i in range(out_ref.shape[0]):
        rows = slice(i * size, (i + 1) * size)
        out_ref[i] = sum(ref[rows, :].astype(F32) for ref in part_refs).astype(BF)


def layers(parts, count):
    height, width = parts[0].shape
    vm = pl.BlockSpec(memory_space=VM)
    return kernel_call(
        layers_kernel,
        parts,
        [vm] * len(parts),
        out_shape=jax.ShapeDtypeStruct((count, height // count, width), BF),
        out_specs=vm,
        cost_estimate=estimate(flops=0, bytes_accessed=0, transcendentals=0),
        name="layers",
    )


def quarter_kernel(small_ref, parts_ref, gbi_ref, gbo_ref, out_ref, *, half_rows):
    small = sum(small_ref[i] for i in range(small_ref.shape[0]))
    width = small.shape[1]
    for i in range(half_rows):
        gbi_ref[:, i * width : (i + 1) * width] = small[i : i + 1, :]
    gbo_ref[...] = small[half_rows : half_rows + 1, :]
    rows = parts_ref.shape[1]
    out_ref[:rows, :] = sum(parts_ref[i].astype(F32) for i in range(parts_ref.shape[0])).astype(BF)
    out_ref[rows:, :] = small.astype(BF)


def quarter(small, parts, half_rows):
    _, rows, width = parts.shape
    vm = pl.BlockSpec(memory_space=VM)
    return kernel_call(
        functools.partial(quarter_kernel, half_rows=half_rows),
        [small, parts],
        [vm] * 2,
        out_shape=(
            jax.ShapeDtypeStruct((1, half_rows * width), F32),
            jax.ShapeDtypeStruct((1, width), F32),
            jax.ShapeDtypeStruct((rows + small.shape[1], width), BF),
        ),
        out_specs=(vm,) * 3,
        cost_estimate=estimate(flops=0, bytes_accessed=0, transcendentals=0),
        name="quarter",
    )


def whole_kernel(base_ref, *refs, blocks, rows, skip, experts):
    block_refs, (matrix_ref, *vector_refs, router_ref) = refs[:blocks], refs[blocks:]
    for i, ref in enumerate(block_refs):
        place = jnp.bitwise_xor(base_ref[0], i) * rows
        matrix_ref[pl.ds(pl.multiple_of(place, 16), rows), :] = ref[:rows, :]
    total = sum(ref[rows:, :].astype(F32) for ref in block_refs)
    for i, ref in enumerate(vector_refs):
        ref[...] = total[skip + i]
    first = skip + len(vector_refs)
    router_ref[...] = total[first : first + experts]


def whole_matrix(base, blocks, rows, skip, experts):
    width = blocks[0].shape[1]
    vm = pl.BlockSpec(memory_space=VM)
    return kernel_call(
        functools.partial(whole_kernel, blocks=len(blocks), rows=rows, skip=skip, experts=experts),
        (base, *blocks),
        [pl.BlockSpec(memory_space=SMEM)] + [vm] * len(blocks),
        out_shape=(jax.ShapeDtypeStruct((len(blocks) * rows, width), BF),)
        + (jax.ShapeDtypeStruct((width,), F32),) * 4
        + (jax.ShapeDtypeStruct((experts, width), F32),),
        out_specs=(vm,) * 6,
        cost_estimate=estimate(flops=0, bytes_accessed=4 * width * width, transcendentals=0),
        name="whole_matrix",
    )


def spread_kernel(core_ref, me_ref, *refs, places, blocks, earlier):
    block_refs, refs = refs[:blocks], refs[blocks + earlier :]
    dwq_ref, dwk_ref, dwv_ref, dwo_ref, wide, sems = refs
    width = dwo_ref.shape[1]
    third = width // 3
    copies = []
    for slot, (matrix, parts) in enumerate(places):
        for index, first, own in parts:
            ref = block_refs[index]
            core = core_ref[0] if own else 1 - core_ref[0]
            rows = pl.ds(pl.multiple_of(core * (width // 2) + first, 16), ref.shape[0])
            wide[slot, rows, :] = ref[...].astype(F32)
        matrix = jnp.bitwise_xor(me_ref[0], matrix)
        lead = pltpu.make_async_copy(wide.at[slot], dwo_ref, sems.at[slot, 0])
        columns = pl.ds(pl.multiple_of(jnp.maximum(matrix - 1, 0) * third, 128), third)
        rest = [
            pltpu.make_async_copy(
                wide.at[slot, :, i * third : (i + 1) * third], out_ref.at[:, columns], sems.at[slot, i]
            )
            for i, out_ref in enumerate((dwq_ref, dwk_ref, dwv_ref))
        ]
        copies.append((matrix, lead, rest))

        @pl.when(matrix == 0)
        def _():
            lead.start()

        @pl.when(matrix > 0)
        def _():
            for copy in rest:
                copy.start()

    for matrix, lead, rest in copies:

        @pl.when(matrix == 0)
        def _():
            lead.wait()

        @pl.when(matrix > 0)
        def _():
            for copy in rest:
                copy.wait()


def spread(core, me, groups, earlier=()):
    flat, places = [], []
    for matrix, parts in groups:
        places.append((matrix, [(len(flat) + i, first, own) for i, (_, first, own) in enumerate(parts)]))
        flat += [value for value, _, _ in parts]
    width = flat[0].shape[1]
    vm, anywhere = pl.BlockSpec(memory_space=VM), pl.BlockSpec(memory_space=pl.ANY)
    return kernel_call(
        functools.partial(spread_kernel, places=places, blocks=len(flat), earlier=len(earlier)),
        (core, me, *flat, *earlier),
        [pl.BlockSpec(memory_space=SMEM)] * 2 + [vm] * len(flat) + [anywhere] * len(earlier),
        out_shape=(jax.ShapeDtypeStruct((width, width), F32),) * 4,
        out_specs=(anywhere,) * 4,
        scratch_shapes=[pltpu.VMEM((len(groups), width, width), F32), pltpu.SemaphoreType.DMA((len(groups), 3))],
        input_output_aliases={2 + len(flat) + i: i for i in range(len(earlier))},
        cost_estimate=estimate(flops=0, bytes_accessed=0, transcendentals=0),
        name="spread",
    )


def butterfly(value, axis):
    step = 1
    while step < lax.axis_size(axis):
        value = (value.astype(F32) + swap(value, axis, step).astype(F32)).astype(value.dtype)
        step *= 2
    return value


def hold(value, after):
    return pl.pallas_call(
        lambda *refs: None,
        out_shape=jax.ShapeDtypeStruct(value.shape, value.dtype),
        in_specs=[pl.BlockSpec(memory_space=pl.ANY)] * 2,
        out_specs=pl.BlockSpec(memory_space=pl.ANY),
        input_output_aliases={0: 0},
        name="hold",
    )(value, after)


def shards(
    tokens,
    cotangent,
    ln1_gain,
    ln1_shift,
    w_query,
    w_key,
    w_value,
    w_output,
    ln2_gain,
    ln2_shift,
    w_router,
    w_inner,
    b_inner,
    w_outer,
    b_outer,
    image_count,
    patches,
    picks,
    slots,
):
    rows, width = tokens.shape
    experts = w_router.shape[1]
    groups = lax.axis_size("expert")
    capacity = 21 * rows // (10 * experts)
    half = w_inner.shape[2]
    g1, s1 = ln1_gain[None, :], ln1_shift[None, :]
    g2, s2 = ln2_gain[None, :], ln2_shift[None, :]
    pick_rows, slot_rows = picks.T, slots.T
    start = jnp.zeros((1,), jnp.int32)
    whole_buffer = [(experts * capacity, width)]

    def exchange(rows_out):
        cut = rows_out.reshape(experts, capacity, width)
        cut = lax.all_to_all(cut, "expert", split_axis=0, concat_axis=0, tiled=True)
        return cut.reshape(experts * capacity, width)

    if groups <= 4:
        me = lax.axis_index("expert").astype(jnp.int32)
        base = me.reshape(1)
        buffers = [(capacity, width)] * groups
        parts = [[i] for i in range(groups)]

        def exchange_block(blocks, i):
            return blocks[i] if i == 0 else swap(blocks[i], "expert", i)

        def exchange_pair(pair, i):
            members = [[j, j ^ i] for j in range(groups) if j < j ^ i]
            return lax.all_to_all(
                pair, "expert", split_axis=0, concat_axis=0, tiled=True, axis_index_groups=members
            )

    else:
        me = jnp.zeros((), jnp.int32)
        base, buffers, parts = start, whole_buffer, [[0]]

        def exchange_block(blocks, i):
            return exchange(blocks[0])

    place = (1 - ((me >> 1) & 1)).reshape(1)
    core = lax.axis_index("hidden").astype(jnp.int32).reshape(1)
    column = lax.axis_index("dp").astype(jnp.int32).reshape(1)
    columns = lax.axis_size("dp")
    cot_out = pack(start, pick_rows, slot_rows, cotangent, whole_buffer, capacity)[0]
    cot_in = exchange(cot_out)
    wi_own, wo_own = w_inner[0], w_outer[0]
    wi_far, wo_far = swap(wi_own, "hidden", 1), swap(wo_own, "hidden", 1)
    bi_all = jnp.concatenate([b_inner, swap(b_inner, "hidden", 1)], axis=1)
    n1, q, k, v, p, linv, mixed, res, *outgoing = front(
        base, image_count, patches, tokens, g1, s1, w_query, w_key, w_value, w_output, g2, s2,
        pick_rows, slot_rows, buffers, capacity, [cot_out],
    )
    xs, sums, hids, gps, gouts, out_rows, gin_back = [], [], [], [], [], [], []
    for which in parts:
        i = which[0]
        local = i == 0 and groups <= 4
        if i > 1:
            outgoing[i] = hold(outgoing[i], cot_in if i == 2 else xs[-1])
        x = [exchange_block(outgoing, i)]
        (hid, gp, gout, *small), outs, gins = expert_pass(
            base, cot_out if local else cot_in, x, which, i > 1, wi_own, wi_far, wo_own, wo_far, bi_all, b_outer,
            w_router, "expert", hids[-1:],
        )
        xs.extend(x)
        hids.append(hid)
        gps.append(gp)
        gouts.append(gout)
        sums.append(small)
        out_rows.extend(outs)
        gin_back.append(exchange_pair(gins[0], i) if i > 1 else exchange_block([gins[0]] * groups, i))
    assembled = assemble(base, out_rows, [])
    dwo_far, dwo_own, dwi_far, dwi_own = outer_pass(xs, gouts, hids, gps, half, [assembled])

    gres, gmix, dwout_keep, dwout_send, ggain2, gshift2 = middle_pass(
        base, place, core, image_count, patches, picks, slots, gin_back, cotangent, res, g2, mixed, w_output,
        capacity, [dwi_own],
    )
    bit_x, bit_y = axis_bits("dp")
    bits, bits_after = jnp.stack([bit_x, bit_y]), jnp.stack([bit_y, bit_x])
    dwo_far, dwi_far = swap(dwo_far, "hidden", 1), swap(dwi_far, "hidden", 1)
    half_o, half_i = half // 2, width // 2
    dwo_send, dwi_send = pick_sums(
        [[1 - bit_x] * 2, [1 - bit_y] * 2],
        [([dwo_own, dwo_far], half_o), ([dwi_own, dwi_far], half_i)],
        [gmix],
    )
    dwo_got, dwi_got = swap(dwo_send, "dp", 1), swap(dwi_send, "dp", 2)
    dq, dk, dv, main_keep, main_send = attend_back(core, n1, q, k, v, p, linv, mixed, gmix, [dwo_send])
    place_o, place_i = 2 * bit_x + 1 - bit_y, 2 * bit_y + 1 - bit_x
    dwo_send, dwi_send = pick_sums(
        [[place_o, place_o, 1 - bit_y], [place_i, place_i, 1 - bit_x]],
        [([dwo_own, dwo_far, dwo_got], half_o // 2), ([dwi_own, dwi_far, dwi_got], half_i // 2)],
        [main_send],
        10**11,
    )
    dwo_last, dwi_last = swap(dwo_send, "dp", 2), swap(dwi_send, "dp", 1)
    blocks = matrices(
        column, dwout_keep, swap(dwout_send, "hidden", 1), main_keep, swap(main_send, "hidden", 1), [dwo_send]
    )
    arrived = [blocks[0]] + [swap(blocks[i], "dp", i) for i in range(1, columns)]
    gtok, small = tokens_pass(
        core, columns, (dq, dk, dv), (w_query, w_key, w_value), tokens, g1, gres, ggain2, gshift2, list(zip(*sums)),
        [blocks[0]],
    )
    out_back = exchange(hold(assembled, gin_back[-1]))
    small = lax.all_to_all(hold(small, out_back), ("hidden", "dp"), split_axis=0, concat_axis=0, tiled=True)
    place_o, place_i, zero = 2 * bit_x + bit_y, 2 * bit_y + bit_x, jnp.zeros_like(bit_x)
    dwo_piece, dwi_piece = pick_sums(
        [[place_o, place_o, bit_y, zero], [place_i, place_i, bit_x, zero]],
        [([dwo_own, dwo_far, dwo_got, dwo_last], half_o // 2), ([dwi_own, dwi_far, dwi_got, dwi_last], half_i // 2)],
        [gtok],
    )
    rows_half = width // 2
    half_rows = half // width
    offset = half_rows + 1
    if groups <= 4:
        parts = layers(arrived, groups)
        parts = lax.all_to_all(parts, "expert", split_axis=0, concat_axis=0, tiled=True)
        gbi, gbo, piece = quarter(small, parts, half_rows)
        pieces = [piece] + [swap(piece, "expert", i) for i in range(1, groups)]
        matrix, *vectors = whole_matrix(base, pieces, rows_half // groups, offset, experts)
    else:
        gbi, gbo, piece = quarter(small, layers(arrived, 1), half_rows)
        matrix, *vectors = whole_matrix(start, [butterfly(piece, "expert")], rows_half, offset, experts)
    dwo_half, dwi_half = merge(
        bits_after,
        [(dwo_piece, swap(dwo_piece, "dp", 2)), (dwi_piece, swap(dwi_piece, "dp", 1))],
        BF,
    )
    block_out = output_pass(start, image_count, patches, picks, slots, [out_back], res, capacity, [blocks[0]])
    dwo, dwi = merge(
        bits, [(dwo_half, swap(dwo_half, "dp", 1)), (dwi_half, swap(dwi_half, "dp", 2))], F32, [block_out]
    )
    across = columns - 1
    cut = rows_half // 2
    near = [swap(matrix, "dp", 1), swap(matrix, "dp", 2)]
    corner = [swap(near[0][:cut], "dp", 2), swap(near[1][cut:], "dp", 1)]
    near = [hold(value, dwi) for value in near]
    early = [
        (i, [(value, 0, True), (swap(value, "hidden", 1), 0, False)]) for i, value in enumerate([matrix, *near])
    ]
    grads = spread(core, column, early)
    corner = [hold(value, grads[0]) for value in corner]
    late = [(corner[0], 0, True), (corner[1], cut, True)]
    late += [(swap(value, "hidden", 1), first, False) for value, first, _ in late]
    dwq, dwk, dwv, dwout = spread(core, column, [(across, late)], grads)
    return (
        block_out,
        gtok,
        vectors[0],
        vectors[1],
        dwq,
        dwk,
        dwv,
        dwout,
        vectors[2],
        vectors[3],
        vectors[4].T,
        dwi[None],
        gbi,
        dwo[None],
        gbo,
    )


def solution(mesh):
    rows = P(("expert", "hidden", "dp"), None)
    device = P(("expert", "hidden", "dp"))
    inner = P("expert", None, "hidden")
    inner_bias = P("expert", "hidden")
    outer = P("expert", "hidden", None)
    outer_bias = P("expert", None)
    return jax.shard_map(
        shards,
        mesh=mesh,
        in_specs=(rows, rows) + (P(),) * 9 + (inner, inner_bias, outer, outer_bias, device, device, rows, rows),
        out_specs=(rows, rows) + (P(),) * 9 + (inner, inner_bias, outer, outer_bias),
        check_vma=False,
    )
```

```python
import functools

import jax
import jax.numpy as jnp
from jax import lax
from jax.experimental import pallas as pl
from jax.experimental.pallas import tpu as pltpu
from jax.sharding import PartitionSpec as P

HEADS = 12
NORM_EPS = 1e-06
MASKED = -1e30
IMAGES_MAX = 8
BF = jnp.bfloat16
F32 = jnp.float32
VMEM_LIMIT = 63 * 1024 * 1024 + 768 * 1024

VM = pltpu.VMEM
SMEM = pltpu.SMEM


COST = 1.0


def estimate(flops, bytes_accessed, transcendentals):
    return pl.CostEstimate(
        flops=int(COST * flops),
        bytes_accessed=int(COST * bytes_accessed),
        transcendentals=int(COST * transcendentals),
    )


def mm(a, b):
    return lax.dot_general(a, b, (((1,), (0,)), ((), ())), preferred_element_type=F32)


def mm_nt(a, b):
    return lax.dot_general(a, b, (((1,), (1,)), ((), ())), preferred_element_type=F32)


def mm_tn(a, b):
    return lax.dot_general(a, b, (((0,), (0,)), ((), ())), preferred_element_type=F32)


def standardize(values):
    center = jnp.mean(values, axis=-1, keepdims=True)
    centered = values - center
    moment = jnp.mean(centered * centered, axis=-1, keepdims=True)
    inv = lax.rsqrt(moment + NORM_EPS)
    return centered * inv, inv


def norm_back(grad_normed, gain, unit, inv):
    g = grad_normed * gain
    first = jnp.mean(g, axis=-1, keepdims=True)
    second = jnp.mean(g * unit, axis=-1, keepdims=True)
    return (g - first - unit * second) * inv


def targets(picks, slots, capacity, base):
    return jnp.where(slots >= 0, jnp.bitwise_xor(picks, base) * capacity + slots, -1)


def pack_into(out_refs, rows_ref, dest):
    for i, out_ref in enumerate(out_refs):
        total, rows = out_ref.shape[0], rows_ref.shape[0]
        step = pack_step(total)
        for start in range(0, total, step):
            index = lax.broadcasted_iota(jnp.int32, (step, rows), 0) + (start + i * total)
            hit = (index == dest[0:1, :]) | (index == dest[1:2, :])
            out_ref[start : start + step, :] = mm(hit.astype(BF), rows_ref[...]).astype(BF)


def unpack_rows(buffer_refs, dest, place=None):
    values = [ref[...] if len(ref.shape) == 2 else ref[place] for ref in buffer_refs]
    buffer = values[0] if len(values) == 1 else jnp.concatenate(values, axis=0)
    index = lax.broadcasted_iota(jnp.int32, (dest.shape[0], buffer.shape[0]), 1)
    hit = (index == dest[:, 0:1]) | (index == dest[:, 1:2])
    return mm(hit.astype(BF), buffer)


def kernel_call(body, inputs, in_specs, after=(), **options):
    def run(*refs):
        body(*refs[len(after) :])

    specs = [pl.BlockSpec(memory_space=pl.ANY)] * len(after) + list(in_specs)
    return pl.pallas_call(run, in_specs=specs, compiler_params=params(), **options)(*after, *inputs)


def pack_step(total):
    for step in (448, 336, 224, 192, 112, 96, 64, 48, 32, 16):
        if total % step == 0:
            return step
    return total


def params():
    return pltpu.CompilerParams(vmem_limit_bytes=VMEM_LIMIT)


def whole(shape):
    return pl.BlockSpec(shape, lambda *_: (0,) * len(shape))


def pack_kernel(base_ref, pick_ref, slot_ref, rows_ref, *out_refs, capacity):
    pack_into(out_refs, rows_ref, targets(pick_ref[...], slot_ref[...], capacity, base_ref[0]))


def pack(base, pick_rows, slot_rows, rows, buffers, capacity):
    count, width = rows.shape
    total = sum(shape[0] for shape in buffers)
    return kernel_call(
        functools.partial(pack_kernel, capacity=capacity),
        (base, pick_rows, slot_rows, rows),
        [pl.BlockSpec(memory_space=SMEM)] + [pl.BlockSpec(memory_space=VM)] * 3,
        out_shape=tuple(jax.ShapeDtypeStruct(shape, BF) for shape in buffers),
        out_specs=(pl.BlockSpec(memory_space=VM),) * len(buffers),
        cost_estimate=estimate(
            flops=2 * total * count * width, bytes_accessed=4 * total * width, transcendentals=0
        ),
        name="pack_rows",
    )


def classes(count, patch, rows, padding):
    row = lax.broadcasted_iota(jnp.int32, (rows, 1), 0)
    image = jnp.zeros((rows, 1), jnp.int32)
    for i in range(1, IMAGES_MAX):
        image = image + (row >= i * patch).astype(jnp.int32)
    return jnp.where(row < count * patch, image, padding)


def front_kernel(
    base_ref,
    count_ref,
    patch_ref,
    tokens_ref,
    gain1_ref,
    shift1_ref,
    wq_ref,
    wk_ref,
    wv_ref,
    wo_ref,
    gain2_ref,
    shift2_ref,
    pick_ref,
    slot_ref,
    n1_ref,
    q_ref,
    k_ref,
    v_ref,
    p_ref,
    linv_ref,
    mixed_ref,
    res_ref,
    *rest,
    capacity,
    head_dim,
    qb,
):
    *out_refs, n2_ref = rest
    j = pl.program_id(0)
    rows, width = tokens_ref.shape
    cols = wq_ref.shape[1]

    @pl.when(j == 0)
    def _():
        x = tokens_ref[...].astype(F32)
        unit, _ = standardize(x)
        n1_ref[...] = (unit * gain1_ref[...] + shift1_ref[...]).astype(BF)
        res_ref[...] = x

    n1 = n1_ref[...]
    q_ref[...] = mm(n1, wq_ref[...]).astype(BF)
    k_ref[...] = mm(n1, wk_ref[...]).astype(BF)
    v_ref[...] = mm(n1, wv_ref[...]).astype(BF)
    cls = classes(count_ref[0], patch_ref[0], rows, head_dim - 1)
    lane = lax.broadcasted_iota(jnp.int32, (rows, 2 * head_dim), 1)
    inner = lane % head_dim
    apart = jnp.where(inner == cls, 0.0, MASKED).astype(BF)
    member = jnp.where(inner == cls, 1.0, 0.0).astype(BF)
    ones = jnp.ones((rows, 2 * head_dim), BF)
    scale = head_dim ** (-0.5)
    for pair in range(cols // (2 * head_dim)):
        sl = slice(pair * 2 * head_dim, (pair + 1) * 2 * head_dim)
        q_pair = q_ref[:, sl] * jnp.asarray(scale, BF)
        k_pair = k_ref[:, sl]
        v_ext = jnp.concatenate([v_ref[:, sl], ones], axis=1)
        for h in range(2):
            mine = (lane >= h * head_dim) & (lane < (h + 1) * head_dim)
            qm = jnp.where(mine, q_pair, apart)
            km = jnp.where(mine, k_pair, member)
            for b in range(0, rows, qb):
                s = mm_nt(qm[b : b + qb], km)
                top = jnp.max(s, axis=-1, keepdims=True)
                p = jnp.exp(s - top).astype(BF)
                p_ref[pair * 2 + h, b : b + qb, :] = p
                ov = mm(p, v_ext)
                linv = 1.0 / ov[:, 2 * head_dim :]
                o = (ov[:, : 2 * head_dim] * linv).astype(BF)
                if h == 0:
                    mixed_ref[b : b + qb, sl] = o
                    linv_ref[b : b + qb, sl] = linv
                else:
                    keep = mine[b : b + qb]
                    mixed_ref[b : b + qb, sl] = jnp.where(keep, o, mixed_ref[b : b + qb, sl])
                    linv_ref[b : b + qb, sl] = jnp.where(keep, linv, linv_ref[b : b + qb, sl])
    res_ref[...] += mm(mixed_ref[...], wo_ref[...])

    @pl.when(j == pl.num_programs(0) - 1)
    def _():
        unit, _ = standardize(res_ref[...])
        n2_ref[...] = (unit * gain2_ref[...] + shift2_ref[...]).astype(BF)
        pack_into(out_refs, n2_ref, targets(pick_ref[...], slot_ref[...], capacity, base_ref[0]))


def front(base, count, patch, tokens, g1, s1, wq, wk, wv, wo, g2, s2, pick_rows, slot_rows, buffers, capacity, after):
    rows, width = tokens.shape
    head_dim = width // HEADS
    quad = 4 * head_dim
    steps = width // quad
    col = pl.BlockSpec((width, quad), lambda j: (0, j))
    seq = pl.BlockSpec((rows, quad), lambda j: (0, j))
    smem = pl.BlockSpec(memory_space=SMEM)
    total = sum(shape[0] for shape in buffers)
    flops = 2 * rows * width * (4 * width + 2 * rows + total)
    row = jax.ShapeDtypeStruct((rows, width), BF)
    wide = jax.ShapeDtypeStruct((rows, width), F32)
    return kernel_call(
        functools.partial(front_kernel, capacity=capacity, head_dim=head_dim, qb=rows // 5),
        (base, count, patch, tokens, g1, s1, wq, wk, wv, wo, g2, s2, pick_rows, slot_rows),
        [
            smem,
            smem,
            smem,
            whole((rows, width)),
            whole((1, width)),
            whole((1, width)),
            col,
            col,
            col,
            pl.BlockSpec((quad, width), lambda j: (j, 0)),
            whole((1, width)),
            whole((1, width)),
            whole(pick_rows.shape),
            whole(slot_rows.shape),
        ],
        after,
        grid=(steps,),
        out_shape=(row, row, row, row, jax.ShapeDtypeStruct((HEADS, rows, rows), BF), wide, row, wide)
        + tuple(jax.ShapeDtypeStruct(shape, BF) for shape in buffers),
        out_specs=(
            whole((rows, width)),
            seq,
            seq,
            seq,
            pl.BlockSpec((4, rows, rows), lambda j: (j, 0, 0)),
            seq,
            seq,
            whole((rows, width)),
        )
        + tuple(whole(shape) for shape in buffers),
        scratch_shapes=[pltpu.VMEM((rows, width), BF)],
        cost_estimate=estimate(
            flops=flops, bytes_accessed=30 * 1024 * 1024, transcendentals=HEADS * rows * rows
        ),
        name="front",
    )


GELU_A = 0.7978845608028654
GELU_B = 0.044715


def expert_kernel(base_ref, c_ref, *refs, which, axis):
    blocks = len(which)
    x_refs, refs = refs[:blocks], refs[blocks:]
    wi_own_ref, wi_far_ref, wo_own_ref, wo_far_ref, bi_ref, bo_ref, router_ref = refs[:7]
    hid_ref, gp_ref, gout_ref, gbi_ref, gbo_ref, grouter_ref = refs[7:13]
    out_refs, gin_refs = refs[13 : 13 + blocks], refs[13 + blocks : 13 + 2 * blocks]
    acc_out, acc_gin, prob = refs[13 + 2 * blocks :]
    f = pl.program_id(0)
    steps = pl.num_programs(0)
    size, width = x_refs[0].shape
    experts = router_ref.shape[1]
    mine = lax.broadcasted_iota(jnp.int32, (size, experts), 1) == lax.axis_index(axis)

    def cot_rows(i):
        place = jnp.bitwise_xor(base_ref[0], which[i]) * size
        return c_ref[pl.ds(pl.multiple_of(place, 16), size), :].astype(F32)

    @pl.when(f == 0)
    def _():
        total = jnp.zeros((1, width), F32)
        for i in range(blocks):
            sl = slice(i * size, (i + 1) * size)
            logits = mm(x_refs[i][...], router_ref[...])
            powers = jnp.exp(logits - jnp.max(logits, axis=-1, keepdims=True))
            probs = powers / jnp.sum(powers, axis=-1, keepdims=True)
            prob[sl, :] = probs
            chosen = jnp.sum(jnp.where(mine, probs, 0.0), axis=-1, keepdims=True)
            grads = (chosen * cot_rows(i)).astype(BF)
            gout_ref[sl, :] = grads
            total = total + jnp.sum(grads.astype(F32), axis=0, keepdims=True)
        gbo_ref[...] = total
        acc_out[...] = jnp.broadcast_to(bo_ref[...].astype(F32), acc_out.shape)
        acc_gin[...] = jnp.zeros(acc_gin.shape, F32)

    near = f < steps // 2
    wi = jnp.where(near, wi_own_ref[...], wi_far_ref[...])
    wo = jnp.where(near, wo_own_ref[...], wo_far_ref[...])
    bi = bi_ref[...].astype(F32)
    bias_sum = jnp.zeros(gbi_ref.shape, F32)
    step = pack_step(size)
    for i in range(blocks):
        for start in range(0, size, step):
            sl = slice(i * size + start, i * size + start + step)
            v = mm(x_refs[i][start : start + step, :], wi) + bi
            gh = mm_nt(gout_ref[sl, :], wo)
            vv = v * v
            t = jnp.tanh(v * (GELU_A + (GELU_A * GELU_B) * vv))
            half = 0.5 + 0.5 * t
            hid = (v * half).astype(BF)
            slope = half + (half * (1.0 - t)) * (v * (GELU_A + (3.0 * GELU_A * GELU_B) * vv))
            gp = (gh * slope).astype(BF)
            hid_ref[0, sl, :] = hid
            gp_ref[0, sl, :] = gp
            bias_sum = bias_sum + jnp.sum(gp.astype(F32), axis=0, keepdims=True)
            acc_out[sl, :] += mm(hid, wo)
            acc_gin[sl, :] += mm_nt(gp, wi)
    gbi_ref[...] = bias_sum

    @pl.when(f == steps - 1)
    def _():
        router = router_ref[...].astype(F32)
        grouter = jnp.zeros(grouter_ref.shape, F32)
        for i in range(blocks):
            sl = slice(i * size, (i + 1) * size)
            probs = prob[sl, :]
            chosen = jnp.sum(jnp.where(mine, probs, 0.0), axis=-1, keepdims=True)
            eo = acc_out[sl, :].astype(BF).astype(F32)
            out_refs[i][...] = (chosen * eo).astype(BF)
            gc = jnp.sum(eo * cot_rows(i), axis=-1, keepdims=True)
            gl = (gc * chosen) * (jnp.where(mine, 1.0, 0.0) - probs)
            extra = lax.dot_general(
                gl,
                router,
                (((1,), (1,)), ((), ())),
                precision=lax.Precision.HIGHEST,
                preferred_element_type=F32,
            )
            gin = (acc_gin[sl, :] + extra).astype(BF)
            if len(gin_refs[i].shape) == 2:
                gin_refs[i][...] = gin
            else:
                gin_refs[i][0] = gin
                gin_refs[i][1] = gin
            high = gl.astype(BF)
            low = (gl - high.astype(F32)).astype(BF)
            x = x_refs[i][...]
            grouter = grouter + mm_tn(high, x) + mm_tn(low, x)
        grouter_ref[...] = grouter


def expert_pass(base, cot, xs, which, twice, wi_own, wi_far, wo_own, wo_far, bi, bo, router, axis, after):
    size, width = xs[0].shape
    blocks = len(xs)
    total = blocks * size
    half = wi_own.shape[1]
    chunk = 512 if half % 512 == 0 else half
    per = half // chunk
    steps = 2 * per
    experts = router.shape[1]
    near = lambda f: jnp.minimum(f, per - 1)
    far = lambda f: jnp.maximum(f - per, 0)
    act = pl.BlockSpec((1, total, chunk), lambda f: (f, 0, 0))
    piece = (size, width)
    back = (2, size, width) if twice else piece
    results = kernel_call(
        functools.partial(expert_kernel, which=which, axis=axis),
        (base, cot, *xs, wi_own, wi_far, wo_own, wo_far, bi, bo, router),
        [pl.BlockSpec(memory_space=SMEM), whole(cot.shape)]
        + [whole((size, width))] * blocks
        + [
            pl.BlockSpec((width, chunk), lambda f: (0, near(f))),
            pl.BlockSpec((width, chunk), lambda f: (0, far(f))),
            pl.BlockSpec((chunk, width), lambda f: (near(f), 0)),
            pl.BlockSpec((chunk, width), lambda f: (far(f), 0)),
            pl.BlockSpec((1, chunk), lambda f: (0, f)),
            whole((1, width)),
            whole((width, experts)),
        ],
        after,
        grid=(steps,),
        out_shape=(
            jax.ShapeDtypeStruct((steps, total, chunk), BF),
            jax.ShapeDtypeStruct((steps, total, chunk), BF),
            jax.ShapeDtypeStruct((total, width), BF),
            jax.ShapeDtypeStruct((1, 2 * half), F32),
            jax.ShapeDtypeStruct((1, width), F32),
            jax.ShapeDtypeStruct((experts, width), F32),
        )
        + (jax.ShapeDtypeStruct(piece, BF),) * blocks
        + (jax.ShapeDtypeStruct(back, BF),) * blocks,
        out_specs=(
            act,
            act,
            whole((total, width)),
            pl.BlockSpec((1, chunk), lambda f: (0, f)),
            whole((1, width)),
            whole((experts, width)),
        )
        + (whole(piece),) * blocks
        + (whole(back),) * blocks,
        scratch_shapes=[
            pltpu.VMEM((total, width), F32),
            pltpu.VMEM((total, width), F32),
            pltpu.VMEM((total, experts), F32),
        ],
        cost_estimate=estimate(
            flops=16 * total * width * half, bytes_accessed=20 * 1024 * 1024, transcendentals=2 * total * half
        ),
        name="expert_pass",
    )
    return results[:6], results[6 : 6 + blocks], results[6 + blocks :]


def outer_kernel(*refs, counts):
    groups = []
    for count in counts:
        values = [ref[...] if len(ref.shape) == 2 else ref[0] for ref in refs[:count]]
        groups.append(values[0] if count == 1 else jnp.concatenate(values, axis=0))
        refs = refs[count:]
    x, g, hid_far, hid_own, gp_far, gp_own = groups
    wo_far_ref, wo_own_ref, wi_far_ref, wi_own_ref = refs
    wo_far_ref[...] = mm_tn(hid_far, g).astype(BF)
    wo_own_ref[...] = mm_tn(hid_own, g).astype(BF)
    wi_far_ref[...] = mm_tn(x, gp_far).astype(BF)
    wi_own_ref[...] = mm_tn(x, gp_own).astype(BF)


def outer_pass(xs, gouts, hids, gps, half, after=()):
    width = xs[0].shape[1]
    total = sum(x.shape[0] for x in xs)
    chunk = hids[0].shape[2]
    per = half // chunk
    cut = lambda values, first: [
        pl.BlockSpec((1, *value.shape[1:]), lambda f: (f + first * per, 0, 0)) for value in values
    ]
    full = lambda values: [whole(value.shape) for value in values]
    groups = (xs, gouts, hids, hids, gps, gps)
    outer = jax.ShapeDtypeStruct((half, width), BF)
    inner = jax.ShapeDtypeStruct((width, half), BF)
    return kernel_call(
        functools.partial(outer_kernel, counts=tuple(len(group) for group in groups)),
        [value for group in groups for value in group],
        full(xs) + full(gouts) + cut(hids, 1) + cut(hids, 0) + cut(gps, 1) + cut(gps, 0),
        after,
        grid=(per,),
        out_shape=(outer, outer, inner, inner),
        out_specs=(pl.BlockSpec((chunk, width), lambda f: (f, 0)),) * 2
        + (pl.BlockSpec((width, chunk), lambda f: (0, f)),) * 2,
        cost_estimate=estimate(
            flops=8 * total * width * half, bytes_accessed=30 * 1024 * 1024, transcendentals=0
        ),
        name="outer_pass",
    )


def live_rows(count, patch, rows):
    row = lax.broadcasted_iota(jnp.int32, (rows, 1), 0)
    return row < count * patch


def assemble_kernel(base_ref, *refs):
    *block_refs, out_ref = refs
    size = block_refs[0].shape[0]
    for i, block_ref in enumerate(block_refs):
        place = jnp.bitwise_xor(base_ref[0], i) * size
        out_ref[pl.ds(pl.multiple_of(place, 16), size), :] = block_ref[...]


def assemble(base, blocks, after):
    size, width = blocks[0].shape
    return kernel_call(
        assemble_kernel,
        (base, *blocks),
        [pl.BlockSpec(memory_space=SMEM)] + [pl.BlockSpec(memory_space=VM)] * len(blocks),
        after,
        out_shape=jax.ShapeDtypeStruct((len(blocks) * size, width), BF),
        out_specs=pl.BlockSpec(memory_space=VM),
        cost_estimate=estimate(flops=0, bytes_accessed=4 * len(blocks) * size * width, transcendentals=0),
        name="assemble",
    )


def output_kernel(base_ref, count_ref, patch_ref, pick_ref, slot_ref, res_ref, *rest, capacity):
    *back_refs, out_ref = rest
    live = live_rows(count_ref[0], patch_ref[0], res_ref.shape[0])
    mixture = unpack_rows(back_refs, targets(pick_ref[...], slot_ref[...], capacity, base_ref[0]))
    out_ref[...] = jnp.where(live, res_ref[...] + mixture, 0.0).astype(BF)


def output_pass(base, count, patch, picks, slots, back, res, capacity, after):
    rows, width = res.shape
    return kernel_call(
        functools.partial(output_kernel, capacity=capacity),
        (base, count, patch, picks, slots, res, *back),
        [pl.BlockSpec(memory_space=SMEM)] * 3 + [pl.BlockSpec(memory_space=VM)] * (3 + len(back)),
        after,
        out_shape=jax.ShapeDtypeStruct((rows, width), BF),
        out_specs=pl.BlockSpec(memory_space=VM),
        cost_estimate=estimate(
            flops=4 * rows * rows * width, bytes_accessed=6 * 1024 * 1024, transcendentals=0
        ),
        name="output_pass",
    )


def middle_kernel(
    base_ref,
    place_ref,
    core_ref,
    count_ref,
    patch_ref,
    pick_ref,
    slot_ref,
    cot_ref,
    res_ref,
    gain2_ref,
    mixed_ref,
    wo_ref,
    *rest,
    capacity,
):
    *back_refs, gres_ref, gmix_ref, keep_ref, send_ref, ggain_ref, gshift_ref = rest
    live = live_rows(count_ref[0], patch_ref[0], res_ref.shape[0])
    gn = unpack_rows(back_refs, targets(pick_ref[...], slot_ref[...], capacity, base_ref[0]), place_ref[0])
    unit, inv = standardize(res_ref[...])
    ggain_ref[...] = jnp.sum(gn * unit, axis=0, keepdims=True)
    gshift_ref[...] = jnp.sum(gn, axis=0, keepdims=True)
    gout = jnp.where(live, cot_ref[...].astype(F32), 0.0)
    gres = gout + norm_back(gn, gain2_ref[...], unit, inv)
    gres_ref[...] = gres
    branch = gres.astype(BF)
    gmix_ref[...] = mm_nt(branch, wo_ref[...]).astype(BF)
    keep_ref[...] = mm_tn(core_half(mixed_ref, core_ref[0]), branch).astype(BF)
    send_ref[...] = mm_tn(core_half(mixed_ref, 1 - core_ref[0]), branch).astype(BF)


def core_half(ref, core):
    size = ref.shape[1] // 2
    return ref[:, pl.ds(pl.multiple_of(core * size, 128), size)]


def middle_pass(base, place, core, count, patch, picks, slots, back, cot, res, g2, mixed, wo, capacity, after):
    rows, width = res.shape
    vm = pl.BlockSpec(memory_space=VM)
    piece = jax.ShapeDtypeStruct((width // 2, width), BF)
    return kernel_call(
        functools.partial(middle_kernel, capacity=capacity),
        (base, place, core, count, patch, picks, slots, cot, res, g2, mixed, wo, *back),
        [pl.BlockSpec(memory_space=SMEM)] * 5 + [vm] * (7 + len(back)),
        after,
        out_shape=(
            jax.ShapeDtypeStruct((rows, width), F32),
            jax.ShapeDtypeStruct((rows, width), BF),
            piece,
            piece,
            jax.ShapeDtypeStruct((1, width), F32),
            jax.ShapeDtypeStruct((1, width), F32),
        ),
        out_specs=(vm,) * 6,
        cost_estimate=estimate(
            flops=400 * rows * width * (rows + width), bytes_accessed=14 * 1024 * 1024, transcendentals=0
        ),
        name="middle_pass",
    )


def attend_back_kernel(
    core_ref,
    n1_ref,
    q_ref,
    k_ref,
    v_ref,
    p_ref,
    linv_ref,
    mixed_ref,
    gmix_ref,
    dq_ref,
    dk_ref,
    dv_ref,
    keep_ref,
    send_ref,
    ds_ref,
    *,
    head_dim,
    qb,
):
    rows, cols = q_ref.shape
    lane = lax.broadcasted_iota(jnp.int32, (rows, 2 * head_dim), 1)
    scale = jnp.asarray(head_dim ** (-0.5), BF)
    zero = jnp.zeros((rows, 2 * head_dim), BF)
    for pair in range(cols // (2 * head_dim)):
        sl = slice(pair * 2 * head_dim, (pair + 1) * 2 * head_dim)
        q_pair = q_ref[:, sl] * scale
        k_pair = k_ref[:, sl] * scale
        v_pair = v_ref[:, sl]
        do_pair = (gmix_ref[:, sl].astype(F32) * linv_ref[:, sl]).astype(BF)
        inner = do_pair.astype(F32) * mixed_ref[:, sl].astype(F32)
        dq = None
        for h in range(2):
            mine = (lane >= h * head_dim) & (lane < (h + 1) * head_dim)
            dom = jnp.where(mine, do_pair, zero)
            qm = jnp.where(mine, q_pair, zero)
            km = jnp.where(mine, k_pair, zero)
            row_inner = jnp.sum(jnp.where(mine, inner, 0.0), axis=-1, keepdims=True)
            head = pair * 2 + h
            for b in range(0, rows, qb):
                dp = mm_nt(dom[b : b + qb], v_pair)
                p = p_ref[head, b : b + qb, :].astype(F32)
                ds_ref[b : b + qb, :] = (p * (dp - row_inner[b : b + qb])).astype(BF)
            ds = ds_ref[...]
            dq_h = mm(ds, km)
            dk_h = mm_tn(ds, qm)
            dv_h = mm_tn(p_ref[head], dom)
            if h == 0:
                dq, dk, dv = dq_h, dk_h, dv_h
            else:
                dq, dk, dv = dq + dq_h, dk + dk_h, dv + dv_h
        dq_ref[:, sl] = dq.astype(BF)
        dk_ref[:, sl] = dk.astype(BF)
        dv_ref[:, sl] = dv.astype(BF)
    grads = jnp.concatenate([dq_ref[...], dk_ref[...], dv_ref[...]], axis=1)
    keep_ref[...] = mm_tn(core_half(n1_ref, core_ref[0]), grads).astype(BF)
    send_ref[...] = mm_tn(core_half(n1_ref, 1 - core_ref[0]), grads).astype(BF)


def attend_back(core, n1, q, k, v, p, linv, mixed, gmix, after):
    rows, width = n1.shape
    head_dim = width // HEADS
    quad = 4 * head_dim
    steps = width // quad
    seq = pl.BlockSpec((rows, quad), lambda j: (0, j))
    grads = pl.BlockSpec((width // 2, 3 * quad), lambda j: (j, 0))
    return kernel_call(
        functools.partial(attend_back_kernel, head_dim=head_dim, qb=rows),
        (core, n1, q, k, v, p, linv, mixed, gmix),
        [
            pl.BlockSpec(memory_space=SMEM),
            whole((rows, width)),
            seq,
            seq,
            seq,
            pl.BlockSpec((4, rows, rows), lambda j: (j, 0, 0)),
            seq,
            seq,
            seq,
        ],
        after,
        grid=(steps,),
        out_shape=(jax.ShapeDtypeStruct((rows, width), BF),) * 3
        + (jax.ShapeDtypeStruct((steps * (width // 2), 3 * quad), BF),) * 2,
        out_specs=(seq, seq, seq, grads, grads),
        scratch_shapes=[pltpu.VMEM((rows, rows), BF)],
        cost_estimate=estimate(
            flops=2 * rows * width * (3 * width + 4 * rows), bytes_accessed=24 * 1024 * 1024, transcendentals=0
        ),
        name="attend_back",
    )


def tokens_kernel(*refs, parts):
    core_ref, dq_ref, dk_ref, dv_ref, wq_ref, wk_ref, wv_ref, tokens_ref, gain1_ref, gres_ref = refs[:10]
    ggain2_ref, gshift2_ref = refs[10:12]
    gbi_refs, refs = refs[12 : 12 + parts], refs[12 + parts :]
    gbo_refs, refs = refs[:parts], refs[parts:]
    grouter_refs, (gtok_ref, small_ref) = refs[:parts], refs[parts:]
    gn = mm_nt(dq_ref[...], wq_ref[...]) + mm_nt(dk_ref[...], wk_ref[...]) + mm_nt(dv_ref[...], wv_ref[...])
    unit, inv = standardize(tokens_ref[...].astype(F32))
    gtok_ref[...] = gres_ref[...] + norm_back(gn, gain1_ref[...], unit, inv)
    width = gn.shape[1]
    gbi = sum(ref[...] for ref in gbi_refs)
    rows = gbi.shape[1] // 2 // width
    experts = grouter_refs[0].shape[0]
    zeros = jnp.zeros((small_ref.shape[1] - rows - 5 - experts, width), F32)
    common = [
        sum(ref[...] for ref in gbo_refs),
        jnp.sum(gn * unit, axis=0, keepdims=True),
        jnp.sum(gn, axis=0, keepdims=True),
        ggain2_ref[...],
        gshift2_ref[...],
        sum(ref[...] for ref in grouter_refs),
    ]
    columns = small_ref.shape[0] // 2
    for core in range(2):
        mine = core_ref[0] == core
        for column in range(columns):
            at = core * columns + column
            for i in range(rows):
                own, far = (gbi[:, (first + i) * width : (first + i + 1) * width] for first in (0, rows))
                small_ref[at, i : i + 1, :] = jnp.where(mine, own, far)
            place = rows
            for value in common:
                small_ref[at, place : place + value.shape[0], :] = value
                place += value.shape[0]
            if zeros.shape[0]:
                small_ref[at, place:, :] = zeros


def tokens_pass(core, columns, grads, weights, tokens, g1, gres, ggain2, gshift2, sums, after):
    rows, width = tokens.shape
    vm = pl.BlockSpec(memory_space=VM)
    gbi, gbo, grouter = sums
    height = gbi[0].shape[1] // 2 // width + 5 + grouter[0].shape[0]
    inputs = (*grads, *weights, tokens, g1, gres, ggain2, gshift2, *gbi, *gbo, *grouter)
    return kernel_call(
        functools.partial(tokens_kernel, parts=len(gbi)),
        (core, *inputs),
        [pl.BlockSpec(memory_space=SMEM)] + [vm] * len(inputs),
        after,
        out_shape=(
            jax.ShapeDtypeStruct((rows, width), F32),
            jax.ShapeDtypeStruct((2 * columns, height + -height % 16, width), F32),
        ),
        out_specs=(vm,) * 2,
        cost_estimate=estimate(flops=600 * rows * width * width, bytes_accessed=0, transcendentals=0),
        name="tokens_pass",
    )


def swap(value, axis, bit):
    return lax.ppermute(value, axis, [(i, i ^ bit) for i in range(lax.axis_size(axis))])


def block(value, index, count):
    size = value.shape[0] // count
    return lax.dynamic_slice_in_dim(value, index * size, size, 0)


def narrow_sum(*terms):
    return functools.reduce(jnp.add, [term.astype(F32) for term in terms]).astype(BF)


def axis_bits(axis):
    me = lax.axis_index(axis)
    return [(me >> level) & 1 for level in range(lax.axis_size(axis).bit_length() - 1)]


def prefetch_call(body, scalars, inputs, in_specs, grid, out_specs, after, **options):
    def run(scalar_ref, *refs):
        body(scalar_ref, *refs[len(after) :])

    spec = pltpu.PrefetchScalarGridSpec(
        num_scalar_prefetch=1,
        grid=grid,
        in_specs=[pl.BlockSpec(memory_space=pl.ANY)] * len(after) + list(in_specs),
        out_specs=out_specs,
    )
    return pl.pallas_call(run, grid_spec=spec, compiler_params=params(), **options)(scalars, *after, *inputs)


def pick_kernel(index_ref, *refs, counts):
    outs = refs[sum(counts) :]
    for count, out_ref in zip(counts, outs):
        terms, refs = refs[:count], refs[count:]
        out_ref[...] = sum(ref[...].astype(F32) for ref in terms).astype(BF)


def pick_sums(indices, groups, after, cost=0):
    flat, in_specs, out_specs, shapes = [], [], [], []
    for group, height in groups:
        width = group[0].shape[1]
        for value in group:
            in_specs.append(pl.BlockSpec((height, width), lambda i, at, k=len(flat): (at[k], 0)))
            flat.append(value)
        out_specs.append(whole((height, width)))
        shapes.append(jax.ShapeDtypeStruct((height, width), BF))
    return prefetch_call(
        functools.partial(pick_kernel, counts=tuple(len(group) for group, _ in groups)),
        indices,
        flat,
        in_specs,
        (1,),
        tuple(out_specs),
        after,
        out_shape=tuple(shapes),
        cost_estimate=estimate(flops=cost, bytes_accessed=2 * sum(v.size for v in flat), transcendentals=0),
        name="pick_sums",
    )


def merge_kernel(bits_ref, *refs):
    outs = refs[len(refs) // 3 * 2 :]
    for i, out_ref in enumerate(outs):
        for ref, bit in ((refs[2 * i], bits_ref[i]), (refs[2 * i + 1], 1 - bits_ref[i])):
            size = ref.shape[0]
            out_ref[pl.ds(pl.multiple_of(bit * size, 16), size), :] = ref[...].astype(out_ref.dtype)


def merge(bits, pairs, dtype, after=()):
    flat = [value for pair in pairs for value in pair]
    vm = pl.BlockSpec(memory_space=VM)
    return kernel_call(
        merge_kernel,
        (bits, *flat),
        [pl.BlockSpec(memory_space=SMEM)] + [vm] * len(flat),
        after,
        out_shape=tuple(jax.ShapeDtypeStruct((2 * mine.shape[0], mine.shape[1]), dtype) for mine, _ in pairs),
        out_specs=(vm,) * len(pairs),
        cost_estimate=estimate(flops=0, bytes_accessed=6 * sum(v.size for v in flat), transcendentals=0),
        name="merge",
    )


def matrices_kernel(me_ref, lead_ref, lead_far_ref, main_ref, main_far_ref, *out_refs, places):
    size = lead_ref.shape[0]
    for (i, first), out_ref in zip(places, out_refs):
        matrix = jnp.bitwise_xor(me_ref[0], i)
        rows = out_ref.shape[0]
        lead = slice(first, first + rows)

        @pl.when(matrix == 0)
        def _():
            out_ref[...] = (lead_ref[lead, :].astype(F32) + lead_far_ref[lead, :].astype(F32)).astype(BF)

        @pl.when(matrix > 0)
        def _():
            place = pl.ds(pl.multiple_of((matrix - 1) * size + first, 16), rows)
            out_ref[...] = (main_ref[place, :].astype(F32) + main_far_ref[place, :].astype(F32)).astype(BF)


def matrices(me, lead, lead_far, main, main_far, after):
    size, width = lead.shape
    count = 1 + main.shape[0] // size
    places = [(i, 0, size) for i in range(count - 1)] + [(count - 1, i * (size // 2), size // 2) for i in range(2)]
    vm = pl.BlockSpec(memory_space=VM)
    return kernel_call(
        functools.partial(matrices_kernel, places=[place[:2] for place in places]),
        (me, lead, lead_far, main, main_far),
        [pl.BlockSpec(memory_space=SMEM)] + [vm] * 4,
        after,
        out_shape=tuple(jax.ShapeDtypeStruct((rows, width), BF) for _, _, rows in places),
        out_specs=(vm,) * len(places),
        cost_estimate=estimate(flops=0, bytes_accessed=8 * size * count * width, transcendentals=0),
        name="matrices",
    )


def relay_kernel(x_ref, y_ref, for_y_ref, for_x_ref, x_out_ref, y_out_ref):
    size = for_x_ref.shape[0]
    x_out_ref[:size, :] = x_ref[:size, :]
    x_out_ref[size:, :] = (x_ref[size:, :].astype(F32) + for_x_ref[...].astype(F32)).astype(BF)
    y_out_ref[:size, :] = (y_ref[:size, :].astype(F32) + for_y_ref[...].astype(F32)).astype(BF)
    y_out_ref[size:, :] = y_ref[size:, :]


def relay(x, y, for_y, for_x, after):
    vm = pl.BlockSpec(memory_space=VM)
    shape = jax.ShapeDtypeStruct(x.shape, BF)
    return kernel_call(
        relay_kernel,
        (x, y, for_y, for_x),
        [vm] * 4,
        after,
        out_shape=(shape, shape),
        out_specs=(vm, vm),
        cost_estimate=estimate(flops=0, bytes_accessed=0, transcendentals=0),
        name="relay",
    )


def layers_kernel(*refs):
    *part_refs, out_ref = refs
    size = out_ref.shape[1]
    for i in range(out_ref.shape[0]):
        rows = slice(i * size, (i + 1) * size)
        out_ref[i] = sum(ref[rows, :].astype(F32) for ref in part_refs).astype(BF)


def layers(parts, count):
    height, width = parts[0].shape
    vm = pl.BlockSpec(memory_space=VM)
    return kernel_call(
        layers_kernel,
        parts,
        [vm] * len(parts),
        out_shape=jax.ShapeDtypeStruct((count, height // count, width), BF),
        out_specs=vm,
        cost_estimate=estimate(flops=0, bytes_accessed=0, transcendentals=0),
        name="layers",
    )


def quarter_kernel(small_ref, parts_ref, gbi_ref, gbo_ref, out_ref, *, half_rows):
    small = sum(small_ref[i] for i in range(small_ref.shape[0]))
    width = small.shape[1]
    for i in range(half_rows):
        gbi_ref[:, i * width : (i + 1) * width] = small[i : i + 1, :]
    gbo_ref[...] = small[half_rows : half_rows + 1, :]
    rows = parts_ref.shape[1]
    out_ref[:rows, :] = sum(parts_ref[i].astype(F32) for i in range(parts_ref.shape[0])).astype(BF)
    out_ref[rows:, :] = small.astype(BF)


def quarter(small, parts, half_rows):
    _, rows, width = parts.shape
    vm = pl.BlockSpec(memory_space=VM)
    return kernel_call(
        functools.partial(quarter_kernel, half_rows=half_rows),
        [small, parts],
        [vm] * 2,
        out_shape=(
            jax.ShapeDtypeStruct((1, half_rows * width), F32),
            jax.ShapeDtypeStruct((1, width), F32),
            jax.ShapeDtypeStruct((rows + small.shape[1], width), BF),
        ),
        out_specs=(vm,) * 3,
        cost_estimate=estimate(flops=0, bytes_accessed=0, transcendentals=0),
        name="quarter",
    )


def whole_kernel(base_ref, *refs, blocks, rows, skip, experts):
    block_refs, (matrix_ref, *vector_refs, router_ref) = refs[:blocks], refs[blocks:]
    for i, ref in enumerate(block_refs):
        place = jnp.bitwise_xor(base_ref[0], i) * rows
        matrix_ref[pl.ds(pl.multiple_of(place, 16), rows), :] = ref[:rows, :]
    total = sum(ref[rows:, :].astype(F32) for ref in block_refs)
    for i, ref in enumerate(vector_refs):
        ref[...] = total[skip + i]
    first = skip + len(vector_refs)
    router_ref[...] = total[first : first + experts]


def whole_matrix(base, blocks, rows, skip, experts):
    width = blocks[0].shape[1]
    vm = pl.BlockSpec(memory_space=VM)
    return kernel_call(
        functools.partial(whole_kernel, blocks=len(blocks), rows=rows, skip=skip, experts=experts),
        (base, *blocks),
        [pl.BlockSpec(memory_space=SMEM)] + [vm] * len(blocks),
        out_shape=(jax.ShapeDtypeStruct((len(blocks) * rows, width), BF),)
        + (jax.ShapeDtypeStruct((width,), F32),) * 4
        + (jax.ShapeDtypeStruct((experts, width), F32),),
        out_specs=(vm,) * 6,
        cost_estimate=estimate(flops=0, bytes_accessed=4 * width * width, transcendentals=0),
        name="whole_matrix",
    )


def spread_kernel(core_ref, me_ref, *refs, places, blocks, earlier):
    block_refs, refs = refs[:blocks], refs[blocks + earlier :]
    dwq_ref, dwk_ref, dwv_ref, dwo_ref, wide, sems = refs
    width = dwo_ref.shape[1]
    third = width // 3
    copies = []
    for slot, (matrix, parts) in enumerate(places):
        for index, first, own in parts:
            ref = block_refs[index]
            core = core_ref[0] if own else 1 - core_ref[0]
            rows = pl.ds(pl.multiple_of(core * (width // 2) + first, 16), ref.shape[0])
            wide[slot, rows, :] = ref[...].astype(F32)
        matrix = jnp.bitwise_xor(me_ref[0], matrix)
        lead = pltpu.make_async_copy(wide.at[slot], dwo_ref, sems.at[slot, 0])
        columns = pl.ds(pl.multiple_of(jnp.maximum(matrix - 1, 0) * third, 128), third)
        rest = [
            pltpu.make_async_copy(
                wide.at[slot, :, i * third : (i + 1) * third], out_ref.at[:, columns], sems.at[slot, i]
            )
            for i, out_ref in enumerate((dwq_ref, dwk_ref, dwv_ref))
        ]
        copies.append((matrix, lead, rest))

        @pl.when(matrix == 0)
        def _():
            lead.start()

        @pl.when(matrix > 0)
        def _():
            for copy in rest:
                copy.start()

    for matrix, lead, rest in copies:

        @pl.when(matrix == 0)
        def _():
            lead.wait()

        @pl.when(matrix > 0)
        def _():
            for copy in rest:
                copy.wait()


def spread(core, me, groups, earlier=()):
    flat, places = [], []
    for matrix, parts in groups:
        places.append((matrix, [(len(flat) + i, first, own) for i, (_, first, own) in enumerate(parts)]))
        flat += [value for value, _, _ in parts]
    width = flat[0].shape[1]
    vm, anywhere = pl.BlockSpec(memory_space=VM), pl.BlockSpec(memory_space=pl.ANY)
    return kernel_call(
        functools.partial(spread_kernel, places=places, blocks=len(flat), earlier=len(earlier)),
        (core, me, *flat, *earlier),
        [pl.BlockSpec(memory_space=SMEM)] * 2 + [vm] * len(flat) + [anywhere] * len(earlier),
        out_shape=(jax.ShapeDtypeStruct((width, width), F32),) * 4,
        out_specs=(anywhere,) * 4,
        scratch_shapes=[pltpu.VMEM((len(groups), width, width), F32), pltpu.SemaphoreType.DMA((len(groups), 3))],
        input_output_aliases={2 + len(flat) + i: i for i in range(len(earlier))},
        cost_estimate=estimate(flops=0, bytes_accessed=0, transcendentals=0),
        name="spread",
    )


def butterfly(value, axis):
    step = 1
    while step < lax.axis_size(axis):
        value = (value.astype(F32) + swap(value, axis, step).astype(F32)).astype(value.dtype)
        step *= 2
    return value


def hold(value, after):
    return pl.pallas_call(
        lambda *refs: None,
        out_shape=jax.ShapeDtypeStruct(value.shape, value.dtype),
        in_specs=[pl.BlockSpec(memory_space=pl.ANY)] * 2,
        out_specs=pl.BlockSpec(memory_space=pl.ANY),
        input_output_aliases={0: 0},
        name="hold",
    )(value, after)


def shards(
    tokens,
    cotangent,
    ln1_gain,
    ln1_shift,
    w_query,
    w_key,
    w_value,
    w_output,
    ln2_gain,
    ln2_shift,
    w_router,
    w_inner,
    b_inner,
    w_outer,
    b_outer,
    image_count,
    patches,
    picks,
    slots,
):
    rows, width = tokens.shape
    experts = w_router.shape[1]
    groups = lax.axis_size("expert")
    capacity = 21 * rows // (10 * experts)
    half = w_inner.shape[2]
    g1, s1 = ln1_gain[None, :], ln1_shift[None, :]
    g2, s2 = ln2_gain[None, :], ln2_shift[None, :]
    pick_rows, slot_rows = picks.T, slots.T
    start = jnp.zeros((1,), jnp.int32)
    whole_buffer = [(experts * capacity, width)]

    def exchange(rows_out):
        cut = rows_out.reshape(experts, capacity, width)
        cut = lax.all_to_all(cut, "expert", split_axis=0, concat_axis=0, tiled=True)
        return cut.reshape(experts * capacity, width)

    if groups <= 4:
        me = lax.axis_index("expert").astype(jnp.int32)
        base = me.reshape(1)
        buffers = [(capacity, width)] * groups
        parts = [[i] for i in range(groups)]

        def exchange_block(blocks, i):
            return blocks[i] if i == 0 else swap(blocks[i], "expert", i)

        def exchange_pair(pair, i):
            members = [[j, j ^ i] for j in range(groups) if j < j ^ i]
            return lax.all_to_all(
                pair, "expert", split_axis=0, concat_axis=0, tiled=True, axis_index_groups=members
            )

    else:
        me = jnp.zeros((), jnp.int32)
        base, buffers, parts = start, whole_buffer, [[0]]

        def exchange_block(blocks, i):
            return exchange(blocks[0])

    place = (1 - ((me >> 1) & 1)).reshape(1)
    core = lax.axis_index("hidden").astype(jnp.int32).reshape(1)
    column = lax.axis_index("dp").astype(jnp.int32).reshape(1)
    columns = lax.axis_size("dp")
    bit_x, bit_y = axis_bits("dp")
    not_x, not_y, zero = 1 - bit_x, 1 - bit_y, jnp.zeros_like(bit_x)
    indices = [
        jnp.stack([not_x] * 2 + [not_y] * 2),
        jnp.stack([2 * bit_x + not_y] * 2 + [not_y] + [2 * bit_y + not_x] * 2 + [not_x]),
        jnp.stack([2 * bit_x + bit_y] * 2 + [bit_y, zero] + [2 * bit_y + bit_x] * 2 + [bit_x, zero]),
    ]
    bits, bits_after = jnp.stack([bit_x, bit_y]), jnp.stack([bit_y, bit_x])
    cot_out = pack(start, pick_rows, slot_rows, cotangent, whole_buffer, capacity)[0]
    cot_in = exchange(cot_out)
    wi_own, wo_own = w_inner[0], w_outer[0]
    wi_far, wo_far = swap(wi_own, "hidden", 1), swap(wo_own, "hidden", 1)
    bi_all = jnp.concatenate([b_inner, swap(b_inner, "hidden", 1)], axis=1)
    n1, q, k, v, p, linv, mixed, res, *outgoing = front(
        base, image_count, patches, tokens, g1, s1, w_query, w_key, w_value, w_output, g2, s2,
        pick_rows, slot_rows, buffers, capacity, [cot_out],
    )
    xs, sums, hids, gps, gouts, out_rows, gin_back = [], [], [], [], [], [], []
    for which in parts:
        i = which[0]
        local = i == 0 and groups <= 4
        if i > 1:
            outgoing[i] = hold(outgoing[i], cot_in if i == 2 else xs[-1])
        x = [exchange_block(outgoing, i)]
        (hid, gp, gout, *small), outs, gins = expert_pass(
            base, cot_out if local else cot_in, x, which, i > 1, wi_own, wi_far, wo_own, wo_far, bi_all, b_outer,
            w_router, "expert", hids[-1:],
        )
        xs.extend(x)
        hids.append(hid)
        gps.append(gp)
        gouts.append(gout)
        sums.append(small)
        out_rows.extend(outs)
        gin_back.append(exchange_pair(gins[0], i) if i > 1 else exchange_block([gins[0]] * groups, i))
    assembled = assemble(base, out_rows, [])
    dwo_far, dwo_own, dwi_far, dwi_own = outer_pass(xs, gouts, hids, gps, half, [assembled])

    gres, gmix, dwout_keep, dwout_send, ggain2, gshift2 = middle_pass(
        base, place, core, image_count, patches, picks, slots, gin_back, cotangent, res, g2, mixed, w_output,
        capacity, [dwi_own],
    )
    dwo_far, dwi_far = swap(dwo_far, "hidden", 1), swap(dwi_far, "hidden", 1)
    half_o, half_i = half // 2, width // 2
    dwo_send, dwi_send = pick_sums(
        indices[0],
        [([dwo_own, dwo_far], half_o), ([dwi_own, dwi_far], half_i)],
        [gmix],
    )
    dwo_got, dwi_got = swap(dwo_send, "dp", 1), swap(dwi_send, "dp", 2)
    dq, dk, dv, main_keep, main_send = attend_back(core, n1, q, k, v, p, linv, mixed, gmix, [dwo_send])
    dwo_send, dwi_send = pick_sums(
        indices[1],
        [([dwo_own, dwo_far, dwo_got], half_o // 2), ([dwi_own, dwi_far, dwi_got], half_i // 2)],
        [main_send],
        10**11,
    )
    dwo_last, dwi_last = swap(dwo_send, "dp", 2), swap(dwi_send, "dp", 1)
    blocks = matrices(
        column, dwout_keep, swap(dwout_send, "hidden", 1), main_keep, swap(main_send, "hidden", 1), [dwo_send]
    )
    gtok, small = tokens_pass(
        core, columns, (dq, dk, dv), (w_query, w_key, w_value), tokens, g1, gres, ggain2, gshift2, list(zip(*sums)),
        [blocks[0]],
    )
    passing = [swap(blocks[3], "dp", 1), swap(blocks[4], "dp", 2)]
    to_x, to_y = relay(blocks[1], blocks[2], *passing, [gtok])
    arrived = [blocks[0], swap(to_x, "dp", 1), swap(to_y, "dp", 2)]
    out_back = exchange(hold(assembled, gin_back[-1]))
    small = lax.all_to_all(hold(small, out_back), ("hidden", "dp"), split_axis=0, concat_axis=0, tiled=True)
    dwo_piece, dwi_piece = pick_sums(
        indices[2],
        [([dwo_own, dwo_far, dwo_got, dwo_last], half_o // 2), ([dwi_own, dwi_far, dwi_got, dwi_last], half_i // 2)],
        [gtok],
    )
    rows_half = width // 2
    half_rows = half // width
    offset = half_rows + 1
    if groups <= 4:
        parts = layers(arrived, groups)
        parts = lax.all_to_all(parts, "expert", split_axis=0, concat_axis=0, tiled=True)
        gbi, gbo, piece = quarter(small, parts, half_rows)
        pieces = [piece] + [swap(piece, "expert", i) for i in range(1, groups)]
        matrix, *vectors = whole_matrix(base, pieces, rows_half // groups, offset, experts)
    else:
        gbi, gbo, piece = quarter(small, layers(arrived, 1), half_rows)
        matrix, *vectors = whole_matrix(start, [butterfly(piece, "expert")], rows_half, offset, experts)
    dwo_half, dwi_half = merge(
        bits_after,
        [(dwo_piece, swap(dwo_piece, "dp", 2)), (dwi_piece, swap(dwi_piece, "dp", 1))],
        BF,
    )
    block_out = output_pass(start, image_count, patches, picks, slots, [out_back], res, capacity, [blocks[0]])
    dwo, dwi = merge(
        bits, [(dwo_half, swap(dwo_half, "dp", 1)), (dwi_half, swap(dwi_half, "dp", 2))], F32, [block_out]
    )
    across = columns - 1
    cut = rows_half // 2
    near = [swap(matrix, "dp", 1), swap(matrix, "dp", 2)]
    corner = pick_sums(jnp.stack([zero, zero + 1]), [([near[0]], cut), ([near[1]], cut)], [])
    corner = [swap(corner[0], "dp", 2), swap(corner[1], "dp", 1)]
    near = [hold(value, dwi) for value in near]
    early = [
        (i, [(value, 0, True), (swap(value, "hidden", 1), 0, False)]) for i, value in enumerate([matrix, *near])
    ]
    grads = spread(core, column, early)
    corner = [hold(value, grads[0]) for value in corner]
    late = [(corner[0], 0, True), (corner[1], cut, True)]
    late += [(swap(value, "hidden", 1), first, False) for value, first, _ in late]
    dwq, dwk, dwv, dwout = spread(core, column, [(across, late)], grads)
    return (
        block_out,
        gtok,
        vectors[0],
        vectors[1],
        dwq,
        dwk,
        dwv,
        dwout,
        vectors[2],
        vectors[3],
        vectors[4].T,
        dwi[None],
        gbi,
        dwo[None],
        gbo,
    )


def solution(mesh):
    rows = P(("expert", "hidden", "dp"), None)
    device = P(("expert", "hidden", "dp"))
    inner = P("expert", None, "hidden")
    inner_bias = P("expert", "hidden")
    outer = P("expert", "hidden", None)
    outer_bias = P("expert", None)
    return jax.shard_map(
        shards,
        mesh=mesh,
        in_specs=(rows, rows) + (P(),) * 9 + (inner, inner_bias, outer, outer_bias, device, device, rows, rows),
        out_specs=(rows, rows) + (P(),) * 9 + (inner, inner_bias, outer, outer_bias),
        check_vma=False,
    )
```

```python
import functools

import jax
import jax.numpy as jnp
from jax import lax
from jax.experimental import pallas as pl
from jax.experimental.pallas import tpu as pltpu
from jax.sharding import PartitionSpec as P

HEADS = 12
NORM_EPS = 1e-06
MASKED = -1e30
IMAGES_MAX = 8
BF = jnp.bfloat16
F32 = jnp.float32
VMEM_LIMIT = 63 * 1024 * 1024 + 768 * 1024

VM = pltpu.VMEM
SMEM = pltpu.SMEM


COST = 1.0


def estimate(flops, bytes_accessed, transcendentals):
    return pl.CostEstimate(
        flops=int(COST * flops),
        bytes_accessed=int(COST * bytes_accessed),
        transcendentals=int(COST * transcendentals),
    )


def mm(a, b):
    return lax.dot_general(a, b, (((1,), (0,)), ((), ())), preferred_element_type=F32)


def mm_nt(a, b):
    return lax.dot_general(a, b, (((1,), (1,)), ((), ())), preferred_element_type=F32)


def mm_tn(a, b):
    return lax.dot_general(a, b, (((0,), (0,)), ((), ())), preferred_element_type=F32)


def standardize(values):
    center = jnp.mean(values, axis=-1, keepdims=True)
    centered = values - center
    moment = jnp.mean(centered * centered, axis=-1, keepdims=True)
    inv = lax.rsqrt(moment + NORM_EPS)
    return centered * inv, inv


def norm_back(grad_normed, gain, unit, inv):
    g = grad_normed * gain
    first = jnp.mean(g, axis=-1, keepdims=True)
    second = jnp.mean(g * unit, axis=-1, keepdims=True)
    return (g - first - unit * second) * inv


def targets(picks, slots, capacity, base):
    return jnp.where(slots >= 0, jnp.bitwise_xor(picks, base) * capacity + slots, -1)


def pack_into(out_refs, rows_ref, dest):
    for i, out_ref in enumerate(out_refs):
        total, rows = out_ref.shape[0], rows_ref.shape[0]
        step = pack_step(total)
        for start in range(0, total, step):
            index = lax.broadcasted_iota(jnp.int32, (step, rows), 0) + (start + i * total)
            hit = (index == dest[0:1, :]) | (index == dest[1:2, :])
            out_ref[start : start + step, :] = mm(hit.astype(BF), rows_ref[...]).astype(BF)


def unpack_rows(buffer_refs, dest, place=None):
    values = [ref[...] if len(ref.shape) == 2 else ref[place] for ref in buffer_refs]
    buffer = values[0] if len(values) == 1 else jnp.concatenate(values, axis=0)
    index = lax.broadcasted_iota(jnp.int32, (dest.shape[0], buffer.shape[0]), 1)
    hit = (index == dest[:, 0:1]) | (index == dest[:, 1:2])
    return mm(hit.astype(BF), buffer)


def kernel_call(body, inputs, in_specs, after=(), **options):
    def run(*refs):
        body(*refs[len(after) :])

    specs = [pl.BlockSpec(memory_space=pl.ANY)] * len(after) + list(in_specs)
    return pl.pallas_call(run, in_specs=specs, compiler_params=params(), **options)(*after, *inputs)


def pack_step(total):
    for step in (448, 336, 224, 192, 112, 96, 64, 48, 32, 16):
        if total % step == 0:
            return step
    return total


def params():
    return pltpu.CompilerParams(vmem_limit_bytes=VMEM_LIMIT)


def whole(shape):
    return pl.BlockSpec(shape, lambda *_: (0,) * len(shape))


def pack_kernel(base_ref, pick_ref, slot_ref, rows_ref, *out_refs, capacity):
    pack_into(out_refs, rows_ref, targets(pick_ref[...], slot_ref[...], capacity, base_ref[0]))


def pack(base, pick_rows, slot_rows, rows, buffers, capacity):
    count, width = rows.shape
    total = sum(shape[0] for shape in buffers)
    return kernel_call(
        functools.partial(pack_kernel, capacity=capacity),
        (base, pick_rows, slot_rows, rows),
        [pl.BlockSpec(memory_space=SMEM)] + [pl.BlockSpec(memory_space=VM)] * 3,
        out_shape=tuple(jax.ShapeDtypeStruct(shape, BF) for shape in buffers),
        out_specs=(pl.BlockSpec(memory_space=VM),) * len(buffers),
        cost_estimate=estimate(
            flops=2 * total * count * width, bytes_accessed=4 * total * width, transcendentals=0
        ),
        name="pack_rows",
    )


def classes(count, patch, rows, padding):
    row = lax.broadcasted_iota(jnp.int32, (rows, 1), 0)
    image = jnp.zeros((rows, 1), jnp.int32)
    for i in range(1, IMAGES_MAX):
        image = image + (row >= i * patch).astype(jnp.int32)
    return jnp.where(row < count * patch, image, padding)


def front_kernel(
    base_ref,
    count_ref,
    patch_ref,
    tokens_ref,
    gain1_ref,
    shift1_ref,
    wq_ref,
    wk_ref,
    wv_ref,
    wo_ref,
    gain2_ref,
    shift2_ref,
    pick_ref,
    slot_ref,
    n1_ref,
    q_ref,
    k_ref,
    v_ref,
    p_ref,
    linv_ref,
    mixed_ref,
    res_ref,
    *rest,
    capacity,
    head_dim,
    qb,
):
    *out_refs, n2_ref = rest
    j = pl.program_id(0)
    rows, width = tokens_ref.shape
    cols = wq_ref.shape[1]

    @pl.when(j == 0)
    def _():
        x = tokens_ref[...].astype(F32)
        unit, _ = standardize(x)
        n1_ref[...] = (unit * gain1_ref[...] + shift1_ref[...]).astype(BF)
        res_ref[...] = x

    n1 = n1_ref[...]
    q_ref[...] = mm(n1, wq_ref[...]).astype(BF)
    k_ref[...] = mm(n1, wk_ref[...]).astype(BF)
    v_ref[...] = mm(n1, wv_ref[...]).astype(BF)
    cls = classes(count_ref[0], patch_ref[0], rows, head_dim - 1)
    lane = lax.broadcasted_iota(jnp.int32, (rows, 2 * head_dim), 1)
    inner = lane % head_dim
    apart = jnp.where(inner == cls, 0.0, MASKED).astype(BF)
    member = jnp.where(inner == cls, 1.0, 0.0).astype(BF)
    ones = jnp.ones((rows, 2 * head_dim), BF)
    scale = head_dim ** (-0.5)
    for pair in range(cols // (2 * head_dim)):
        sl = slice(pair * 2 * head_dim, (pair + 1) * 2 * head_dim)
        q_pair = q_ref[:, sl] * jnp.asarray(scale, BF)
        k_pair = k_ref[:, sl]
        v_ext = jnp.concatenate([v_ref[:, sl], ones], axis=1)
        for h in range(2):
            mine = (lane >= h * head_dim) & (lane < (h + 1) * head_dim)
            qm = jnp.where(mine, q_pair, apart)
            km = jnp.where(mine, k_pair, member)
            for b in range(0, rows, qb):
                s = mm_nt(qm[b : b + qb], km)
                top = jnp.max(s, axis=-1, keepdims=True)
                p = jnp.exp(s - top).astype(BF)
                p_ref[pair * 2 + h, b : b + qb, :] = p
                ov = mm(p, v_ext)
                linv = 1.0 / ov[:, 2 * head_dim :]
                o = (ov[:, : 2 * head_dim] * linv).astype(BF)
                if h == 0:
                    mixed_ref[b : b + qb, sl] = o
                    linv_ref[b : b + qb, sl] = linv
                else:
                    keep = mine[b : b + qb]
                    mixed_ref[b : b + qb, sl] = jnp.where(keep, o, mixed_ref[b : b + qb, sl])
                    linv_ref[b : b + qb, sl] = jnp.where(keep, linv, linv_ref[b : b + qb, sl])
    res_ref[...] += mm(mixed_ref[...], wo_ref[...])

    @pl.when(j == pl.num_programs(0) - 1)
    def _():
        unit, _ = standardize(res_ref[...])
        n2_ref[...] = (unit * gain2_ref[...] + shift2_ref[...]).astype(BF)
        pack_into(out_refs, n2_ref, targets(pick_ref[...], slot_ref[...], capacity, base_ref[0]))


def front(base, count, patch, tokens, g1, s1, wq, wk, wv, wo, g2, s2, pick_rows, slot_rows, buffers, capacity, after):
    rows, width = tokens.shape
    head_dim = width // HEADS
    quad = 4 * head_dim
    steps = width // quad
    col = pl.BlockSpec((width, quad), lambda j: (0, j))
    seq = pl.BlockSpec((rows, quad), lambda j: (0, j))
    smem = pl.BlockSpec(memory_space=SMEM)
    total = sum(shape[0] for shape in buffers)
    flops = 2 * rows * width * (4 * width + 2 * rows + total)
    row = jax.ShapeDtypeStruct((rows, width), BF)
    wide = jax.ShapeDtypeStruct((rows, width), F32)
    return kernel_call(
        functools.partial(front_kernel, capacity=capacity, head_dim=head_dim, qb=rows // 5),
        (base, count, patch, tokens, g1, s1, wq, wk, wv, wo, g2, s2, pick_rows, slot_rows),
        [
            smem,
            smem,
            smem,
            whole((rows, width)),
            whole((width,)),
            whole((width,)),
            col,
            col,
            col,
            pl.BlockSpec((quad, width), lambda j: (j, 0)),
            whole((width,)),
            whole((width,)),
            whole(pick_rows.shape),
            whole(slot_rows.shape),
        ],
        after,
        grid=(steps,),
        out_shape=(row, row, row, row, jax.ShapeDtypeStruct((HEADS, rows, rows), BF), wide, row, wide)
        + tuple(jax.ShapeDtypeStruct(shape, BF) for shape in buffers),
        out_specs=(
            whole((rows, width)),
            seq,
            seq,
            seq,
            pl.BlockSpec((4, rows, rows), lambda j: (j, 0, 0)),
            seq,
            seq,
            whole((rows, width)),
        )
        + tuple(whole(shape) for shape in buffers),
        scratch_shapes=[pltpu.VMEM((rows, width), BF)],
        cost_estimate=estimate(
            flops=flops, bytes_accessed=30 * 1024 * 1024, transcendentals=HEADS * rows * rows
        ),
        name="front",
    )


GELU_A = 0.7978845608028654
GELU_B = 0.044715


def expert_kernel(base_ref, c_ref, *refs, which, axis):
    blocks = len(which)
    x_refs, refs = refs[:blocks], refs[blocks:]
    wi_own_ref, wi_far_ref, wo_own_ref, wo_far_ref, bi_ref, bo_ref, router_ref = refs[:7]
    hid_ref, gp_ref, gout_ref, gbi_ref, gbo_ref, grouter_ref = refs[7:13]
    out_refs, gin_refs = refs[13 : 13 + blocks], refs[13 + blocks : 13 + 2 * blocks]
    acc_out, acc_gin, prob = refs[13 + 2 * blocks :]
    f = pl.program_id(0)
    steps = pl.num_programs(0)
    size, width = x_refs[0].shape
    experts = router_ref.shape[1]
    mine = lax.broadcasted_iota(jnp.int32, (size, experts), 1) == lax.axis_index(axis)

    def cot_rows(i):
        place = jnp.bitwise_xor(base_ref[0], which[i]) * size
        return c_ref[pl.ds(pl.multiple_of(place, 16), size), :].astype(F32)

    @pl.when(f == 0)
    def _():
        total = jnp.zeros((1, width), F32)
        for i in range(blocks):
            sl = slice(i * size, (i + 1) * size)
            logits = mm(x_refs[i][...], router_ref[...])
            powers = jnp.exp(logits - jnp.max(logits, axis=-1, keepdims=True))
            probs = powers / jnp.sum(powers, axis=-1, keepdims=True)
            prob[sl, :] = probs
            chosen = jnp.sum(jnp.where(mine, probs, 0.0), axis=-1, keepdims=True)
            grads = (chosen * cot_rows(i)).astype(BF)
            gout_ref[sl, :] = grads
            total = total + jnp.sum(grads.astype(F32), axis=0, keepdims=True)
        gbo_ref[...] = total
        acc_out[...] = jnp.broadcast_to(bo_ref[...].astype(F32), acc_out.shape)
        acc_gin[...] = jnp.zeros(acc_gin.shape, F32)

    near = f < steps // 2
    wi = jnp.where(near, wi_own_ref[...], wi_far_ref[...])
    wo = jnp.where(near, wo_own_ref[...], wo_far_ref[...])
    bi = bi_ref[...].astype(F32)
    bias_sum = jnp.zeros(gbi_ref.shape, F32)
    step = pack_step(size)
    for i in range(blocks):
        for start in range(0, size, step):
            sl = slice(i * size + start, i * size + start + step)
            v = mm(x_refs[i][start : start + step, :], wi) + bi
            gh = mm_nt(gout_ref[sl, :], wo)
            vv = v * v
            t = jnp.tanh(v * (GELU_A + (GELU_A * GELU_B) * vv))
            half = 0.5 + 0.5 * t
            hid = (v * half).astype(BF)
            slope = half + (half * (1.0 - t)) * (v * (GELU_A + (3.0 * GELU_A * GELU_B) * vv))
            gp = (gh * slope).astype(BF)
            hid_ref[0, sl, :] = hid
            gp_ref[0, sl, :] = gp
            bias_sum = bias_sum + jnp.sum(gp.astype(F32), axis=0, keepdims=True)
            acc_out[sl, :] += mm(hid, wo)
            acc_gin[sl, :] += mm_nt(gp, wi)
    gbi_ref[...] = bias_sum

    @pl.when(f == steps - 1)
    def _():
        router = router_ref[...].astype(F32)
        grouter = jnp.zeros(grouter_ref.shape, F32)
        for i in range(blocks):
            sl = slice(i * size, (i + 1) * size)
            probs = prob[sl, :]
            chosen = jnp.sum(jnp.where(mine, probs, 0.0), axis=-1, keepdims=True)
            eo = acc_out[sl, :].astype(BF).astype(F32)
            out_refs[i][...] = (chosen * eo).astype(BF)
            gc = jnp.sum(eo * cot_rows(i), axis=-1, keepdims=True)
            gl = (gc * chosen) * (jnp.where(mine, 1.0, 0.0) - probs)
            extra = lax.dot_general(
                gl,
                router,
                (((1,), (1,)), ((), ())),
                precision=lax.Precision.HIGHEST,
                preferred_element_type=F32,
            )
            gin = (acc_gin[sl, :] + extra).astype(BF)
            if len(gin_refs[i].shape) == 2:
                gin_refs[i][...] = gin
            else:
                gin_refs[i][0] = gin
                gin_refs[i][1] = gin
            high = gl.astype(BF)
            low = (gl - high.astype(F32)).astype(BF)
            x = x_refs[i][...]
            grouter = grouter + mm_tn(high, x) + mm_tn(low, x)
        grouter_ref[...] = grouter


def expert_pass(base, cot, xs, which, twice, wi_own, wi_far, wo_own, wo_far, bi, bo, router, axis, after):
    size, width = xs[0].shape
    blocks = len(xs)
    total = blocks * size
    half = wi_own.shape[1]
    chunk = 512 if half % 512 == 0 else half
    per = half // chunk
    steps = 2 * per
    experts = router.shape[1]
    near = lambda f: jnp.minimum(f, per - 1)
    far = lambda f: jnp.maximum(f - per, 0)
    act = pl.BlockSpec((1, total, chunk), lambda f: (f, 0, 0))
    piece = (size, width)
    back = (2, size, width) if twice else piece
    results = kernel_call(
        functools.partial(expert_kernel, which=which, axis=axis),
        (base, cot, *xs, wi_own, wi_far, wo_own, wo_far, bi, bo, router),
        [pl.BlockSpec(memory_space=SMEM), whole(cot.shape)]
        + [whole((size, width))] * blocks
        + [
            pl.BlockSpec((width, chunk), lambda f: (0, near(f))),
            pl.BlockSpec((width, chunk), lambda f: (0, far(f))),
            pl.BlockSpec((chunk, width), lambda f: (near(f), 0)),
            pl.BlockSpec((chunk, width), lambda f: (far(f), 0)),
            pl.BlockSpec((1, chunk), lambda f: (0, f)),
            whole((1, width)),
            whole((width, experts)),
        ],
        after,
        grid=(steps,),
        out_shape=(
            jax.ShapeDtypeStruct((steps, total, chunk), BF),
            jax.ShapeDtypeStruct((steps, total, chunk), BF),
            jax.ShapeDtypeStruct((total, width), BF),
            jax.ShapeDtypeStruct((1, 2 * half), F32),
            jax.ShapeDtypeStruct((1, width), F32),
            jax.ShapeDtypeStruct((experts, width), F32),
        )
        + (jax.ShapeDtypeStruct(piece, BF),) * blocks
        + (jax.ShapeDtypeStruct(back, BF),) * blocks,
        out_specs=(
            act,
            act,
            whole((total, width)),
            pl.BlockSpec((1, chunk), lambda f: (0, f)),
            whole((1, width)),
            whole((experts, width)),
        )
        + (whole(piece),) * blocks
        + (whole(back),) * blocks,
        scratch_shapes=[
            pltpu.VMEM((total, width), F32),
            pltpu.VMEM((total, width), F32),
            pltpu.VMEM((total, experts), F32),
        ],
        cost_estimate=estimate(
            flops=16 * total * width * half, bytes_accessed=20 * 1024 * 1024, transcendentals=2 * total * half
        ),
        name="expert_pass",
    )
    return results[:6], results[6 : 6 + blocks], results[6 + blocks :]


def outer_kernel(*refs, counts):
    groups = []
    for count in counts:
        values = [ref[...] if len(ref.shape) == 2 else ref[0] for ref in refs[:count]]
        groups.append(values[0] if count == 1 else jnp.concatenate(values, axis=0))
        refs = refs[count:]
    x, g, hid_far, hid_own, gp_far, gp_own = groups
    wo_far_ref, wo_own_ref, wi_far_ref, wi_own_ref = refs
    wo_far_ref[...] = mm_tn(hid_far, g).astype(BF)
    wo_own_ref[...] = mm_tn(hid_own, g).astype(BF)
    wi_far_ref[...] = mm_tn(x, gp_far).astype(BF)
    wi_own_ref[...] = mm_tn(x, gp_own).astype(BF)


def outer_pass(xs, gouts, hids, gps, half, after=()):
    width = xs[0].shape[1]
    total = sum(x.shape[0] for x in xs)
    chunk = hids[0].shape[2]
    per = half // chunk
    cut = lambda values, first: [
        pl.BlockSpec((1, *value.shape[1:]), lambda f: (f + first * per, 0, 0)) for value in values
    ]
    full = lambda values: [whole(value.shape) for value in values]
    groups = (xs, gouts, hids, hids, gps, gps)
    outer = jax.ShapeDtypeStruct((half, width), BF)
    inner = jax.ShapeDtypeStruct((width, half), BF)
    return kernel_call(
        functools.partial(outer_kernel, counts=tuple(len(group) for group in groups)),
        [value for group in groups for value in group],
        full(xs) + full(gouts) + cut(hids, 1) + cut(hids, 0) + cut(gps, 1) + cut(gps, 0),
        after,
        grid=(per,),
        out_shape=(outer, outer, inner, inner),
        out_specs=(pl.BlockSpec((chunk, width), lambda f: (f, 0)),) * 2
        + (pl.BlockSpec((width, chunk), lambda f: (0, f)),) * 2,
        cost_estimate=estimate(
            flops=8 * total * width * half, bytes_accessed=30 * 1024 * 1024, transcendentals=0
        ),
        name="outer_pass",
    )


def live_rows(count, patch, rows):
    row = lax.broadcasted_iota(jnp.int32, (rows, 1), 0)
    return row < count * patch


def assemble_kernel(base_ref, *refs):
    *block_refs, out_ref = refs
    size = block_refs[0].shape[0]
    for i, block_ref in enumerate(block_refs):
        place = jnp.bitwise_xor(base_ref[0], i) * size
        out_ref[pl.ds(pl.multiple_of(place, 16), size), :] = block_ref[...]


def assemble(base, blocks, after):
    size, width = blocks[0].shape
    return kernel_call(
        assemble_kernel,
        (base, *blocks),
        [pl.BlockSpec(memory_space=SMEM)] + [pl.BlockSpec(memory_space=VM)] * len(blocks),
        after,
        out_shape=jax.ShapeDtypeStruct((len(blocks) * size, width), BF),
        out_specs=pl.BlockSpec(memory_space=VM),
        cost_estimate=estimate(flops=0, bytes_accessed=4 * len(blocks) * size * width, transcendentals=0),
        name="assemble",
    )


def output_kernel(base_ref, count_ref, patch_ref, pick_ref, slot_ref, res_ref, *rest, capacity):
    *back_refs, out_ref = rest
    live = live_rows(count_ref[0], patch_ref[0], res_ref.shape[0])
    mixture = unpack_rows(back_refs, targets(pick_ref[...], slot_ref[...], capacity, base_ref[0]))
    out_ref[...] = jnp.where(live, res_ref[...] + mixture, 0.0).astype(BF)


def output_pass(base, count, patch, picks, slots, back, res, capacity, after):
    rows, width = res.shape
    return kernel_call(
        functools.partial(output_kernel, capacity=capacity),
        (base, count, patch, picks, slots, res, *back),
        [pl.BlockSpec(memory_space=SMEM)] * 3 + [pl.BlockSpec(memory_space=VM)] * (3 + len(back)),
        after,
        out_shape=jax.ShapeDtypeStruct((rows, width), BF),
        out_specs=pl.BlockSpec(memory_space=VM),
        cost_estimate=estimate(
            flops=4 * rows * rows * width, bytes_accessed=6 * 1024 * 1024, transcendentals=0
        ),
        name="output_pass",
    )


def middle_kernel(
    base_ref,
    place_ref,
    core_ref,
    count_ref,
    patch_ref,
    pick_ref,
    slot_ref,
    cot_ref,
    res_ref,
    gain2_ref,
    mixed_ref,
    wo_ref,
    *rest,
    capacity,
):
    *back_refs, gres_ref, gmix_ref, keep_ref, send_ref, ggain_ref, gshift_ref = rest
    live = live_rows(count_ref[0], patch_ref[0], res_ref.shape[0])
    gn = unpack_rows(back_refs, targets(pick_ref[...], slot_ref[...], capacity, base_ref[0]), place_ref[0])
    unit, inv = standardize(res_ref[...])
    ggain_ref[...] = jnp.sum(gn * unit, axis=0, keepdims=True)
    gshift_ref[...] = jnp.sum(gn, axis=0, keepdims=True)
    gout = jnp.where(live, cot_ref[...].astype(F32), 0.0)
    gres = gout + norm_back(gn, gain2_ref[...], unit, inv)
    gres_ref[...] = gres
    branch = gres.astype(BF)
    gmix_ref[...] = mm_nt(branch, wo_ref[...]).astype(BF)
    keep_ref[...] = mm_tn(core_half(mixed_ref, core_ref[0]), branch).astype(BF)
    send_ref[...] = mm_tn(core_half(mixed_ref, 1 - core_ref[0]), branch).astype(BF)


def core_half(ref, core):
    size = ref.shape[1] // 2
    return ref[:, pl.ds(pl.multiple_of(core * size, 128), size)]


def middle_pass(base, place, core, count, patch, picks, slots, back, cot, res, g2, mixed, wo, capacity, after):
    rows, width = res.shape
    vm = pl.BlockSpec(memory_space=VM)
    piece = jax.ShapeDtypeStruct((width // 2, width), BF)
    return kernel_call(
        functools.partial(middle_kernel, capacity=capacity),
        (base, place, core, count, patch, picks, slots, cot, res, g2, mixed, wo, *back),
        [pl.BlockSpec(memory_space=SMEM)] * 5 + [vm] * (7 + len(back)),
        after,
        out_shape=(
            jax.ShapeDtypeStruct((rows, width), F32),
            jax.ShapeDtypeStruct((rows, width), BF),
            piece,
            piece,
            jax.ShapeDtypeStruct((1, width), F32),
            jax.ShapeDtypeStruct((1, width), F32),
        ),
        out_specs=(vm,) * 6,
        cost_estimate=estimate(
            flops=400 * rows * width * (rows + width), bytes_accessed=14 * 1024 * 1024, transcendentals=0
        ),
        name="middle_pass",
    )


def attend_back_kernel(
    core_ref,
    n1_ref,
    q_ref,
    k_ref,
    v_ref,
    p_ref,
    linv_ref,
    mixed_ref,
    gmix_ref,
    dq_ref,
    dk_ref,
    dv_ref,
    keep_ref,
    send_ref,
    ds_ref,
    *,
    head_dim,
    qb,
):
    rows, cols = q_ref.shape
    lane = lax.broadcasted_iota(jnp.int32, (rows, 2 * head_dim), 1)
    scale = jnp.asarray(head_dim ** (-0.5), BF)
    zero = jnp.zeros((rows, 2 * head_dim), BF)
    for pair in range(cols // (2 * head_dim)):
        sl = slice(pair * 2 * head_dim, (pair + 1) * 2 * head_dim)
        q_pair = q_ref[:, sl] * scale
        k_pair = k_ref[:, sl] * scale
        v_pair = v_ref[:, sl]
        do_pair = (gmix_ref[:, sl].astype(F32) * linv_ref[:, sl]).astype(BF)
        inner = do_pair.astype(F32) * mixed_ref[:, sl].astype(F32)
        dq = None
        for h in range(2):
            mine = (lane >= h * head_dim) & (lane < (h + 1) * head_dim)
            dom = jnp.where(mine, do_pair, zero)
            qm = jnp.where(mine, q_pair, zero)
            km = jnp.where(mine, k_pair, zero)
            row_inner = jnp.sum(jnp.where(mine, inner, 0.0), axis=-1, keepdims=True)
            head = pair * 2 + h
            for b in range(0, rows, qb):
                dp = mm_nt(dom[b : b + qb], v_pair)
                p = p_ref[head, b : b + qb, :].astype(F32)
                ds_ref[b : b + qb, :] = (p * (dp - row_inner[b : b + qb])).astype(BF)
            ds = ds_ref[...]
            dq_h = mm(ds, km)
            dk_h = mm_tn(ds, qm)
            dv_h = mm_tn(p_ref[head], dom)
            if h == 0:
                dq, dk, dv = dq_h, dk_h, dv_h
            else:
                dq, dk, dv = dq + dq_h, dk + dk_h, dv + dv_h
        dq_ref[:, sl] = dq.astype(BF)
        dk_ref[:, sl] = dk.astype(BF)
        dv_ref[:, sl] = dv.astype(BF)
    grads = jnp.concatenate([dq_ref[...], dk_ref[...], dv_ref[...]], axis=1)
    keep_ref[...] = mm_tn(core_half(n1_ref, core_ref[0]), grads).astype(BF)
    send_ref[...] = mm_tn(core_half(n1_ref, 1 - core_ref[0]), grads).astype(BF)


def attend_back(core, n1, q, k, v, p, linv, mixed, gmix, after):
    rows, width = n1.shape
    head_dim = width // HEADS
    quad = 4 * head_dim
    steps = width // quad
    seq = pl.BlockSpec((rows, quad), lambda j: (0, j))
    grads = pl.BlockSpec((width // 2, 3 * quad), lambda j: (j, 0))
    return kernel_call(
        functools.partial(attend_back_kernel, head_dim=head_dim, qb=rows),
        (core, n1, q, k, v, p, linv, mixed, gmix),
        [
            pl.BlockSpec(memory_space=SMEM),
            whole((rows, width)),
            seq,
            seq,
            seq,
            pl.BlockSpec((4, rows, rows), lambda j: (j, 0, 0)),
            seq,
            seq,
            seq,
        ],
        after,
        grid=(steps,),
        out_shape=(jax.ShapeDtypeStruct((rows, width), BF),) * 3
        + (jax.ShapeDtypeStruct((steps * (width // 2), 3 * quad), BF),) * 2,
        out_specs=(seq, seq, seq, grads, grads),
        scratch_shapes=[pltpu.VMEM((rows, rows), BF)],
        cost_estimate=estimate(
            flops=2 * rows * width * (3 * width + 4 * rows), bytes_accessed=24 * 1024 * 1024, transcendentals=0
        ),
        name="attend_back",
    )


def tokens_kernel(*refs, parts):
    core_ref, dq_ref, dk_ref, dv_ref, wq_ref, wk_ref, wv_ref, tokens_ref, gain1_ref, gres_ref = refs[:10]
    ggain2_ref, gshift2_ref = refs[10:12]
    gbi_refs, refs = refs[12 : 12 + parts], refs[12 + parts :]
    gbo_refs, refs = refs[:parts], refs[parts:]
    grouter_refs, (gtok_ref, small_ref) = refs[:parts], refs[parts:]
    gn = mm_nt(dq_ref[...], wq_ref[...]) + mm_nt(dk_ref[...], wk_ref[...]) + mm_nt(dv_ref[...], wv_ref[...])
    unit, inv = standardize(tokens_ref[...].astype(F32))
    gtok_ref[...] = gres_ref[...] + norm_back(gn, gain1_ref[...], unit, inv)
    width = gn.shape[1]
    gbi = sum(ref[...] for ref in gbi_refs)
    rows = gbi.shape[1] // 2 // width
    experts = grouter_refs[0].shape[0]
    zeros = jnp.zeros((small_ref.shape[1] - rows - 5 - experts, width), F32)
    common = [
        sum(ref[...] for ref in gbo_refs),
        jnp.sum(gn * unit, axis=0, keepdims=True),
        jnp.sum(gn, axis=0, keepdims=True),
        ggain2_ref[...],
        gshift2_ref[...],
        sum(ref[...] for ref in grouter_refs),
    ]
    columns = small_ref.shape[0] // 2
    for core in range(2):
        mine = core_ref[0] == core
        for column in range(columns):
            at = core * columns + column
            for i in range(rows):
                own, far = (gbi[:, (first + i) * width : (first + i + 1) * width] for first in (0, rows))
                small_ref[at, i : i + 1, :] = jnp.where(mine, own, far)
            place = rows
            for value in common:
                small_ref[at, place : place + value.shape[0], :] = value
                place += value.shape[0]
            if zeros.shape[0]:
                small_ref[at, place:, :] = zeros


def tokens_pass(core, columns, grads, weights, tokens, g1, gres, ggain2, gshift2, sums, after):
    rows, width = tokens.shape
    vm = pl.BlockSpec(memory_space=VM)
    gbi, gbo, grouter = sums
    height = gbi[0].shape[1] // 2 // width + 5 + grouter[0].shape[0]
    inputs = (*grads, *weights, tokens, g1, gres, ggain2, gshift2, *gbi, *gbo, *grouter)
    return kernel_call(
        functools.partial(tokens_kernel, parts=len(gbi)),
        (core, *inputs),
        [pl.BlockSpec(memory_space=SMEM)] + [vm] * len(inputs),
        after,
        out_shape=(
            jax.ShapeDtypeStruct((rows, width), F32),
            jax.ShapeDtypeStruct((2 * columns, height + -height % 16, width), F32),
        ),
        out_specs=(vm,) * 2,
        cost_estimate=estimate(flops=600 * rows * width * width, bytes_accessed=0, transcendentals=0),
        name="tokens_pass",
    )


def swap(value, axis, bit):
    return lax.ppermute(value, axis, [(i, i ^ bit) for i in range(lax.axis_size(axis))])


def block(value, index, count):
    size = value.shape[0] // count
    return lax.dynamic_slice_in_dim(value, index * size, size, 0)


def narrow_sum(*terms):
    return functools.reduce(jnp.add, [term.astype(F32) for term in terms]).astype(BF)


def axis_bits(axis):
    me = lax.axis_index(axis)
    return [(me >> level) & 1 for level in range(lax.axis_size(axis).bit_length() - 1)]


def prefetch_call(body, scalars, inputs, in_specs, grid, out_specs, after, **options):
    def run(scalar_ref, *refs):
        body(scalar_ref, *refs[len(after) :])

    spec = pltpu.PrefetchScalarGridSpec(
        num_scalar_prefetch=1,
        grid=grid,
        in_specs=[pl.BlockSpec(memory_space=pl.ANY)] * len(after) + list(in_specs),
        out_specs=out_specs,
    )
    return pl.pallas_call(run, grid_spec=spec, compiler_params=params(), **options)(scalars, *after, *inputs)


def pick_kernel(index_ref, *refs, counts):
    outs = refs[sum(counts) :]
    for count, out_ref in zip(counts, outs):
        terms, refs = refs[:count], refs[count:]
        out_ref[...] = sum(ref[...].astype(F32) for ref in terms).astype(BF)


def pick_sums(indices, groups, after, cost=0):
    flat, in_specs, out_specs, shapes = [], [], [], []
    for group, height in groups:
        width = group[0].shape[1]
        for value in group:
            in_specs.append(pl.BlockSpec((height, width), lambda i, at, k=len(flat): (at[k], 0)))
            flat.append(value)
        out_specs.append(whole((height, width)))
        shapes.append(jax.ShapeDtypeStruct((height, width), BF))
    return prefetch_call(
        functools.partial(pick_kernel, counts=tuple(len(group) for group, _ in groups)),
        indices,
        flat,
        in_specs,
        (1,),
        tuple(out_specs),
        after,
        out_shape=tuple(shapes),
        cost_estimate=estimate(flops=cost, bytes_accessed=2 * sum(v.size for v in flat), transcendentals=0),
        name="pick_sums",
    )


def merge_kernel(bits_ref, *refs):
    outs = refs[len(refs) // 3 * 2 :]
    for i, out_ref in enumerate(outs):
        for ref, bit in ((refs[2 * i], bits_ref[i]), (refs[2 * i + 1], 1 - bits_ref[i])):
            size = ref.shape[0]
            out_ref[pl.ds(pl.multiple_of(bit * size, 16), size), :] = ref[...].astype(out_ref.dtype)


def merge(bits, pairs, dtype, after=()):
    flat = [value for pair in pairs for value in pair]
    vm = pl.BlockSpec(memory_space=VM)
    return kernel_call(
        merge_kernel,
        (bits, *flat),
        [pl.BlockSpec(memory_space=SMEM)] + [vm] * len(flat),
        after,
        out_shape=tuple(jax.ShapeDtypeStruct((2 * mine.shape[0], mine.shape[1]), dtype) for mine, _ in pairs),
        out_specs=(vm,) * len(pairs),
        cost_estimate=estimate(flops=0, bytes_accessed=6 * sum(v.size for v in flat), transcendentals=0),
        name="merge",
    )


def matrices_kernel(me_ref, lead_ref, lead_far_ref, main_ref, main_far_ref, *out_refs, places):
    size = lead_ref.shape[0]
    for (i, first), out_ref in zip(places, out_refs):
        matrix = jnp.bitwise_xor(me_ref[0], i)
        rows = out_ref.shape[0]
        lead = slice(first, first + rows)

        @pl.when(matrix == 0)
        def _():
            out_ref[...] = (lead_ref[lead, :].astype(F32) + lead_far_ref[lead, :].astype(F32)).astype(BF)

        @pl.when(matrix > 0)
        def _():
            place = pl.ds(pl.multiple_of((matrix - 1) * size + first, 16), rows)
            out_ref[...] = (main_ref[place, :].astype(F32) + main_far_ref[place, :].astype(F32)).astype(BF)


def matrices(me, lead, lead_far, main, main_far, after):
    size, width = lead.shape
    count = 1 + main.shape[0] // size
    places = [(i, 0, size) for i in range(count - 1)] + [(count - 1, i * (size // 2), size // 2) for i in range(2)]
    vm = pl.BlockSpec(memory_space=VM)
    return kernel_call(
        functools.partial(matrices_kernel, places=[place[:2] for place in places]),
        (me, lead, lead_far, main, main_far),
        [pl.BlockSpec(memory_space=SMEM)] + [vm] * 4,
        after,
        out_shape=tuple(jax.ShapeDtypeStruct((rows, width), BF) for _, _, rows in places),
        out_specs=(vm,) * len(places),
        cost_estimate=estimate(flops=0, bytes_accessed=8 * size * count * width, transcendentals=0),
        name="matrices",
    )


def relay_kernel(x_ref, y_ref, for_y_ref, for_x_ref, x_out_ref, y_out_ref):
    size = for_x_ref.shape[0]
    x_out_ref[:size, :] = x_ref[:size, :]
    x_out_ref[size:, :] = (x_ref[size:, :].astype(F32) + for_x_ref[...].astype(F32)).astype(BF)
    y_out_ref[:size, :] = (y_ref[:size, :].astype(F32) + for_y_ref[...].astype(F32)).astype(BF)
    y_out_ref[size:, :] = y_ref[size:, :]


def relay(x, y, for_y, for_x, after):
    vm = pl.BlockSpec(memory_space=VM)
    shape = jax.ShapeDtypeStruct(x.shape, BF)
    return kernel_call(
        relay_kernel,
        (x, y, for_y, for_x),
        [vm] * 4,
        after,
        out_shape=(shape, shape),
        out_specs=(vm, vm),
        cost_estimate=estimate(flops=0, bytes_accessed=0, transcendentals=0),
        name="relay",
    )


def layers_kernel(*refs):
    *part_refs, out_ref = refs
    size = out_ref.shape[1]
    for i in range(out_ref.shape[0]):
        rows = slice(i * size, (i + 1) * size)
        out_ref[i] = sum(ref[rows, :].astype(F32) for ref in part_refs).astype(BF)


def layers(parts, count):
    height, width = parts[0].shape
    vm = pl.BlockSpec(memory_space=VM)
    return kernel_call(
        layers_kernel,
        parts,
        [vm] * len(parts),
        out_shape=jax.ShapeDtypeStruct((count, height // count, width), BF),
        out_specs=vm,
        cost_estimate=estimate(flops=0, bytes_accessed=0, transcendentals=0),
        name="layers",
    )


def quarter_kernel(small_ref, parts_ref, gbi_ref, gbo_ref, out_ref, *, half_rows):
    small = sum(small_ref[i] for i in range(small_ref.shape[0]))
    width = small.shape[1]
    for i in range(half_rows):
        gbi_ref[:, i * width : (i + 1) * width] = small[i : i + 1, :]
    gbo_ref[...] = small[half_rows : half_rows + 1, :]
    rows = parts_ref.shape[1]
    out_ref[:rows, :] = sum(parts_ref[i].astype(F32) for i in range(parts_ref.shape[0])).astype(BF)
    out_ref[rows:, :] = small.astype(BF)


def quarter(small, parts, half_rows):
    _, rows, width = parts.shape
    vm = pl.BlockSpec(memory_space=VM)
    return kernel_call(
        functools.partial(quarter_kernel, half_rows=half_rows),
        [small, parts],
        [vm] * 2,
        out_shape=(
            jax.ShapeDtypeStruct((1, half_rows * width), F32),
            jax.ShapeDtypeStruct((1, width), F32),
            jax.ShapeDtypeStruct((rows + small.shape[1], width), BF),
        ),
        out_specs=(vm,) * 3,
        cost_estimate=estimate(flops=0, bytes_accessed=0, transcendentals=0),
        name="quarter",
    )


def whole_kernel(base_ref, *refs, blocks, rows, skip, experts):
    block_refs, (matrix_ref, *vector_refs, router_ref) = refs[:blocks], refs[blocks:]
    for i, ref in enumerate(block_refs):
        place = jnp.bitwise_xor(base_ref[0], i) * rows
        matrix_ref[pl.ds(pl.multiple_of(place, 16), rows), :] = ref[:rows, :]
    total = sum(ref[rows:, :].astype(F32) for ref in block_refs)
    for i, ref in enumerate(vector_refs):
        ref[...] = total[skip + i]
    first = skip + len(vector_refs)
    router_ref[...] = total[first : first + experts]


def whole_matrix(base, blocks, rows, skip, experts):
    width = blocks[0].shape[1]
    vm = pl.BlockSpec(memory_space=VM)
    return kernel_call(
        functools.partial(whole_kernel, blocks=len(blocks), rows=rows, skip=skip, experts=experts),
        (base, *blocks),
        [pl.BlockSpec(memory_space=SMEM)] + [vm] * len(blocks),
        out_shape=(jax.ShapeDtypeStruct((len(blocks) * rows, width), BF),)
        + (jax.ShapeDtypeStruct((width,), F32),) * 4
        + (jax.ShapeDtypeStruct((experts, width), F32),),
        out_specs=(vm,) * 6,
        cost_estimate=estimate(flops=0, bytes_accessed=4 * width * width, transcendentals=0),
        name="whole_matrix",
    )


def spread_kernel(core_ref, me_ref, *refs, places, blocks, earlier):
    block_refs, refs = refs[:blocks], refs[blocks + earlier :]
    dwq_ref, dwk_ref, dwv_ref, dwo_ref, wide, sems = refs
    width = dwo_ref.shape[1]
    third = width // 3
    copies = []
    for slot, (matrix, parts) in enumerate(places):
        for index, first, own in parts:
            ref = block_refs[index]
            core = core_ref[0] if own else 1 - core_ref[0]
            rows = pl.ds(pl.multiple_of(core * (width // 2) + first, 16), ref.shape[0])
            wide[slot, rows, :] = ref[...].astype(F32)
        matrix = jnp.bitwise_xor(me_ref[0], matrix)
        lead = pltpu.make_async_copy(wide.at[slot], dwo_ref, sems.at[slot, 0])
        columns = pl.ds(pl.multiple_of(jnp.maximum(matrix - 1, 0) * third, 128), third)
        rest = [
            pltpu.make_async_copy(
                wide.at[slot, :, i * third : (i + 1) * third], out_ref.at[:, columns], sems.at[slot, i]
            )
            for i, out_ref in enumerate((dwq_ref, dwk_ref, dwv_ref))
        ]
        copies.append((matrix, lead, rest))

        @pl.when(matrix == 0)
        def _():
            lead.start()

        @pl.when(matrix > 0)
        def _():
            for copy in rest:
                copy.start()

    for matrix, lead, rest in copies:

        @pl.when(matrix == 0)
        def _():
            lead.wait()

        @pl.when(matrix > 0)
        def _():
            for copy in rest:
                copy.wait()


def spread(core, me, groups, earlier=()):
    flat, places = [], []
    for matrix, parts in groups:
        places.append((matrix, [(len(flat) + i, first, own) for i, (_, first, own) in enumerate(parts)]))
        flat += [value for value, _, _ in parts]
    width = flat[0].shape[1]
    vm, anywhere = pl.BlockSpec(memory_space=VM), pl.BlockSpec(memory_space=pl.ANY)
    return kernel_call(
        functools.partial(spread_kernel, places=places, blocks=len(flat), earlier=len(earlier)),
        (core, me, *flat, *earlier),
        [pl.BlockSpec(memory_space=SMEM)] * 2 + [vm] * len(flat) + [anywhere] * len(earlier),
        out_shape=(jax.ShapeDtypeStruct((width, width), F32),) * 4,
        out_specs=(anywhere,) * 4,
        scratch_shapes=[pltpu.VMEM((len(groups), width, width), F32), pltpu.SemaphoreType.DMA((len(groups), 3))],
        input_output_aliases={2 + len(flat) + i: i for i in range(len(earlier))},
        cost_estimate=estimate(flops=0, bytes_accessed=0, transcendentals=0),
        name="spread",
    )


def butterfly(value, axis):
    step = 1
    while step < lax.axis_size(axis):
        value = (value.astype(F32) + swap(value, axis, step).astype(F32)).astype(value.dtype)
        step *= 2
    return value


def hold(value, after):
    return pl.pallas_call(
        lambda *refs: None,
        out_shape=jax.ShapeDtypeStruct(value.shape, value.dtype),
        in_specs=[pl.BlockSpec(memory_space=pl.ANY)] * 2,
        out_specs=pl.BlockSpec(memory_space=pl.ANY),
        input_output_aliases={0: 0},
        name="hold",
    )(value, after)


def shards(
    tokens,
    cotangent,
    ln1_gain,
    ln1_shift,
    w_query,
    w_key,
    w_value,
    w_output,
    ln2_gain,
    ln2_shift,
    w_router,
    w_inner,
    b_inner,
    w_outer,
    b_outer,
    image_count,
    patches,
    picks,
    slots,
):
    rows, width = tokens.shape
    experts = w_router.shape[1]
    groups = lax.axis_size("expert")
    capacity = 21 * rows // (10 * experts)
    half = w_inner.shape[2]
    g1, s1, g2, s2 = ln1_gain, ln1_shift, ln2_gain, ln2_shift
    pick_rows, slot_rows = picks.T, slots.T
    start = jnp.zeros((1,), jnp.int32)
    whole_buffer = [(experts * capacity, width)]

    def exchange(rows_out):
        cut = rows_out.reshape(experts, capacity, width)
        cut = lax.all_to_all(cut, "expert", split_axis=0, concat_axis=0, tiled=True)
        return cut.reshape(experts * capacity, width)

    if groups <= 4:
        me = lax.axis_index("expert").astype(jnp.int32)
        base = me.reshape(1)
        buffers = [(capacity, width)] * groups
        parts = [[i] for i in range(groups)]

        def exchange_block(blocks, i):
            return blocks[i] if i == 0 else swap(blocks[i], "expert", i)

        def exchange_pair(pair, i):
            members = [[j, j ^ i] for j in range(groups) if j < j ^ i]
            return lax.all_to_all(
                pair, "expert", split_axis=0, concat_axis=0, tiled=True, axis_index_groups=members
            )

    else:
        me = jnp.zeros((), jnp.int32)
        base, buffers, parts = start, whole_buffer, [[0]]

        def exchange_block(blocks, i):
            return exchange(blocks[0])

    place = (1 - ((me >> 1) & 1)).reshape(1)
    core = lax.axis_index("hidden").astype(jnp.int32).reshape(1)
    column = lax.axis_index("dp").astype(jnp.int32).reshape(1)
    columns = lax.axis_size("dp")
    bit_x, bit_y = axis_bits("dp")
    not_x, not_y, zero = 1 - bit_x, 1 - bit_y, jnp.zeros_like(bit_x)
    indices = [
        jnp.stack([not_x] * 2 + [not_y] * 2),
        jnp.stack([2 * bit_x + not_y] * 2 + [not_y] + [2 * bit_y + not_x] * 2 + [not_x]),
        jnp.stack([2 * bit_x + bit_y] * 2 + [bit_y, zero] + [2 * bit_y + bit_x] * 2 + [bit_x, zero]),
    ]
    bits, bits_after = jnp.stack([bit_x, bit_y]), jnp.stack([bit_y, bit_x])
    cot_out = pack(start, pick_rows, slot_rows, cotangent, whole_buffer, capacity)[0]
    cot_in = exchange(cot_out)
    wi_own, wo_own = w_inner[0], w_outer[0]
    wi_far, wo_far = swap(wi_own, "hidden", 1), swap(wo_own, "hidden", 1)
    bi_all = jnp.concatenate([b_inner, swap(b_inner, "hidden", 1)], axis=1)
    n1, q, k, v, p, linv, mixed, res, *outgoing = front(
        base, image_count, patches, tokens, g1, s1, w_query, w_key, w_value, w_output, g2, s2,
        pick_rows, slot_rows, buffers, capacity, [cot_out],
    )
    xs, sums, hids, gps, gouts, out_rows, gin_back = [], [], [], [], [], [], []
    for which in parts:
        i = which[0]
        local = i == 0 and groups <= 4
        if i > 1:
            outgoing[i] = hold(outgoing[i], cot_in if i == 2 else xs[-1])
        x = [exchange_block(outgoing, i)]
        (hid, gp, gout, *small), outs, gins = expert_pass(
            base, cot_out if local else cot_in, x, which, i > 1, wi_own, wi_far, wo_own, wo_far, bi_all, b_outer,
            w_router, "expert", hids[-1:],
        )
        xs.extend(x)
        hids.append(hid)
        gps.append(gp)
        gouts.append(gout)
        sums.append(small)
        out_rows.extend(outs)
        gin_back.append(exchange_pair(gins[0], i) if i > 1 else exchange_block([gins[0]] * groups, i))
    assembled = assemble(base, out_rows, [])
    dwo_far, dwo_own, dwi_far, dwi_own = outer_pass(xs, gouts, hids, gps, half, [assembled])

    gres, gmix, dwout_keep, dwout_send, ggain2, gshift2 = middle_pass(
        base, place, core, image_count, patches, picks, slots, gin_back, cotangent, res, g2, mixed, w_output,
        capacity, [dwi_own],
    )
    dwo_far, dwi_far = swap(dwo_far, "hidden", 1), swap(dwi_far, "hidden", 1)
    half_o, half_i = half // 2, width // 2
    dwo_send, dwi_send = pick_sums(
        indices[0],
        [([dwo_own, dwo_far], half_o), ([dwi_own, dwi_far], half_i)],
        [gmix],
    )
    dwo_got, dwi_got = swap(dwo_send, "dp", 1), swap(dwi_send, "dp", 2)
    dq, dk, dv, main_keep, main_send = attend_back(core, n1, q, k, v, p, linv, mixed, gmix, [dwo_send])
    dwo_send, dwi_send = pick_sums(
        indices[1],
        [([dwo_own, dwo_far, dwo_got], half_o // 2), ([dwi_own, dwi_far, dwi_got], half_i // 2)],
        [main_send],
        10**11,
    )
    dwo_last, dwi_last = swap(dwo_send, "dp", 2), swap(dwi_send, "dp", 1)
    blocks = matrices(
        column, dwout_keep, swap(dwout_send, "hidden", 1), main_keep, swap(main_send, "hidden", 1), [dwo_send]
    )
    gtok, small = tokens_pass(
        core, columns, (dq, dk, dv), (w_query, w_key, w_value), tokens, g1, gres, ggain2, gshift2, list(zip(*sums)),
        [blocks[0]],
    )
    passing = [swap(blocks[3], "dp", 1), swap(blocks[4], "dp", 2)]
    to_x, to_y = relay(blocks[1], blocks[2], *passing, [gtok])
    arrived = [blocks[0], swap(to_x, "dp", 1), swap(to_y, "dp", 2)]
    out_back = exchange(hold(assembled, gin_back[-1]))
    small = lax.all_to_all(hold(small, out_back), ("hidden", "dp"), split_axis=0, concat_axis=0, tiled=True)
    dwo_piece, dwi_piece = pick_sums(
        indices[2],
        [([dwo_own, dwo_far, dwo_got, dwo_last], half_o // 2), ([dwi_own, dwi_far, dwi_got, dwi_last], half_i // 2)],
        [gtok],
    )
    rows_half = width // 2
    half_rows = half // width
    offset = half_rows + 1
    if groups <= 4:
        parts = layers(arrived, groups)
        parts = lax.all_to_all(parts, "expert", split_axis=0, concat_axis=0, tiled=True)
        gbi, gbo, piece = quarter(small, parts, half_rows)
        pieces = [piece] + [swap(piece, "expert", i) for i in range(1, groups)]
        matrix, *vectors = whole_matrix(base, pieces, rows_half // groups, offset, experts)
    else:
        gbi, gbo, piece = quarter(small, layers(arrived, 1), half_rows)
        matrix, *vectors = whole_matrix(start, [butterfly(piece, "expert")], rows_half, offset, experts)
    dwo_half, dwi_half = merge(
        bits_after,
        [(dwo_piece, swap(dwo_piece, "dp", 2)), (dwi_piece, swap(dwi_piece, "dp", 1))],
        BF,
    )
    block_out = output_pass(start, image_count, patches, picks, slots, [out_back], res, capacity, [blocks[0]])
    dwo, dwi = merge(
        bits, [(dwo_half, swap(dwo_half, "dp", 1)), (dwi_half, swap(dwi_half, "dp", 2))], F32, [block_out]
    )
    across = columns - 1
    cut = rows_half // 2
    near = [swap(matrix, "dp", 1), swap(matrix, "dp", 2)]
    corner = pick_sums(jnp.stack([zero, zero + 1]), [([near[0]], cut), ([near[1]], cut)], [])
    corner = [swap(corner[0], "dp", 2), swap(corner[1], "dp", 1)]
    near = [hold(value, dwi) for value in near]
    early = [
        (i, [(value, 0, True), (swap(value, "hidden", 1), 0, False)]) for i, value in enumerate([matrix, *near])
    ]
    grads = spread(core, column, early)
    corner = [hold(value, grads[0]) for value in corner]
    late = [(corner[0], 0, True), (corner[1], cut, True)]
    late += [(swap(value, "hidden", 1), first, False) for value, first, _ in late]
    dwq, dwk, dwv, dwout = spread(core, column, [(across, late)], grads)
    return (
        block_out,
        gtok,
        vectors[0],
        vectors[1],
        dwq,
        dwk,
        dwv,
        dwout,
        vectors[2],
        vectors[3],
        vectors[4].T,
        dwi[None],
        gbi,
        dwo[None],
        gbo,
    )


def solution(mesh):
    rows = P(("expert", "hidden", "dp"), None)
    device = P(("expert", "hidden", "dp"))
    inner = P("expert", None, "hidden")
    inner_bias = P("expert", "hidden")
    outer = P("expert", "hidden", None)
    outer_bias = P("expert", None)
    return jax.shard_map(
        shards,
        mesh=mesh,
        in_specs=(rows, rows) + (P(),) * 9 + (inner, inner_bias, outer, outer_bias, device, device, rows, rows),
        out_specs=(rows, rows) + (P(),) * 9 + (inner, inner_bias, outer, outer_bias),
        check_vma=False,
    )
```
